32 devices in a mesh: ens: 2 (over x), tile: 16 (over z, y, core).
Axes of the slice: x: 2, y: 2, z: 4, core: 2. Of those that a mesh axis runs over, the one named last changes fastest.
Arguments:
- fields: bfloat16 [2, 16, 48, 48, 128], P('ens', 'tile'), may hold values from -6 to 6
- weight_first: bfloat16 [3, 3, 128, 128], replicated, may hold values from -0.1875 to 0.1875
- weight_second: bfloat16 [3, 3, 128, 128], replicated, may hold values from -0.1875 to 0.1875
- neighbours: int32 [16, 4], replicated, may hold values from 0 to 15, as said below
- cotangent: bfloat16 [2, 16, 48, 48, 128], P('ens', 'tile'), may hold values from -6 to 6
Outputs:
- out_field: bfloat16 [2, 16, 48, 48, 128], P('ens', 'tile')
- grad_fields: bfloat16 [2, 16, 48, 48, 128], P('ens', 'tile')
- grad_first: float32 [3, 3, 128, 128], replicated
- grad_second: float32 [3, 3, 128, 128], replicated
The draws below stay inside these ranges and needn't reach their ends.
Inputs may be any that keep to these rules, and one draw needn't show every extreme that they name: The tiles form a grid of 4 rows of 4: the tile at index p has the four neighbours p - 4, p + 1, p + 4 and p - 1 modulo 16, one beside each side, listed clockwise from a starting side that varies from tile to tile; the relation is mutual.
All inputs are finite; a program needn't handle non-finite values.
Results may differ from the reference program's by a relative error of at most 0.0061.
Values may be sent and summed in bfloat16 or wider, within the bound.
No kernel may reach another device: no remote copies, remote signals or barrier semaphores. Data moves between devices by JAX's collectives and lax.ppermute only.
A program may use at most 64 MiB of HBM per device.

```python
import jax
import jax.numpy as jnp
from jax import lax

C = 128
S = 48
ENS = 2
NT = 16
COLS = 4


def draw_neighbours(key, part):
    turns = jax.random.randint(key, (NT,), 0, 4)
    offsets = jnp.array([-COLS, 1, COLS, -1], jnp.int32)
    sides = jnp.arange(4, dtype=jnp.int32)
    global_side = (sides[None, :] + turns[:, None]) % 4
    tiles = jnp.arange(NT, dtype=jnp.int32)[:, None]
    return ((tiles + offsets[global_side]) % NT).astype(jnp.int32)


def levels(own_key, shape, pieces, low, high):
    factor_of, own = 1.0, jax.random.fold_in(own_key, 6)
    for axis_at, blocks in pieces:
        steps = jnp.exp(jax.random.uniform(jax.random.fold_in(own, axis_at), (blocks,), jnp.float32, low / len(pieces), high / len(pieces)))
        factor_of = factor_of * jnp.repeat(steps, shape[axis_at] // blocks).reshape([-1 if axis == axis_at else 1 for axis in range(len(shape))])
    return factor_of


def normal_values(key, shape, spread, reach, cuts=(), held_as=jnp.bfloat16):
    level = levels(key, shape, cuts, -0.22, 0.18) if cuts else 1.0
    result = jax.random.normal(key, shape, jnp.float32) * spread * level
    return jnp.minimum(jnp.maximum(result, -reach), reach).astype(held_as)


def setup_inputs(seed: int = 0) -> dict:
    key_of = jax.random.split(jax.random.key(seed), 6)
    fields = normal_values(key_of[0], (ENS, NT, S, S, C), 1.0, 6.0, ((0, 2), (1, 16)))
    weight_first = normal_values(key_of[1], (3, 3, C, C), (9 * C) ** -0.5, 0.1875)
    weight_second = normal_values(key_of[2], (3, 3, C, C), (9 * C) ** -0.5, 0.1875)
    neighbours = draw_neighbours(jax.random.fold_in(key_of[5], 71), 0)
    cotangent = normal_values(key_of[4], (ENS, NT, S, S, C), 1.0, 6.0, ((0, 2), (1, 16)))
    return {"fields": fields, "weight_first": weight_first, "weight_second": weight_second, "neighbours": neighbours, "cotangent": cotangent}


root_half = 0.7071067811865476
inv_root_tau = 0.3989422804014327

def gelu_value(pre):
    return 0.5 * pre * (1.0 + lax.erf(pre * root_half))

def gelu_slope(pre):
    return 0.5 * (1.0 + lax.erf(pre * root_half)) + pre * jnp.exp(-0.5 * pre * pre) * inv_root_tau

def strips(block):
    top_row = block[..., 0, :, :]
    right_col = block[..., :, -1, :]
    bottom_row = block[..., -1, ::-1, :]
    left_col = block[..., ::-1, 0, :]
    return jnp.stack([top_row, right_col, bottom_row, left_col], axis=-3)

def assemble(block, halo_strips):
    top_row = halo_strips[..., 0, :, :]
    right_col = halo_strips[..., 1, :, :]
    bottom_row = halo_strips[..., 2, ::-1, :]
    left_col = halo_strips[..., 3, ::-1, :]
    corner_nw = 0.5 * (top_row[..., 0, :] + left_col[..., 0, :])
    corner_ne = 0.5 * (top_row[..., -1, :] + right_col[..., 0, :])
    corner_sw = 0.5 * (left_col[..., -1, :] + bottom_row[..., 0, :])
    corner_se = 0.5 * (bottom_row[..., -1, :] + right_col[..., -1, :])
    first_row = jnp.concatenate([corner_nw[..., None, :], top_row, corner_ne[..., None, :]], axis=-2)
    last_row = jnp.concatenate([corner_sw[..., None, :], bottom_row, corner_se[..., None, :]], axis=-2)
    middle = jnp.concatenate([left_col[..., :, None, :], block, right_col[..., :, None, :]], axis=-2)
    return jnp.concatenate([first_row[..., None, :, :], middle, last_row[..., None, :, :]], axis=-3)

def convolve(padded, weight):
    extent = padded.shape[-2] - 2
    accumulated = 0.0
    for a in range(3):
        for b in range(3):
            window = padded[..., a:a + extent, b:b + extent, :].reshape(-1, padded.shape[-1])
            accumulated = accumulated + jnp.dot(window, weight[a, b], preferred_element_type=jnp.float32)
    return accumulated.reshape(padded.shape[:-3] + (extent, extent, weight.shape[-1]))

def weight_grad(padded, delta):
    extent = delta.shape[-2]
    flat_delta = delta.reshape(-1, delta.shape[-1])
    tap_rows = []
    for a in range(3):
        tap_cols = []
        for b in range(3):
            window = padded[..., a:a + extent, b:b + extent, :].reshape(-1, padded.shape[-1])
            tap_cols.append(jnp.dot(window.T, flat_delta, preferred_element_type=jnp.float32))
        tap_rows.append(jnp.stack(tap_cols))
    return jnp.stack(tap_rows)

def convolve_back(delta, weight):
    flat_delta = delta.reshape(-1, delta.shape[-1])
    accumulated = 0.0
    for a in range(3):
        for b in range(3):
            term = jnp.dot(flat_delta, weight[a, b].T, preferred_element_type=jnp.float32)
            term = term.reshape(delta.shape[:-1] + (weight.shape[-2],))
            widths = [(0, 0)] * (delta.ndim - 3) + [(a, 2 - a), (b, 2 - b), (0, 0)]
            accumulated = accumulated + jnp.pad(term, widths)
    return accumulated

def pull_whole(own_strips, neighbours, facing):
    return own_strips[neighbours, facing][:, :, ::-1, :]

def forward_layer(block, weight, neighbours, facing):
    halo_strips = pull_whole(strips(block), neighbours, facing)
    padded = assemble(block.astype(jnp.float32), halo_strips.astype(jnp.float32)).astype(jnp.bfloat16)
    return (padded, halo_strips, convolve(padded, weight))

def backward_layer(block, halo_strips, delta, weight, neighbours, facing):
    grad_padded = convolve_back(delta, weight)
    unused, adjoint = jax.vjp(assemble, block.astype(jnp.float32), halo_strips.astype(jnp.float32))
    grad_block, grad_halo = adjoint(grad_padded)
    returned = pull_whole(grad_halo.astype(jnp.bfloat16), neighbours, facing)
    unused_two, strip_adjoint = jax.vjp(strips, block.astype(jnp.float32))
    rim_term, = strip_adjoint(returned.astype(jnp.float32))
    return grad_block + rim_term

def reference(fields, weight_first, weight_second, neighbours, cotangent):
    back_links = neighbours[neighbours]
    matches = back_links == jnp.arange(NT, dtype=jnp.int32)[:, None, None]
    facing = lax.optimization_barrier(jnp.sum(jnp.where(matches, jnp.arange(4, dtype=jnp.int32)[None, None, :], 0), axis=-1)).astype(jnp.int32)
    outputs = []
    grads = []
    grad_first = jnp.zeros((3, 3, C, C), jnp.float32)
    grad_second = jnp.zeros((3, 3, C, C), jnp.float32)
    for m in range(ENS):
        block = fields[m]
        padded_one, halo_one, first_pre = forward_layer(block, weight_first, neighbours, facing)
        hidden = gelu_value(first_pre).astype(jnp.bfloat16)
        padded_two, halo_two, second_pre = forward_layer(hidden, weight_second, neighbours, facing)
        outputs.append(gelu_value(second_pre).astype(jnp.bfloat16))
        delta_second = (cotangent[m].astype(jnp.float32) * gelu_slope(second_pre)).astype(jnp.bfloat16)
        grad_second = grad_second + weight_grad(padded_two, delta_second)
        grad_hidden = backward_layer(hidden, halo_two, delta_second, weight_second, neighbours, facing)
        delta_first = (grad_hidden * gelu_slope(first_pre)).astype(jnp.bfloat16)
        grad_first = grad_first + weight_grad(padded_one, delta_first)
        grad_block = backward_layer(block, halo_one, delta_first, weight_first, neighbours, facing)
        grads.append(grad_block.astype(jnp.bfloat16))
    return (jnp.stack(outputs), jnp.stack(grads), grad_first, grad_second)
```

```python
import jax
import jax.numpy as jnp
from jax import lax
from jax.sharding import PartitionSpec as P

root_half = 0.7071067811865476
inv_root_tau = 0.3989422804014327


def from_behind(block, axis, distance):
    devices = range(lax.axis_size(axis))
    route = [((i - distance) % len(devices), i) for i in devices]
    return lax.ppermute(block, axis, route)


def gelu_value(pre):
    return 0.5 * pre * (1.0 + lax.erf(pre * root_half))


def gelu_slope(pre):
    return 0.5 * (1.0 + lax.erf(pre * root_half)) + pre * jnp.exp(-0.5 * pre * pre) * inv_root_tau


def strips(block):
    top_row = block[..., 0, :, :]
    right_col = block[..., :, -1, :]
    bottom_row = block[..., -1, ::-1, :]
    left_col = block[..., ::-1, 0, :]
    return jnp.stack([top_row, right_col, bottom_row, left_col], axis=-3)


def assemble(block, halo_strips):
    top_row = halo_strips[..., 0, :, :]
    right_col = halo_strips[..., 1, :, :]
    bottom_row = halo_strips[..., 2, ::-1, :]
    left_col = halo_strips[..., 3, ::-1, :]
    corner_nw = 0.5 * (top_row[..., 0, :] + left_col[..., 0, :])
    corner_ne = 0.5 * (top_row[..., -1, :] + right_col[..., 0, :])
    corner_sw = 0.5 * (left_col[..., -1, :] + bottom_row[..., 0, :])
    corner_se = 0.5 * (bottom_row[..., -1, :] + right_col[..., -1, :])
    first_row = jnp.concatenate(
        [corner_nw[..., None, :], top_row, corner_ne[..., None, :]], axis=-2
    )
    last_row = jnp.concatenate(
        [corner_sw[..., None, :], bottom_row, corner_se[..., None, :]], axis=-2
    )
    middle = jnp.concatenate(
        [left_col[..., :, None, :], block, right_col[..., :, None, :]], axis=-2
    )
    return jnp.concatenate([first_row[..., None, :, :], middle, last_row[..., None, :, :]], axis=-3)


def convolve(padded, weight):
    extent = padded.shape[-2] - 2
    accumulated = 0.0
    for a in range(3):
        for b in range(3):
            window = padded[..., a : a + extent, b : b + extent, :].reshape(-1, padded.shape[-1])
            accumulated = accumulated + jnp.dot(
                window, weight[a, b], preferred_element_type=jnp.float32
            )
    return accumulated.reshape(padded.shape[:-3] + (extent, extent, weight.shape[-1]))


def weight_grad(padded, delta):
    extent = delta.shape[-2]
    flat_delta = delta.reshape(-1, delta.shape[-1])
    tap_rows = []
    for a in range(3):
        tap_cols = []
        for b in range(3):
            window = padded[..., a : a + extent, b : b + extent, :].reshape(-1, padded.shape[-1])
            tap_cols.append(jnp.dot(window.T, flat_delta, preferred_element_type=jnp.float32))
        tap_rows.append(jnp.stack(tap_cols))
    return jnp.stack(tap_rows)


def convolve_back(delta, weight):
    flat_delta = delta.reshape(-1, delta.shape[-1])
    accumulated = 0.0
    for a in range(3):
        for b in range(3):
            term = jnp.dot(flat_delta, weight[a, b].T, preferred_element_type=jnp.float32)
            term = term.reshape(delta.shape[:-1] + (weight.shape[-2],))
            widths = [(0, 0)] * (delta.ndim - 3) + [(a, 2 - a), (b, 2 - b), (0, 0)]
            accumulated = accumulated + jnp.pad(term, widths)
    return accumulated


def pull_strips(own_strips, neighbours, returning):
    tile_index = lax.axis_index("tile")
    tile_count = lax.axis_size("tile")
    row_length = max(4, tile_count // 8)
    offsets = [1, -1, row_length, -row_length]
    own_links = lax.dynamic_slice(neighbours, (tile_index, 0), (1, 4))[0]
    relative = (own_links - tile_index) % tile_count
    strip_width = own_strips.shape[1] * own_strips.shape[2]
    flattened = own_strips.reshape(4, strip_width)
    received = []
    for offset in offsets:
        if returning:
            bundle = from_behind(flattened, "tile", -offset)
        else:
            bundle = from_behind(flattened, "tile", -offset)
        sender = (tile_index + offset) % tile_count
        sender_links = lax.dynamic_slice(neighbours, (sender, 0), (1, 4))
        choose_side = (sender_links == tile_index).astype(jnp.bfloat16)
        incoming = jnp.dot(choose_side, bundle, preferred_element_type=jnp.float32).astype(
            jnp.bfloat16
        )
        received.append(incoming)
    stacked = jnp.concatenate(received, axis=0)
    targets = jnp.array([offset % tile_count for offset in offsets], jnp.int32)
    direction_hit = (relative[:, None] == targets[None, :]).astype(jnp.bfloat16)
    halo_strips = jnp.dot(direction_hit, stacked, preferred_element_type=jnp.float32).astype(
        jnp.bfloat16
    )
    return halo_strips.reshape(own_strips.shape)[:, ::-1, :]


def forward_layer(block, weight, neighbours):
    halo_strips = pull_strips(strips(block), neighbours, False)
    padded = assemble(block.astype(jnp.float32), halo_strips.astype(jnp.float32)).astype(
        jnp.bfloat16
    )
    return (padded, halo_strips, convolve(padded, weight))


def backward_layer(block, halo_strips, delta, weight, neighbours):
    grad_padded = convolve_back(delta, weight)
    unused, adjoint = jax.vjp(assemble, block.astype(jnp.float32), halo_strips.astype(jnp.float32))
    grad_block, grad_halo = adjoint(grad_padded)
    returned = pull_strips(grad_halo.astype(jnp.bfloat16), neighbours, True)
    unused_two, strip_adjoint = jax.vjp(strips, block.astype(jnp.float32))
    (rim_term,) = strip_adjoint(returned.astype(jnp.float32))
    return grad_block + rim_term


def flip_swap(block, mask_ens, mask_tile):
    ens, tile = lax.axis_size("ens"), lax.axis_size("tile")
    route = [
        (e * tile + t, (e ^ mask_ens) * tile + (t ^ mask_tile))
        for e in range(ens)
        for t in range(tile)
    ]
    return lax.ppermute(block, ("ens", "tile"), route)


def pick(parts, index):
    return lax.dynamic_index_in_dim(parts, index, 0, keepdims=False)


def all_sum(block):
    tile = lax.axis_index("tile")
    core = tile & 1
    rows, lanes = block.shape
    halves = block.reshape(2, rows // 2, lanes)
    given = flip_swap(pick(halves, 1 - core).astype(jnp.bfloat16), 0, 1)
    part = pick(halves, core) + given.astype(jnp.float32)
    seat = lax.axis_index("ens") * 2 + (tile >> 1 & 1)
    quarters = part.reshape(4, rows // 8, lanes)
    sent = quarters.astype(jnp.bfloat16)
    part = pick(quarters, seat)
    for k in (1, 2, 3):
        part = part + flip_swap(pick(sent, seat ^ k), k >> 1, (k & 1) << 1).astype(jnp.float32)
    bit = 4
    while bit < lax.axis_size("tile"):
        own = part.astype(jnp.bfloat16)
        part = lax.reduce_precision(part, 8, 7)
        if bit * 2 < lax.axis_size("tile"):
            one, two, three = (flip_swap(own, 0, bit * k).astype(jnp.float32) for k in (1, 2, 3))
            part = (part + one) + (two + three)
            bit *= 4
        else:
            part = part + flip_swap(own, 0, bit).astype(jnp.float32)
            bit *= 2
    part = part.astype(jnp.bfloat16)
    whole = jnp.zeros((4,) + part.shape, part.dtype)
    whole = lax.dynamic_update_index_in_dim(whole, part, seat, 0)
    for k in (1, 2, 3):
        got = flip_swap(part, k >> 1, (k & 1) << 1)
        whole = lax.dynamic_update_index_in_dim(whole, got, seat ^ k, 0)
    half = whole.reshape(rows // 2, lanes)
    other = flip_swap(half, 0, 1)
    return jnp.concatenate([jnp.where(core == 0, half, other), jnp.where(core == 0, other, half)])


def local(fields, weight_first, weight_second, neighbours, cotangent):
    block = fields[0, 0]
    padded_one, halo_one, first_pre = forward_layer(block, weight_first, neighbours)
    hidden = gelu_value(first_pre).astype(jnp.bfloat16)
    padded_two, halo_two, second_pre = forward_layer(hidden, weight_second, neighbours)
    out_field = gelu_value(second_pre).astype(jnp.bfloat16)
    delta_second = (cotangent[0, 0].astype(jnp.float32) * gelu_slope(second_pre)).astype(
        jnp.bfloat16
    )
    grad_second = weight_grad(padded_two, delta_second)
    grad_hidden = backward_layer(hidden, halo_two, delta_second, weight_second, neighbours)
    delta_first = (grad_hidden * gelu_slope(first_pre)).astype(jnp.bfloat16)
    grad_first = weight_grad(padded_one, delta_first)
    grad_block = backward_layer(block, halo_one, delta_first, weight_first, neighbours)
    shape = grad_first.shape
    both = jnp.stack([grad_first, grad_second]).reshape(-1, shape[-1])
    both = all_sum(both).astype(jnp.float32).reshape((2,) + shape)
    grad_first, grad_second = both[0], both[1]
    return (
        out_field[None, None],
        grad_block.astype(jnp.bfloat16)[None, None],
        grad_first,
        grad_second,
    )


def solution(mesh):
    placed = (P("ens", "tile", None, None, None), P(), P(), P(), P("ens", "tile", None, None, None))
    return jax.shard_map(
        local,
        mesh=mesh,
        in_specs=placed,
        out_specs=(
            P("ens", "tile", None, None, None),
            P("ens", "tile", None, None, None),
            P(),
            P(),
        ),
        check_vma=False,
    )
```

```python
import functools

import jax
import jax.numpy as jnp
from jax import lax
from jax.experimental import pallas as pl
from jax.experimental.pallas import tpu as pltpu
from jax.sharding import PartitionSpec as P

root_half = 0.7071067811865476
inv_root_tau = 0.3989422804014327
bf16, f32 = jnp.bfloat16, jnp.float32
NT = (((1,), (1,)), ((), ()))
TN = (((0,), (0,)), ((), ()))


def gelu_both(pre):
    bell = 0.5 * (1.0 + lax.erf(pre * root_half))
    return pre * bell, bell + pre * jnp.exp(-0.5 * pre * pre) * inv_root_tau


def partners(index, count, cols):
    odd, row_odd = index & 1, (index // cols) & 1
    return [
        (index + cols * (2 * row_odd - 1) + count) % count,
        (index + cols * (1 - 2 * row_odd) + count) % count,
        (index - 1 + 2 * odd + count) % count,
        (index + 1 - 2 * odd + count) % count,
    ]


def links(table, cols):
    count = lax.axis_size("tile")
    me = lax.axis_index("tile")
    found = []
    for other in partners(me, count, cols):
        side, back = jnp.int32(0), jnp.int32(0)
        for s in range(1, 4):
            side = jnp.where(table[me, s] == other, s, side)
            back = jnp.where(table[other, s] == me, s, back)
        found.append((side, (side >= 2) == (back >= 2)))
    return found


def send_strips(table, cols, strips, outs):
    size = strips.shape[1]
    at_row = lax.broadcasted_iota(jnp.int32, (size, size), 0)
    at_col = lax.broadcasted_iota(jnp.int32, (size, size), 1)
    for (side, turn), out in zip(links(table, cols), outs):
        order = (at_col == jnp.where(turn, size - 1 - at_row, at_row)).astype(f32).astype(bf16)
        out[...] = jnp.dot(order, strips[side].astype(bf16), preferred_element_type=f32).astype(
            bf16
        )


def take_strips(table, cols, received, strips):
    for (side, _), block in zip(links(table, cols), received):
        strips[side] = block[...].astype(f32)


def swap_all(blocks, cols):
    count = lax.axis_size("tile")
    ways = [partners(p, count, cols) for p in range(count)]
    return [
        lax.ppermute(block, "tile", [(p, ways[p][k]) for p in range(count)])
        for k, block in enumerate(blocks)
    ]


def fill_columns(shifted, pairs):
    count, size, lanes = pairs.shape
    c = lanes // 2
    at = lax.broadcasted_iota(jnp.int32, (size, c), 0)
    first, last = at == 0, at == size - 1
    shifted[0:size, 0 : 3 * c] = jnp.zeros((size, 3 * c), bf16)
    shifted[count * size :, 3 * c :] = jnp.zeros((size, 3 * c), bf16)
    for i in range(count):
        for parity, row, lane in ((1, (i + 1) * size, 0), (0, i * size, 3 * c)):
            value = pairs[i, :, parity * c : (parity + 1) * c].astype(f32)
            before = jnp.where(first, 0.0, pltpu.roll(value, 1, 0))
            after = jnp.where(last, 0.0, pltpu.roll(value, size - 1, 0))
            shifted[row : row + size, lane : lane + c] = before.astype(bf16)
            shifted[row : row + size, lane + c : lane + 2 * c] = value.astype(bf16)
            shifted[row : row + size, lane + 2 * c : lane + 3 * c] = after.astype(bf16)


def blocks_of_pairs(tap, lower, upper, c):
    for b in range(3):
        for half, parity, target, a in (
            (lower, 0, 0, 0),
            (lower, 0, 1, None),
            (lower, 1, 0, 1),
            (lower, 1, 1, 0),
            (upper, 0, 0, 2),
            (upper, 0, 1, 1),
            (upper, 1, 0, None),
            (upper, 1, 1, 2),
        ):
            yield half, (parity * 3 + b) * c, target * c, tap(a, b) if a is not None else None


def bulk_conv(shifted, weight, lower, upper, out, backward):
    c = weight.shape[-1]
    count, size, lanes = out.shape
    if backward:
        tap = lambda a, b: weight[(2 - a) * 3 + 2 - b]
    else:
        tap = lambda a, b: weight[a * 3 + b]
    for half, depth, target, block in blocks_of_pairs(tap, lower, upper, c):
        if block is None:
            block = jnp.zeros((c, c), bf16)
        if backward:
            half[target : target + c, depth : depth + c] = block
        else:
            half[depth : depth + c, target : target + c] = block
    rows = count * size
    dims = NT if backward else (((1,), (0,)), ((), ()))
    total = lax.dot_general(
        shifted[0:rows, :], lower[...], dims, preferred_element_type=f32
    ) + lax.dot_general(shifted[size : size + rows, :], upper[...], dims, preferred_element_type=f32)
    out[...] = total.reshape(count, size, lanes)


def bulk_weight_grad(shifted, delta, out):
    count, size, lanes = delta.shape
    c = lanes // 2
    rows = count * size
    flat = delta[...].reshape(rows, lanes)
    low = lax.dot_general(shifted[0:rows, :], flat, TN, preferred_element_type=f32)
    high = lax.dot_general(shifted[size : size + rows, :], flat, TN, preferred_element_type=f32)
    for b in range(3):
        here, there = b * c, (3 + b) * c
        out[b] = low[here : here + c, 0:c] + low[there : there + c, c:]
        out[3 + b] = low[there : there + c, 0:c] + high[here : here + c, c:]
        out[6 + b] = high[here : here + c, 0:c] + high[there : there + c, c:]


def load_edges(left, right, top, bottom):
    return left[...], right[...], top[0], bottom[0]


def to_pairs(strip, room):
    room[...] = strip
    half = strip.shape[0] // 2
    return jnp.concatenate(
        [room[pl.ds(0, half, stride=2), :], room[pl.ds(1, half, stride=2), :]], axis=1
    )


def add_strips(edges, strips, rooms):
    left, right, top, bottom = edges
    t, r, b, l = strips
    c = t.shape[1]
    half, depth, size = left.shape[0], left.shape[1], t.shape[0]
    at = lax.broadcasted_iota(jnp.int32, left.shape, 1)
    left_room, right_room, top_room, bottom_room, strip_a, strip_b = rooms
    left_room[...] = left + jnp.where(at == 0, to_pairs(l, strip_a)[:, None, :], 0.0)
    right_room[...] = right + jnp.where(at == depth - 1, to_pairs(r, strip_b)[:, None, :], 0.0)
    left_room[0, :, 0:c] += t[0:depth]
    left_room[half - 1, :, c:] += b[0:depth]
    right_room[0, :, 0:c] += t[size - depth :]
    right_room[half - 1, :, c:] += b[size - depth :]
    top_room[...] = top + t
    bottom_room[...] = bottom + b
    top_room[0:depth] = left_room[0, :, 0:c]
    top_room[size - depth :] = right_room[0, :, 0:c]
    bottom_room[0:depth] = left_room[half - 1, :, c:]
    bottom_room[size - depth :] = right_room[half - 1, :, c:]
    return left_room[...], right_room[...], top_room[...], bottom_room[...]


def edge_strips(edges, strips):
    left, right, top, bottom = edges
    c = top.shape[1]
    half = left.shape[0]
    strips[0] = top
    strips[2] = bottom
    for side, column in ((1, right[:, -1, :]), (3, left[:, 0, :])):
        strips[side, pl.ds(0, half, stride=2), :] = column[:, 0:c]
        strips[side, pl.ds(1, half, stride=2), :] = column[:, c:]


def lay_edges(pairs, left, right, top, bottom):
    depth = left.shape[1]
    size = pairs.shape[1]
    c = top.shape[-1]
    pairs[:, 0:depth, :] = left[...]
    pairs[:, size - depth :, :] = right[...]
    pairs[0, :, 0:c] = top[...]
    pairs[pairs.shape[0] - 1, :, c:] = bottom[...]


def halo_windows(strips, rooms):
    size = strips.shape[1]
    top, right, bottom, left = (strips[s] for s in range(4))
    zero = jnp.zeros_like(top[0:1])
    ends = [
        (0.5 * (top[0:1] + left[0:1]), 0.5 * (top[size - 1 :] + right[0:1])),
        (zero, zero),
        (0.5 * (left[size - 1 :] + bottom[0:1]), 0.5 * (bottom[size - 1 :] + right[size - 1 :])),
        (zero, zero),
    ]
    windows = []
    for s, (strip, (before, after)) in enumerate(zip((top, right, bottom, left), ends)):
        rooms[s, 7:8, :] = before
        rooms[s, 8 : 8 + size, :] = strip
        rooms[s, 8 + size : 9 + size, :] = after
        windows.append(
            jnp.concatenate([rooms[s, 7 + k : 7 + k + size, :] for k in range(3)], axis=1).astype(
                bf16
            )
        )
    return windows


side_taps = ((0, 1, 2), (2, 5, 8), (6, 7, 8), (0, 3, 6))


def halo_terms(windows, weight):
    return [
        jnp.dot(
            window,
            jnp.concatenate([weight[tap] for tap in taps], axis=0),
            preferred_element_type=f32,
        )
        for window, taps in zip(windows, side_taps)
    ]


def halo_weight_grad(windows, strips, out):
    c = out.shape[-1]
    for s, (window, taps) in enumerate(zip(windows, side_taps)):
        term = lax.dot_general(window, strips[s].astype(bf16), TN, preferred_element_type=f32)
        for k, tap in enumerate(taps):
            out[tap] += term[k * c : (k + 1) * c]


def halo_grads(strips, weight, rooms, grads):
    size, c = strips.shape[1:]
    long = size + 8
    for s, taps in enumerate(side_taps):
        rooms[s, 0:8, :] = jnp.zeros((8, c), f32)
        rooms[s, 8 : 8 + size, :] = strips[s]
        rooms[s, 8 + size :, :] = jnp.zeros((8, c), f32)
        copies = jnp.concatenate([rooms[s, 8 - k : 8 - k + long, :] for k in range(3)], axis=1)
        rims = jnp.concatenate([weight[tap] for tap in taps], axis=1)
        rim = lax.dot_general(copies.astype(bf16), rims, NT, preferred_element_type=f32)
        rooms[s, 0:long, :] = rim
        at = lax.broadcasted_iota(jnp.int32, (size, c), 0)
        corner = jnp.where(at == 0, rooms[s, 0:1, :], 0.0) + jnp.where(
            at == size - 1, rooms[s, size + 1 : size + 2, :], 0.0
        )
        grads[s] = rooms[s, 1 : 1 + size, :] + 0.5 * corner


def exact(values):
    return [value.astype(bf16).astype(f32) for value in values]


def first_strips(cols, table, block, *refs):
    outs, strips = refs[:4], refs[4]
    size = block.shape[0]
    strips[0] = block[0].astype(f32)
    strips[2] = block[size - 1].astype(f32)
    strips[3] = block[:, 0:16, :].astype(f32)[:, 0, :]
    strips[1] = block[:, size - 16 :, :].astype(f32)[:, 15, :]
    send_strips(table, cols, strips, outs)


def first_bulk(block, weight, shifted, pre, hidden, slope, pairs, lower, upper):
    count, size, lanes = pre.shape
    c = lanes // 2
    for i in range(count):
        pairs[i, :, 0:c] = block[2 * i]
        pairs[i, :, c:] = block[2 * i + 1]
    fill_columns(shifted, pairs)
    bulk_conv(shifted, weight, lower, upper, pre, False)
    for i in range(count):
        value, rate = gelu_both(pre[i])
        hidden[i] = value.astype(bf16)
        slope[i] = rate.astype(bf16)


def first_edges(cols, table, *refs):
    received, weight, blocks = refs[:4], refs[4], refs[5:9]
    outs, hidden, slope, halo = refs[9:13], refs[13:17], refs[17:21], refs[21]
    rooms, strips, long = refs[22:28], refs[28], refs[29]
    take_strips(table, cols, received, halo)
    terms = halo_terms(halo_windows(halo, long), weight)
    edges = add_strips(load_edges(*blocks), terms, rooms)
    both = [gelu_both(edge) for edge in edges]
    values = exact([value for value, _ in both])
    for k in range(4):
        hidden[k][...] = values[k]
        slope[k][...] = both[k][1]
    edge_strips(values, strips)
    send_strips(table, cols, strips, outs)


def second_bulk(hidden, left, right, top, bottom, weight, cotangent, *refs):
    shifted, pre, out_field, delta, pairs, lower, upper = refs
    count, size, lanes = pre.shape
    c = lanes // 2
    pairs[...] = hidden[...].astype(f32)
    lay_edges(pairs, left, right, top, bottom)
    fill_columns(shifted, pairs)
    bulk_conv(shifted, weight, lower, upper, pre, False)
    for i in range(count):
        for parity in range(2):
            part = slice(parity * c, (parity + 1) * c)
            value, rate = gelu_both(pre[i, :, part])
            out_field[i, :, part] = value.astype(bf16)
            delta[i, :, part] = (cotangent[2 * i + parity].astype(f32) * rate).astype(bf16)


def second_edges(cols, table, *refs):
    received, weight, blocks, wanted = refs[:4], refs[4], refs[5:9], refs[9:13]
    outs, out_field, delta, halo = refs[13:17], refs[17:21], refs[21:25], refs[25]
    rooms, strips, long, grads = refs[26:32], refs[32], refs[33], refs[34]
    half, depth = blocks[0].shape[:2]
    take_strips(table, cols, received, halo)
    terms = halo_terms(halo_windows(halo, long), weight)
    edges = add_strips(load_edges(*blocks), terms, rooms)
    cots = []
    for ref, at in ((wanted[0], 0), (wanted[1], 16 - depth)):
        block = ref[...].astype(f32)
        block = block.reshape((half, 2) + block.shape[1:])[:, :, at : at + depth, :]
        cots.append(jnp.concatenate([block[:, 0], block[:, 1]], axis=-1))
    cots += [wanted[2][0].astype(f32), wanted[3][0].astype(f32)]
    both = [gelu_both(edge) for edge in edges]
    deltas = exact([cot * rate for cot, (_, rate) in zip(cots, both)])
    for k in range(4):
        out_field[k][...] = both[k][0]
        delta[k][...] = deltas[k]
    edge_strips(deltas, strips)
    halo_grads(strips, weight, long, grads)
    send_strips(table, cols, grads, outs)


def second_back(*refs):
    bulk_out, bulk_delta, out_edges, delta_edges, halo = (
        refs[0],
        refs[1],
        refs[2:6],
        refs[6:10],
        refs[10],
    )
    shifted, weight, bulk_slope = refs[11:14]
    out_field, grad_weight, grad_hidden, delta_first = refs[14:18]
    pairs, delta, lower, upper, moved, strips, long = refs[18:25]
    count, size, lanes = pairs.shape
    c = lanes // 2
    pairs[...] = bulk_out[...].astype(f32)
    lay_edges(pairs, *out_edges)
    for i in range(count):
        out_field[2 * i] = pairs[i, :, 0:c].astype(bf16)
        out_field[2 * i + 1] = pairs[i, :, c:].astype(bf16)
    pairs[...] = bulk_delta[...].astype(f32)
    lay_edges(pairs, *delta_edges)
    delta[...] = pairs[...].astype(bf16)
    bulk_weight_grad(shifted, delta, grad_weight)
    edge_strips([ref[...] for ref in delta_edges], strips)
    halo_weight_grad(halo_windows(halo, long), strips, grad_weight)
    fill_columns(moved, pairs)
    bulk_conv(moved, weight, lower, upper, grad_hidden, True)
    for i in range(count):
        delta_first[i] = (grad_hidden[i] * bulk_slope[i].astype(f32)).astype(bf16)


def first_back(cols, table, *refs):
    received, weight, blocks, slope, bulk_delta = (
        refs[:4],
        refs[4],
        refs[5:9],
        refs[9:13],
        refs[13],
    )
    halo, shifted, other_grad = refs[14:17]
    outs, delta, kept, given = refs[17:21], refs[21], refs[22], refs[23]
    rooms, strips, long, grads, back, pairs, grad_weight = (
        refs[24:30],
        refs[30],
        refs[31],
        refs[32],
        refs[33],
        refs[34],
        refs[35],
    )
    take_strips(table, cols, received, back)
    edges = add_strips(load_edges(*blocks), [back[s] for s in range(4)], rooms)
    deltas = exact([edge * rate[...] for edge, rate in zip(edges, slope)])
    edge_strips(deltas, strips)
    halo_grads(strips, weight, long, grads)
    send_strips(table, cols, grads, outs)
    pairs[...] = bulk_delta[...].astype(f32)
    lay_edges(pairs, *deltas)
    delta[...] = pairs[...].astype(bf16)
    bulk_weight_grad(shifted, delta, grad_weight)
    halo_weight_grad(halo_windows(halo, long), strips, grad_weight)
    core = lax.axis_index("tile") & 1
    for tap in range(grad_weight.shape[0]):
        one, two = grad_weight[tap], other_grad[tap]
        kept[tap] = jnp.where(core == 0, one, two)
        given[tap] = jnp.where(core == 0, two, one).astype(bf16)


def last_bulk(delta, weight, interior, pairs, moved, lower, upper):
    pairs[...] = delta[...].astype(f32)
    fill_columns(moved, pairs)
    bulk_conv(moved, weight, lower, upper, interior, True)


def last_edges(cols, table, *refs):
    received, interior, grad = refs[:4], refs[4], refs[5]
    rooms, back, pairs = refs[6:12], refs[12], refs[13]
    count, size, lanes = interior.shape
    c = lanes // 2
    take_strips(table, cols, received, back)
    edges = (
        interior[:, 0:8, :],
        interior[:, size - 8 :, :],
        interior[0, :, 0:c],
        interior[count - 1, :, c:],
    )
    edges = add_strips(edges, [back[s] for s in range(4)], rooms)
    pairs[...] = interior[...]
    lay_edges(pairs, *edges)
    for i in range(count):
        grad[2 * i] = pairs[i, :, 0:c].astype(bf16)
        grad[2 * i + 1] = pairs[i, :, c:].astype(bf16)


def flip_swap(block, mask_ens, mask_tile):
    ens, tile = lax.axis_size("ens"), lax.axis_size("tile")
    route = [
        (e * tile + t, (e ^ mask_ens) * tile + (t ^ mask_tile))
        for e in range(ens)
        for t in range(tile)
    ]
    return lax.ppermute(block, ("ens", "tile"), route)


def pick(parts, index):
    return lax.dynamic_index_in_dim(parts, index, 0, keepdims=False)


def all_sum(kept, given):
    tile = lax.axis_index("tile")
    rows, lanes = kept.shape
    part = kept + flip_swap(given, 0, 1).astype(f32)
    seat = lax.axis_index("ens") * 2 + (tile >> 1 & 1)
    quarters = part.reshape(4, rows // 4, lanes)
    sent = quarters.astype(bf16)
    part = pick(quarters, seat)
    for k in (1, 2, 3):
        part = part + flip_swap(pick(sent, seat ^ k), k >> 1, (k & 1) << 1).astype(f32)
    bit = 4
    while bit < lax.axis_size("tile"):
        own = part.astype(bf16)
        part = lax.reduce_precision(part, 8, 7)
        if bit * 2 < lax.axis_size("tile"):
            one, two, three = (flip_swap(own, 0, bit * k).astype(f32) for k in (1, 2, 3))
            part = (part + one) + (two + three)
            bit *= 4
        else:
            part = part + flip_swap(own, 0, bit).astype(f32)
            bit *= 2
    part = part.astype(bf16)
    whole = jnp.zeros((4,) + part.shape, part.dtype)
    whole = lax.dynamic_update_index_in_dim(whole, part, seat, 0)
    for k in (1, 2, 3):
        got = flip_swap(part, k >> 1, (k & 1) << 1)
        whole = lax.dynamic_update_index_in_dim(whole, got, seat ^ k, 0)
    half = whole.reshape(rows, lanes)
    other = flip_swap(half, 0, 1)
    first = (tile & 1) == 0
    return jnp.where(first, half, other), jnp.where(first, other, half)


def call(kernel, name, ins, outs, scratch, cost=0):
    whole = pl.BlockSpec(memory_space=pltpu.VMEM)
    return pl.pallas_call(
        kernel,
        name=name,
        grid=(1,),
        in_specs=[spec or whole for _, spec in ins],
        out_specs=[whole] * len(outs),
        out_shape=outs,
        scratch_shapes=scratch,
        compiler_params=pltpu.CompilerParams(vmem_limit_bytes=40 << 20),
        cost_estimate=pl.CostEstimate(flops=cost, bytes_accessed=2 << 20, transcendentals=0),
    )(*[array for array, _ in ins])


def local(fields, weight_first, weight_second, neighbours, cotangent):
    block, wanted = fields[0, 0], cotangent[0, 0]
    size, c = block.shape[0], block.shape[-1]
    half = size // 2
    count = lax.axis_size("tile")
    cols = max(4, count // 8)
    shape = weight_first.shape
    one, two = weight_first.reshape(9, c, c), weight_second.reshape(9, c, c)
    flops = 2 * size * size * 9 * c * c

    S = jax.ShapeDtypeStruct
    table = (neighbours, pl.BlockSpec(memory_space=pltpu.SMEM))
    sent = [S((size, c), bf16)] * 4
    halo = S((4, size, c), f32)
    edge = [S((half, 8, 2 * c), f32)] * 2 + [S((size, c), f32)] * 2
    pairs = lambda kind: S((half, size, 2 * c), kind)
    shifted = S(((half + 1) * size, 6 * c), bf16)
    V = lambda leaf: pltpu.VMEM(leaf.shape, leaf.dtype)
    ahead = [pltpu.VMEM((6 * c, 2 * c), bf16)] * 2
    back = [pltpu.VMEM((2 * c, 6 * c), bf16)] * 2
    rooms = [V(leaf) for leaf in edge] + [pltpu.VMEM((size, c), f32)] * 2
    long = pltpu.VMEM((4, size + 16, c), f32)
    whole = lambda arrays: [(array, None) for array in arrays]

    def edge_blocks(array):
        last = size // 8 - 1
        return [
            (array, pl.BlockSpec((half, 8, 2 * c), lambda step: (0, 0, 0))),
            (array, pl.BlockSpec((half, 8, 2 * c), lambda step: (0, last, 0))),
            (array, pl.BlockSpec((1, size, c), lambda step: (0, 0, 0))),
            (array, pl.BlockSpec((1, size, c), lambda step: (half - 1, 0, 1))),
        ]

    def image_edges(array):
        last = size // 16 - 1
        return [
            (array, pl.BlockSpec((size, 16, c), lambda step: (0, 0, 0))),
            (array, pl.BlockSpec((size, 16, c), lambda step: (0, last, 0))),
            (array, pl.BlockSpec((1, size, c), lambda step: (0, 0, 0))),
            (array, pl.BlockSpec((1, size, c), lambda step: (size - 1, 0, 0))),
        ]

    strips = call(
        functools.partial(first_strips, cols),
        "first_strips",
        [table, (block, None)],
        sent,
        [V(halo)],
    )
    strips = swap_all(strips, cols)
    shifted_one, pre_one, hidden, slope = call(
        first_bulk,
        "first_bulk",
        whole([block, one]),
        [shifted, pairs(f32), pairs(bf16), pairs(bf16)],
        [V(pairs(bf16))] + ahead,
        flops,
    )
    found = call(
        functools.partial(first_edges, cols),
        "first_edges",
        [table] + whole(strips) + [(one, None)] + edge_blocks(pre_one),
        sent + edge + edge + [halo],
        rooms + [V(halo), long],
    )
    strips, hidden_edges, slope_edges, halo_one = found[:4], found[4:8], found[8:12], found[12]
    strips = swap_all(strips, cols)
    shifted_two, pre_two, out_bulk, delta_bulk = call(
        second_bulk,
        "second_bulk",
        whole([hidden, *hidden_edges, two, wanted]),
        [shifted, pairs(f32), pairs(bf16), pairs(bf16)],
        [V(pairs(f32))] + ahead,
        flops,
    )
    found = call(
        functools.partial(second_edges, cols),
        "second_edges",
        [table] + whole(strips) + [(two, None)] + edge_blocks(pre_two) + image_edges(wanted),
        sent + edge + edge + [halo],
        rooms + [V(halo), long, V(halo)],
    )
    strips, out_edges, delta_edges, halo_two = found[:4], found[4:8], found[8:12], found[12]
    strips = swap_all(strips, cols)
    out_field, grad_two, grad_hidden, delta_one = call(
        second_back,
        "second_back",
        whole(
            [out_bulk, delta_bulk, *out_edges, *delta_edges, halo_two, shifted_two, two, slope]
        ),
        [S(block.shape, bf16), S((9, c, c), f32), pairs(f32), pairs(bf16)],
        [V(pairs(f32)), V(pairs(bf16))] + back + [V(shifted), V(halo), long],
        2 * flops,
    )
    found = call(
        functools.partial(first_back, cols),
        "first_back",
        [table]
        + whole(strips)
        + [(one, None)]
        + edge_blocks(grad_hidden)
        + whole([*slope_edges, delta_one, halo_one, shifted_one, grad_two]),
        sent + [pairs(bf16), S((9, c, c), f32), S((9, c, c), bf16)],
        rooms
        + [V(halo), long, V(halo), V(halo), V(pairs(f32)), pltpu.VMEM((9, c, c), f32)],
        flops,
    )
    strips, delta_one, kept, given = found[:4], *found[4:7]
    strips = swap_all(strips, cols)
    (interior,) = call(
        last_bulk,
        "last_bulk",
        whole([delta_one, one]),
        [pairs(f32)],
        [V(pairs(f32)), V(shifted)] + back,
        flops,
    )
    (grad_block,) = call(
        functools.partial(last_edges, cols),
        "last_edges",
        [table] + whole([*strips, interior]),
        [S(block.shape, bf16)],
        rooms + [V(halo), V(pairs(f32))],
    )
    grads = all_sum(kept.reshape(9 * c, c), given.reshape(9 * c, c))
    grad_first, grad_second = (grad.astype(f32).reshape(shape) for grad in grads)
    return (out_field[None, None], grad_block[None, None], grad_first, grad_second)


def solution(mesh):
    placed = (P("ens", "tile", None, None, None), P(), P(), P(), P("ens", "tile", None, None, None))
    return jax.shard_map(
        local,
        mesh=mesh,
        in_specs=placed,
        out_specs=(
            P("ens", "tile", None, None, None),
            P("ens", "tile", None, None, None),
            P(),
            P(),
        ),
        check_vma=False,
    )
```

```python
import functools

import jax
import jax.numpy as jnp
from jax import lax
from jax.experimental import pallas as pl
from jax.experimental.pallas import tpu as pltpu
from jax.sharding import PartitionSpec as P

root_half = 0.7071067811865476
inv_root_tau = 0.3989422804014327
bf16, f32 = jnp.bfloat16, jnp.float32
NT = (((1,), (1,)), ((), ()))
TN = (((0,), (0,)), ((), ()))


def gelu_both(pre):
    bell = 0.5 * (1.0 + lax.erf(pre * root_half))
    return pre * bell, bell + pre * jnp.exp(-0.5 * pre * pre) * inv_root_tau


def partners(index, count, cols):
    odd, row_odd = index & 1, (index // cols) & 1
    return [
        (index + cols * (2 * row_odd - 1) + count) % count,
        (index + cols * (1 - 2 * row_odd) + count) % count,
        (index - 1 + 2 * odd + count) % count,
        (index + 1 - 2 * odd + count) % count,
    ]


def write_links(table, cols, found):
    count = lax.axis_size("tile")
    me = lax.axis_index("tile")
    for k, other in enumerate(partners(me, count, cols)):
        side, back = jnp.int32(0), jnp.int32(0)
        for s in range(1, 4):
            side = jnp.where(table[s, me] == other, s, side)
            back = jnp.where(table[s, other] == me, s, back)
        turn = jnp.where((side >= 2) == (back >= 2), 1, 0)
        found[k] = jnp.full(found.shape[1:], side, jnp.int32)
        found[4 + k] = jnp.full(found.shape[1:], turn, jnp.int32)


def send_strips(found, strips, outs):
    _, size, c = strips.shape
    at_row = lax.broadcasted_iota(jnp.int32, (size, size), 0)
    at_col = lax.broadcasted_iota(jnp.int32, (size, size), 1)
    for k, out in enumerate(outs):
        turn = found[4 + k][0:1, 0:size] == 1
        order = (at_col == jnp.where(turn, size - 1 - at_row, at_row)).astype(f32).astype(bf16)
        side = found[k][None]
        chosen = jnp.zeros((size // 8, 8, c), f32)
        for s in range(4):
            chosen = jnp.where(side == s, strips[s].reshape(chosen.shape), chosen)
        chosen = chosen.reshape(size, c).astype(bf16)
        out[...] = jnp.dot(order, chosen, preferred_element_type=f32).astype(bf16)


def take_strips(found, received, strips):
    _, size, c = strips.shape
    blocks = [block[...].astype(f32).reshape(size // 8, 8, c) for block in received]
    for s in range(4):
        taken = blocks[0]
        for k in range(1, 4):
            taken = jnp.where(found[k][None] == s, blocks[k], taken)
        strips[s] = taken.reshape(size, c)


def routes(cols):
    count = lax.axis_size("tile")
    return list(zip(*[partners(p, count, cols) for p in range(count)]))


def swap_all(blocks, cols):
    return [
        lax.ppermute(block, "tile", list(enumerate(way)))
        for block, way in zip(blocks, routes(cols))
    ]


def fill_columns(shifted, pairs):
    count, size, lanes = pairs.shape
    c = lanes // 2
    at = lax.broadcasted_iota(jnp.int32, (size, c), 0)
    first, last = at == 0, at == size - 1
    shifted[0:size, 0 : 3 * c] = jnp.zeros((size, 3 * c), bf16)
    shifted[count * size :, 3 * c :] = jnp.zeros((size, 3 * c), bf16)
    for i in range(count):
        for parity, row, lane in ((1, (i + 1) * size, 0), (0, i * size, 3 * c)):
            value = pairs[i, :, parity * c : (parity + 1) * c].astype(f32)
            before = jnp.where(first, 0.0, pltpu.roll(value, 1, 0))
            after = jnp.where(last, 0.0, pltpu.roll(value, size - 1, 0))
            shifted[row : row + size, lane : lane + c] = before.astype(bf16)
            shifted[row : row + size, lane + c : lane + 2 * c] = value.astype(bf16)
            shifted[row : row + size, lane + 2 * c : lane + 3 * c] = after.astype(bf16)


def blocks_of_pairs(tap, lower, upper, c):
    for b in range(3):
        for half, parity, target, a in (
            (lower, 0, 0, 0),
            (lower, 0, 1, None),
            (lower, 1, 0, 1),
            (lower, 1, 1, 0),
            (upper, 0, 0, 2),
            (upper, 0, 1, 1),
            (upper, 1, 0, None),
            (upper, 1, 1, 2),
        ):
            yield half, (parity * 3 + b) * c, target * c, tap(a, b) if a is not None else None


def bulk_conv(shifted, weight, lower, upper, out, backward):
    c = weight.shape[-1]
    count, size, lanes = out.shape
    if backward:
        tap = lambda a, b: weight[(2 - a) * 3 + 2 - b]
    else:
        tap = lambda a, b: weight[a * 3 + b]
    for half, depth, target, block in blocks_of_pairs(tap, lower, upper, c):
        if block is None:
            block = jnp.zeros((c, c), bf16)
        if backward:
            half[target : target + c, depth : depth + c] = block
        else:
            half[depth : depth + c, target : target + c] = block
    rows = count * size
    dims = NT if backward else (((1,), (0,)), ((), ()))
    total = lax.dot_general(
        shifted[0:rows, :], lower[...], dims, preferred_element_type=f32
    ) + lax.dot_general(shifted[size : size + rows, :], upper[...], dims, preferred_element_type=f32)
    out[...] = total.reshape(count, size, lanes)


def bulk_weight_grad(shifted, delta, out):
    count, size, lanes = delta.shape
    c = lanes // 2
    rows = count * size
    flat = delta[...].reshape(rows, lanes)
    low = lax.dot_general(shifted[0:rows, :], flat, TN, preferred_element_type=f32)
    high = lax.dot_general(shifted[size : size + rows, :], flat, TN, preferred_element_type=f32)
    for b in range(3):
        here, there = b * c, (3 + b) * c
        out[b] = low[here : here + c, 0:c] + low[there : there + c, c:]
        out[3 + b] = low[there : there + c, 0:c] + high[here : here + c, c:]
        out[6 + b] = high[here : here + c, 0:c] + high[there : there + c, c:]


def load_edges(left, right, top, bottom):
    return left[...], right[...], top[0], bottom[0]


def to_pairs(strip, room):
    room[...] = strip
    half = strip.shape[0] // 2
    return jnp.concatenate(
        [room[pl.ds(0, half, stride=2), :], room[pl.ds(1, half, stride=2), :]], axis=1
    )


def add_strips(edges, strips, rooms):
    left, right, top, bottom = edges
    t, r, b, l = strips
    c = t.shape[1]
    half, depth, size = left.shape[0], left.shape[1], t.shape[0]
    at = lax.broadcasted_iota(jnp.int32, left.shape, 1)
    left_room, right_room, top_room, bottom_room, strip_a, strip_b = rooms
    left_room[...] = left + jnp.where(at == 0, to_pairs(l, strip_a)[:, None, :], 0.0)
    right_room[...] = right + jnp.where(at == depth - 1, to_pairs(r, strip_b)[:, None, :], 0.0)
    left_room[0, :, 0:c] += t[0:depth]
    left_room[half - 1, :, c:] += b[0:depth]
    right_room[0, :, 0:c] += t[size - depth :]
    right_room[half - 1, :, c:] += b[size - depth :]
    top_room[...] = top + t
    bottom_room[...] = bottom + b
    top_room[0:depth] = left_room[0, :, 0:c]
    top_room[size - depth :] = right_room[0, :, 0:c]
    bottom_room[0:depth] = left_room[half - 1, :, c:]
    bottom_room[size - depth :] = right_room[half - 1, :, c:]
    return left_room[...], right_room[...], top_room[...], bottom_room[...]


def edge_strips(edges, strips):
    left, right, top, bottom = edges
    c = top.shape[1]
    half = left.shape[0]
    strips[0] = top
    strips[2] = bottom
    for side, column in ((1, right[:, -1, :]), (3, left[:, 0, :])):
        strips[side, pl.ds(0, half, stride=2), :] = column[:, 0:c]
        strips[side, pl.ds(1, half, stride=2), :] = column[:, c:]


def lay_edges(pairs, left, right, top, bottom):
    depth = left.shape[1]
    size = pairs.shape[1]
    c = top.shape[-1]
    pairs[:, 0:depth, :] = left[...]
    pairs[:, size - depth :, :] = right[...]
    pairs[0, :, 0:c] = top[...]
    pairs[pairs.shape[0] - 1, :, c:] = bottom[...]


def halo_windows(strips, rooms):
    size = strips.shape[1]
    top, right, bottom, left = (strips[s] for s in range(4))
    zero = jnp.zeros_like(top[0:1])
    ends = [
        (0.5 * (top[0:1] + left[0:1]), 0.5 * (top[size - 1 :] + right[0:1])),
        (zero, zero),
        (0.5 * (left[size - 1 :] + bottom[0:1]), 0.5 * (bottom[size - 1 :] + right[size - 1 :])),
        (zero, zero),
    ]
    windows = []
    for s, (strip, (before, after)) in enumerate(zip((top, right, bottom, left), ends)):
        rooms[s, 7:8, :] = before
        rooms[s, 8 : 8 + size, :] = strip
        rooms[s, 8 + size : 9 + size, :] = after
        windows.append(
            jnp.concatenate([rooms[s, 7 + k : 7 + k + size, :] for k in range(3)], axis=1).astype(
                bf16
            )
        )
    return windows


side_taps = ((0, 1, 2), (2, 5, 8), (6, 7, 8), (0, 3, 6))


def halo_terms(windows, weight):
    return [
        jnp.dot(
            window,
            jnp.concatenate([weight[tap] for tap in taps], axis=0),
            preferred_element_type=f32,
        )
        for window, taps in zip(windows, side_taps)
    ]


def halo_weight_grad(windows, strips, out):
    c = out.shape[-1]
    for s, (window, taps) in enumerate(zip(windows, side_taps)):
        term = lax.dot_general(window, strips[s].astype(bf16), TN, preferred_element_type=f32)
        for k, tap in enumerate(taps):
            out[tap] += term[k * c : (k + 1) * c]


def halo_grads(strips, weight, rooms, grads):
    size, c = strips.shape[1:]
    long = size + 8
    for s, taps in enumerate(side_taps):
        rooms[s, 0:8, :] = jnp.zeros((8, c), f32)
        rooms[s, 8 : 8 + size, :] = strips[s]
        rooms[s, 8 + size :, :] = jnp.zeros((8, c), f32)
        copies = jnp.concatenate([rooms[s, 8 - k : 8 - k + long, :] for k in range(3)], axis=1)
        rims = jnp.concatenate([weight[tap] for tap in taps], axis=1)
        rim = lax.dot_general(copies.astype(bf16), rims, NT, preferred_element_type=f32)
        rooms[s, 0:long, :] = rim
        at = lax.broadcasted_iota(jnp.int32, (size, c), 0)
        corner = jnp.where(at == 0, rooms[s, 0:1, :], 0.0) + jnp.where(
            at == size - 1, rooms[s, size + 1 : size + 2, :], 0.0
        )
        grads[s] = rooms[s, 1 : 1 + size, :] + 0.5 * corner


def exact(values):
    return [value.astype(bf16).astype(f32) for value in values]


def first_strips(cols, table, block, weight, *refs):
    outs, found, held, held_weight = refs[:4], *refs[4:7]
    strips, columns, rows, near, arrived = refs[7:12]
    size = block.shape[0]
    pairs = [
        (table, near),
        (block.at[0], rows.at[0]),
        (block.at[size - 1], rows.at[1]),
        (block.at[:, pl.ds(0, 16), :], columns.at[0]),
        (block.at[:, pl.ds(size - 16, 16), :], columns.at[1]),
        (block, held),
        (weight, held_weight),
    ]
    copies = [
        pltpu.make_async_copy(source, target, arrived.at[k])
        for k, (source, target) in enumerate(pairs)
    ]
    for copy in copies:
        copy.start()
    for copy in copies[:5]:
        copy.wait()
    write_links(near, cols, found)
    strips[0] = rows[0].astype(f32)
    strips[2] = rows[1].astype(f32)
    strips[3] = columns[0].astype(f32)[:, 0, :]
    strips[1] = columns[1].astype(f32)[:, 15, :]
    send_strips(found, strips, outs)
    for copy in copies[5:]:
        copy.wait()


def first_bulk(block, weight, shifted, pre, hidden, slope, pairs, lower, upper):
    count, size, lanes = pre.shape
    c = lanes // 2
    for i in range(count):
        pairs[i, :, 0:c] = block[2 * i]
        pairs[i, :, c:] = block[2 * i + 1]
    fill_columns(shifted, pairs)
    bulk_conv(shifted, weight, lower, upper, pre, False)
    for i in range(count):
        value, rate = gelu_both(pre[i])
        hidden[i] = value.astype(bf16)
        slope[i] = rate.astype(bf16)


def first_edges(found, *refs):
    received, weight, blocks = refs[:4], refs[4], refs[5:9]
    outs, hidden, slope, halo = refs[9:13], refs[13:17], refs[17:21], refs[21]
    rooms, strips, long = refs[22:28], refs[28], refs[29]
    take_strips(found, received, halo)
    terms = halo_terms(halo_windows(halo, long), weight)
    edges = add_strips(load_edges(*blocks), terms, rooms)
    both = [gelu_both(edge) for edge in edges]
    values = exact([value for value, _ in both])
    for k in range(4):
        hidden[k][...] = values[k]
        slope[k][...] = both[k][1]
    edge_strips(values, strips)
    send_strips(found, strips, outs)


def second_bulk(hidden, left, right, top, bottom, weight, cotangent, *refs):
    shifted, pre, out_field, delta, pairs, lower, upper = refs
    count, size, lanes = pre.shape
    c = lanes // 2
    pairs[...] = hidden[...].astype(f32)
    lay_edges(pairs, left, right, top, bottom)
    fill_columns(shifted, pairs)
    bulk_conv(shifted, weight, lower, upper, pre, False)
    for i in range(count):
        for parity in range(2):
            part = slice(parity * c, (parity + 1) * c)
            value, rate = gelu_both(pre[i, :, part])
            out_field[i, :, part] = value.astype(bf16)
            delta[i, :, part] = (cotangent[2 * i + parity].astype(f32) * rate).astype(bf16)


def second_edges(found, *refs):
    received, weight, blocks, wanted = refs[:4], refs[4], refs[5:9], refs[9:13]
    outs, out_field, delta, halo = refs[13:17], refs[17:21], refs[21:25], refs[25]
    rooms, strips, long, grads = refs[26:32], refs[32], refs[33], refs[34]
    half, depth = blocks[0].shape[:2]
    take_strips(found, received, halo)
    terms = halo_terms(halo_windows(halo, long), weight)
    edges = add_strips(load_edges(*blocks), terms, rooms)
    cots = []
    for ref, at in ((wanted[0], 0), (wanted[1], 16 - depth)):
        block = ref[...].astype(f32)
        block = block.reshape((half, 2) + block.shape[1:])[:, :, at : at + depth, :]
        cots.append(jnp.concatenate([block[:, 0], block[:, 1]], axis=-1))
    cots += [wanted[2][0].astype(f32), wanted[3][0].astype(f32)]
    both = [gelu_both(edge) for edge in edges]
    deltas = exact([cot * rate for cot, (_, rate) in zip(cots, both)])
    for k in range(4):
        out_field[k][...] = both[k][0]
        delta[k][...] = deltas[k]
    edge_strips(deltas, strips)
    halo_grads(strips, weight, long, grads)
    send_strips(found, grads, outs)


def second_back(*refs):
    bulk_delta, delta_edges, halo = refs[0], refs[1:5], refs[5]
    shifted, weight, bulk_slope = refs[6:9]
    grad_weight, grad_hidden, delta_first = refs[9:12]
    pairs, delta, lower, upper, moved, strips, long = refs[12:19]
    count = pairs.shape[0]
    pairs[...] = bulk_delta[...].astype(f32)
    lay_edges(pairs, *delta_edges)
    delta[...] = pairs[...].astype(bf16)
    bulk_weight_grad(shifted, delta, grad_weight)
    edge_strips([ref[...] for ref in delta_edges], strips)
    halo_weight_grad(halo_windows(halo, long), strips, grad_weight)
    fill_columns(moved, pairs)
    bulk_conv(moved, weight, lower, upper, grad_hidden, True)
    for i in range(count):
        delta_first[i] = (grad_hidden[i] * bulk_slope[i].astype(f32)).astype(bf16)


def first_back(found, *refs):
    received, blocks, slope, bulk_delta = refs[:4], refs[4:8], refs[8:12], refs[12]
    halo, shifted, other_grad = refs[13:16]
    delta, edges_out, kept, given = refs[16], refs[17:21], refs[21], refs[22]
    rooms, strips, long, back, pairs, grad_weight = refs[23:29], *refs[29:34]
    take_strips(found, received, back)
    edges = add_strips(load_edges(*blocks), [back[s] for s in range(4)], rooms)
    deltas = exact([edge * rate[...] for edge, rate in zip(edges, slope)])
    for k in range(4):
        edges_out[k][...] = deltas[k]
    edge_strips(deltas, strips)
    pairs[...] = bulk_delta[...].astype(f32)
    lay_edges(pairs, *deltas)
    delta[...] = pairs[...].astype(bf16)
    bulk_weight_grad(shifted, delta, grad_weight)
    halo_weight_grad(halo_windows(halo, long), strips, grad_weight)
    core = lax.axis_index("tile") & 1
    for tap in range(grad_weight.shape[0]):
        one, two = grad_weight[tap], other_grad[tap]
        kept[tap] = jnp.where(core == 0, one, two)
        given[tap] = jnp.where(core == 0, two, one).astype(bf16)


def first_returns(found, *refs):
    edges, weight, outs = refs[:4], refs[4], refs[5:9]
    strips, long, grads = refs[9:12]
    edge_strips([edge[...] for edge in edges], strips)
    halo_grads(strips, weight, long, grads)
    send_strips(found, grads, outs)


def last_bulk(delta, weight, bulk_out, *refs):
    out_edges, interior, out_field, pairs, moved, lower, upper = refs[:4], *refs[4:10]
    count, size, lanes = pairs.shape
    c = lanes // 2
    pairs[...] = bulk_out[...].astype(f32)
    lay_edges(pairs, *out_edges)
    for i in range(count):
        out_field[2 * i] = pairs[i, :, 0:c].astype(bf16)
        out_field[2 * i + 1] = pairs[i, :, c:].astype(bf16)
    pairs[...] = delta[...].astype(f32)
    fill_columns(moved, pairs)
    bulk_conv(moved, weight, lower, upper, interior, True)


def last_edges(found, *refs):
    received, interior, grad = refs[:4], refs[4], refs[5]
    rooms, back, pairs = refs[6:12], refs[12], refs[13]
    count, size, lanes = interior.shape
    c = lanes // 2
    take_strips(found, received, back)
    edges = (
        interior[:, 0:8, :],
        interior[:, size - 8 :, :],
        interior[0, :, 0:c],
        interior[count - 1, :, c:],
    )
    edges = add_strips(edges, [back[s] for s in range(4)], rooms)
    pairs[...] = interior[...]
    lay_edges(pairs, *edges)
    for i in range(count):
        grad[2 * i] = pairs[i, :, 0:c].astype(bf16)
        grad[2 * i + 1] = pairs[i, :, c:].astype(bf16)


def flip_swap(block, mask_ens, mask_tile):
    ens, tile = lax.axis_size("ens"), lax.axis_size("tile")
    route = [
        (e * tile + t, (e ^ mask_ens) * tile + (t ^ mask_tile))
        for e in range(ens)
        for t in range(tile)
    ]
    return lax.ppermute(block, ("ens", "tile"), route)


def pick(parts, index):
    return lax.dynamic_index_in_dim(parts, index, 0, keepdims=False)


def summed_part(kept, given, riders, ways, beside):
    tile = lax.axis_index("tile")
    rows, lanes = kept.shape
    carried = [None] * len(riders)

    def swap(block, mask):
        way = tuple(t ^ mask for t in range(lax.axis_size("tile")))
        if way not in ways or carried[ways.index(way)] is not None:
            return flip_swap(block, 0, mask)
        k = ways.index(way)
        both = flip_swap(jnp.concatenate([block, riders[k]]), 0, mask)
        carried[k] = both[block.shape[0] :]
        return both[: block.shape[0]]

    given, riders = lax.optimization_barrier((flip_swap(given, 0, 1), riders))
    part = kept + given.astype(f32)
    seat = lax.axis_index("ens") * 2 + (tile >> 1 & 1)
    quarters = part.reshape(4, rows // 4, lanes)
    sent = quarters.astype(bf16)
    part = pick(quarters, seat)
    for k in (1, 2, 3):
        part = part + flip_swap(pick(sent, seat ^ k), k >> 1, (k & 1) << 1).astype(f32)
    part, beside = lax.optimization_barrier((part, beside))
    bit = 4
    while bit < lax.axis_size("tile"):
        own = part.astype(bf16)
        part = lax.reduce_precision(part, 8, 7)
        if bit * 2 < lax.axis_size("tile"):
            one, two, three = (swap(own, bit * k).astype(f32) for k in (1, 2, 3))
            part = (part + one) + (two + three)
            bit *= 4
        else:
            part = part + swap(own, bit).astype(f32)
            bit *= 2
    for k, way in enumerate(ways):
        if carried[k] is None:
            carried[k] = lax.ppermute(riders[k], "tile", list(enumerate(way)))
    return part.astype(bf16), carried, beside


def gather_quarters(part):
    seat = lax.axis_index("ens") * 2 + (lax.axis_index("tile") >> 1 & 1)
    whole = jnp.zeros((4,) + part.shape, part.dtype)
    whole = lax.dynamic_update_index_in_dim(whole, part, seat, 0)
    for k in (1, 2, 3):
        got = flip_swap(part, k >> 1, (k & 1) << 1)
        whole = lax.dynamic_update_index_in_dim(whole, got, seat ^ k, 0)
    return whole.reshape(-1, part.shape[-1])


def both_grads(half, other, first, second):
    core = lax.axis_index("tile") & 1
    one, two = half[...].astype(f32), other[...].astype(f32)
    first[...] = jnp.where(core == 0, one, two)
    second[...] = jnp.where(core == 0, two, one)


def call(kernel, name, ins, outs, scratch, cost=0, room=16 << 20):
    whole = pl.BlockSpec(memory_space=pltpu.VMEM)
    return pl.pallas_call(
        kernel,
        name=name,
        grid=(1,),
        in_specs=[spec or whole for _, spec in ins],
        out_specs=[whole] * len(outs),
        out_shape=outs,
        scratch_shapes=scratch,
        compiler_params=pltpu.CompilerParams(vmem_limit_bytes=room),
        cost_estimate=pl.CostEstimate(flops=cost, bytes_accessed=2 << 20, transcendentals=0),
    )(*[array for array, _ in ins])


def local(fields, weight_first, weight_second, neighbours, cotangent):
    block, wanted = fields[0, 0], cotangent[0, 0]
    size, c = block.shape[0], block.shape[-1]
    half = size // 2
    count = lax.axis_size("tile")
    cols = max(4, count // 8)
    shape = weight_first.shape
    one, two = weight_first.reshape(9, c, c), weight_second.reshape(9, c, c)
    flops = 2 * size * size * 9 * c * c

    S = jax.ShapeDtypeStruct
    sent = [S((size, c), bf16)] * 4
    halo = S((4, size, c), f32)
    edge = [S((half, 8, 2 * c), f32)] * 2 + [S((size, c), f32)] * 2
    pairs = lambda kind: S((half, size, 2 * c), kind)
    shifted = S(((half + 1) * size, 6 * c), bf16)
    V = lambda leaf: pltpu.VMEM(leaf.shape, leaf.dtype)
    ahead = [pltpu.VMEM((6 * c, 2 * c), bf16)] * 2
    back = [pltpu.VMEM((2 * c, 6 * c), bf16)] * 2
    rooms = [V(leaf) for leaf in edge] + [pltpu.VMEM((size, c), f32)] * 2
    long = pltpu.VMEM((4, size + 16, c), f32)
    whole = lambda arrays: [(array, None) for array in arrays]

    def edge_blocks(array):
        last = size // 8 - 1
        return [
            (array, pl.BlockSpec((half, 8, 2 * c), lambda step: (0, 0, 0))),
            (array, pl.BlockSpec((half, 8, 2 * c), lambda step: (0, last, 0))),
            (array, pl.BlockSpec((1, size, c), lambda step: (0, 0, 0))),
            (array, pl.BlockSpec((1, size, c), lambda step: (half - 1, 0, 1))),
        ]

    def image_edges(array):
        last = size // 16 - 1
        return [
            (array, pl.BlockSpec((size, 16, c), lambda step: (0, 0, 0))),
            (array, pl.BlockSpec((size, 16, c), lambda step: (0, last, 0))),
            (array, pl.BlockSpec((1, size, c), lambda step: (0, 0, 0))),
            (array, pl.BlockSpec((1, size, c), lambda step: (size - 1, 0, 0))),
        ]

    far = pl.BlockSpec(memory_space=pl.ANY)
    stay = lambda array: (pltpu.with_memory_space_constraint(array, pltpu.HBM), far)
    *strips, found, block, one = call(
        functools.partial(first_strips, cols),
        "first_strips",
        [stay(neighbours.T), stay(block), stay(one)],
        sent + [S((8, 8, 128), jnp.int32), S(block.shape, bf16), S(one.shape, bf16)],
        [V(halo), pltpu.VMEM((2, size, 16, c), bf16), pltpu.VMEM((2, size, c), bf16)]
        + [pltpu.SMEM(neighbours.shape[::-1], jnp.int32), pltpu.SemaphoreType.DMA((7,))],
    )
    links = (found, None)
    strips = swap_all(strips, cols)
    shifted_one, pre_one, hidden, slope = call(
        first_bulk,
        "first_bulk",
        whole([block, one]),
        [shifted, pairs(f32), pairs(bf16), pairs(bf16)],
        [V(pairs(bf16))] + ahead,
        flops,
    )
    found = call(
        first_edges,
        "first_edges",
        [links] + whole(strips) + [(one, None)] + edge_blocks(pre_one),
        sent + edge + edge + [halo],
        rooms + [V(halo), long],
    )
    strips, hidden_edges, slope_edges, halo_one = found[:4], found[4:8], found[8:12], found[12]
    strips = swap_all(strips, cols)
    shifted_two, pre_two, out_bulk, delta_bulk = call(
        second_bulk,
        "second_bulk",
        whole([hidden, *hidden_edges, two, wanted]),
        [shifted, pairs(f32), pairs(bf16), pairs(bf16)],
        [V(pairs(f32))] + ahead,
        flops,
    )
    found = call(
        second_edges,
        "second_edges",
        [links] + whole(strips) + [(two, None)] + edge_blocks(pre_two) + image_edges(wanted),
        sent + edge + edge + [halo],
        rooms + [V(halo), long, V(halo)],
    )
    strips, out_edges, delta_edges, halo_two = found[:4], found[4:8], found[8:12], found[12]
    strips = swap_all(strips, cols)
    grad_two, grad_hidden, delta_one = call(
        second_back,
        "second_back",
        whole(
            [delta_bulk, *delta_edges, halo_two, shifted_two, two, slope]
        ),
        [S((9, c, c), f32), pairs(f32), pairs(bf16)],
        [V(pairs(f32)), V(pairs(bf16))] + back + [V(shifted), V(halo), long],
        2 * flops,
    )
    found = call(
        first_back,
        "first_back",
        [links]
        + whole(strips)
        + edge_blocks(grad_hidden)
        + whole([*slope_edges, delta_one, halo_one, shifted_one, grad_two]),
        [pairs(bf16)] + edge + [S((9, c, c), f32), S((9, c, c), bf16)],
        rooms + [V(halo), long, V(halo), V(pairs(f32)), pltpu.VMEM((9, c, c), f32)],
        flops,
    )
    delta_one, delta_edges, kept, given = found[0], found[1:5], *found[5:]
    strips = call(
        first_returns,
        "first_returns",
        [links] + whole([*delta_edges, one]),
        sent,
        [V(halo), long, V(halo)],
    )
    interior, out_field = call(
        last_bulk,
        "last_bulk",
        whole([delta_one, one, out_bulk, *out_edges]),
        [pairs(f32), S(block.shape, bf16)],
        [V(pairs(f32)), V(shifted)] + back,
        flops,
    )
    part, strips, interior = summed_part(
        kept.reshape(9 * c, c), given.reshape(9 * c, c), strips, routes(cols), interior
    )
    part, strips = lax.optimization_barrier((part, strips))
    (grad_block,) = call(
        last_edges,
        "last_edges",
        [links] + whole([*strips, interior]),
        [S(block.shape, bf16)],
        rooms + [V(halo), V(pairs(f32))],
    )
    half_grads = gather_quarters(part)
    half_grads, grad_block = lax.optimization_barrier((half_grads, grad_block))
    grads = call(
        both_grads,
        "both_grads",
        whole([half_grads, flip_swap(half_grads, 0, 1)]),
        [S((9 * c, c), f32)] * 2,
        [],
    )
    grad_first, grad_second = (grad.reshape(shape) for grad in grads)
    return (out_field[None, None], grad_block[None, None], grad_first, grad_second)


def solution(mesh):
    placed = (P("ens", "tile", None, None, None), P(), P(), P(), P("ens", "tile", None, None, None))
    return jax.shard_map(
        local,
        mesh=mesh,
        in_specs=placed,
        out_specs=(
            P("ens", "tile", None, None, None),
            P("ens", "tile", None, None, None),
            P(),
            P(),
        ),
        check_vma=False,
    )
```

```python
import functools

import jax
import jax.numpy as jnp
from jax import lax
from jax.experimental import pallas as pl
from jax.experimental.pallas import tpu as pltpu
from jax.sharding import PartitionSpec as P

root_half = 0.7071067811865476
inv_root_tau = 0.3989422804014327
bf16, f32 = jnp.bfloat16, jnp.float32
NT = (((1,), (1,)), ((), ()))
TN = (((0,), (0,)), ((), ()))


def gelu_both(pre):
    bell = 0.5 * (1.0 + lax.erf(pre * root_half))
    return pre * bell, bell + pre * jnp.exp(-0.5 * pre * pre) * inv_root_tau


def partners(index, count, cols):
    odd, row_odd = index & 1, (index // cols) & 1
    return [
        (index + cols * (2 * row_odd - 1) + count) % count,
        (index + cols * (1 - 2 * row_odd) + count) % count,
        (index - 1 + 2 * odd + count) % count,
        (index + 1 - 2 * odd + count) % count,
    ]


def write_links(table, cols, found):
    count = lax.axis_size("tile")
    me = lax.axis_index("tile")
    for k, other in enumerate(partners(me, count, cols)):
        side, back = jnp.int32(0), jnp.int32(0)
        for s in range(1, 4):
            side = jnp.where(table[s, me] == other, s, side)
            back = jnp.where(table[s, other] == me, s, back)
        turn = jnp.where((side >= 2) == (back >= 2), 1, 0)
        found[k] = jnp.full(found.shape[1:], side, jnp.int32)
        found[4 + k] = jnp.full(found.shape[1:], turn, jnp.int32)


def send_strips(found, strips, outs):
    _, size, c = strips.shape
    at_row = lax.broadcasted_iota(jnp.int32, (size, size), 0)
    at_col = lax.broadcasted_iota(jnp.int32, (size, size), 1)
    for k, out in enumerate(outs):
        turn = found[4 + k][0:1, 0:size] == 1
        order = (at_col == jnp.where(turn, size - 1 - at_row, at_row)).astype(f32).astype(bf16)
        side = found[k][None]
        chosen = jnp.zeros((size // 8, 8, c), f32)
        for s in range(4):
            chosen = jnp.where(side == s, strips[s].reshape(chosen.shape), chosen)
        chosen = chosen.reshape(size, c).astype(bf16)
        out[...] = jnp.dot(order, chosen, preferred_element_type=f32).astype(bf16)


def take_strips(found, received, strips):
    _, size, c = strips.shape
    blocks = [block[...].astype(f32).reshape(size // 8, 8, c) for block in received]
    for s in range(4):
        taken = blocks[0]
        for k in range(1, 4):
            taken = jnp.where(found[k][None] == s, blocks[k], taken)
        strips[s] = taken.reshape(size, c)


def routes(cols):
    count = lax.axis_size("tile")
    return list(zip(*[partners(p, count, cols) for p in range(count)]))


def swap_all(blocks, cols):
    return [
        lax.ppermute(block, "tile", list(enumerate(way)))
        for block, way in zip(blocks, routes(cols))
    ]


def fill_columns(shifted, pairs):
    count, size, lanes = pairs.shape
    c = lanes // 2
    at = lax.broadcasted_iota(jnp.int32, (size, c), 0)
    first, last = at == 0, at == size - 1
    shifted[0:size, 0 : 3 * c] = jnp.zeros((size, 3 * c), bf16)
    shifted[count * size :, 3 * c :] = jnp.zeros((size, 3 * c), bf16)
    for i in range(count):
        for parity, row, lane in ((1, (i + 1) * size, 0), (0, i * size, 3 * c)):
            value = pairs[i, :, parity * c : (parity + 1) * c].astype(f32)
            before = jnp.where(first, 0.0, pltpu.roll(value, 1, 0))
            after = jnp.where(last, 0.0, pltpu.roll(value, size - 1, 0))
            shifted[row : row + size, lane : lane + c] = before.astype(bf16)
            shifted[row : row + size, lane + c : lane + 2 * c] = value.astype(bf16)
            shifted[row : row + size, lane + 2 * c : lane + 3 * c] = after.astype(bf16)


def blocks_of_pairs(tap, lower, upper, c):
    for b in range(3):
        for half, parity, target, a in (
            (lower, 0, 0, 0),
            (lower, 0, 1, None),
            (lower, 1, 0, 1),
            (lower, 1, 1, 0),
            (upper, 0, 0, 2),
            (upper, 0, 1, 1),
            (upper, 1, 0, None),
            (upper, 1, 1, 2),
        ):
            yield half, (parity * 3 + b) * c, target * c, tap(a, b) if a is not None else None


def bulk_conv(shifted, weight, lower, upper, out, backward):
    c = weight.shape[-1]
    count, size, lanes = out.shape
    if backward:
        tap = lambda a, b: weight[(2 - a) * 3 + 2 - b]
    else:
        tap = lambda a, b: weight[a * 3 + b]
    for half, depth, target, block in blocks_of_pairs(tap, lower, upper, c):
        if block is None:
            block = jnp.zeros((c, c), bf16)
        if backward:
            half[target : target + c, depth : depth + c] = block
        else:
            half[depth : depth + c, target : target + c] = block
    rows = count * size
    dims = NT if backward else (((1,), (0,)), ((), ()))
    total = lax.dot_general(
        shifted[0:rows, :], lower[...], dims, preferred_element_type=f32
    ) + lax.dot_general(shifted[size : size + rows, :], upper[...], dims, preferred_element_type=f32)
    out[...] = total.reshape(count, size, lanes)


def bulk_weight_grad(shifted, delta, out):
    count, size, lanes = delta.shape
    c = lanes // 2
    rows = count * size
    flat = delta[...].reshape(rows, lanes)
    low = lax.dot_general(shifted[0:rows, :], flat, TN, preferred_element_type=f32)
    high = lax.dot_general(shifted[size : size + rows, :], flat, TN, preferred_element_type=f32)
    for b in range(3):
        here, there = b * c, (3 + b) * c
        out[b] = low[here : here + c, 0:c] + low[there : there + c, c:]
        out[3 + b] = low[there : there + c, 0:c] + high[here : here + c, c:]
        out[6 + b] = high[here : here + c, 0:c] + high[there : there + c, c:]


def load_edges(left, right, top, bottom):
    return left[...], right[...], top[0], bottom[0]


def to_pairs(strip, room):
    room[...] = strip
    half = strip.shape[0] // 2
    return jnp.concatenate(
        [room[pl.ds(0, half, stride=2), :], room[pl.ds(1, half, stride=2), :]], axis=1
    )


def add_strips(edges, strips, rooms):
    left, right, top, bottom = edges
    t, r, b, l = strips
    c = t.shape[1]
    half, depth, size = left.shape[0], left.shape[1], t.shape[0]
    at = lax.broadcasted_iota(jnp.int32, left.shape, 1)
    left_room, right_room, top_room, bottom_room, strip_a, strip_b = rooms
    left_room[...] = left + jnp.where(at == 0, to_pairs(l, strip_a)[:, None, :], 0.0)
    right_room[...] = right + jnp.where(at == depth - 1, to_pairs(r, strip_b)[:, None, :], 0.0)
    left_room[0, :, 0:c] += t[0:depth]
    left_room[half - 1, :, c:] += b[0:depth]
    right_room[0, :, 0:c] += t[size - depth :]
    right_room[half - 1, :, c:] += b[size - depth :]
    top_room[...] = top + t
    bottom_room[...] = bottom + b
    top_room[0:depth] = left_room[0, :, 0:c]
    top_room[size - depth :] = right_room[0, :, 0:c]
    bottom_room[0:depth] = left_room[half - 1, :, c:]
    bottom_room[size - depth :] = right_room[half - 1, :, c:]
    return left_room[...], right_room[...], top_room[...], bottom_room[...]


def edge_strips(edges, strips):
    left, right, top, bottom = edges
    c = top.shape[1]
    half = left.shape[0]
    strips[0] = top
    strips[2] = bottom
    for side, column in ((1, right[:, -1, :]), (3, left[:, 0, :])):
        strips[side, pl.ds(0, half, stride=2), :] = column[:, 0:c]
        strips[side, pl.ds(1, half, stride=2), :] = column[:, c:]


def lay_edges(pairs, left, right, top, bottom):
    depth = left.shape[1]
    size = pairs.shape[1]
    c = top.shape[-1]
    pairs[:, 0:depth, :] = left[...]
    pairs[:, size - depth :, :] = right[...]
    pairs[0, :, 0:c] = top[...]
    pairs[pairs.shape[0] - 1, :, c:] = bottom[...]


def halo_windows(strips, rooms):
    size = strips.shape[1]
    top, right, bottom, left = (strips[s] for s in range(4))
    zero = jnp.zeros_like(top[0:1])
    ends = [
        (0.5 * (top[0:1] + left[0:1]), 0.5 * (top[size - 1 :] + right[0:1])),
        (zero, zero),
        (0.5 * (left[size - 1 :] + bottom[0:1]), 0.5 * (bottom[size - 1 :] + right[size - 1 :])),
        (zero, zero),
    ]
    windows = []
    for s, (strip, (before, after)) in enumerate(zip((top, right, bottom, left), ends)):
        rooms[s, 7:8, :] = before
        rooms[s, 8 : 8 + size, :] = strip
        rooms[s, 8 + size : 9 + size, :] = after
        windows.append(
            jnp.concatenate([rooms[s, 7 + k : 7 + k + size, :] for k in range(3)], axis=1).astype(
                bf16
            )
        )
    return windows


side_taps = ((0, 1, 2), (2, 5, 8), (6, 7, 8), (0, 3, 6))


def halo_terms(windows, weight):
    return [
        jnp.dot(
            window,
            jnp.concatenate([weight[tap] for tap in taps], axis=0),
            preferred_element_type=f32,
        )
        for window, taps in zip(windows, side_taps)
    ]


def halo_weight_grad(windows, strips, out):
    c = out.shape[-1]
    for s, (window, taps) in enumerate(zip(windows, side_taps)):
        term = lax.dot_general(window, strips[s].astype(bf16), TN, preferred_element_type=f32)
        for k, tap in enumerate(taps):
            out[tap] += term[k * c : (k + 1) * c]


def halo_grads(strips, weight, rooms, grads):
    size, c = strips.shape[1:]
    long = size + 8
    for s, taps in enumerate(side_taps):
        rooms[s, 0:8, :] = jnp.zeros((8, c), f32)
        rooms[s, 8 : 8 + size, :] = strips[s]
        rooms[s, 8 + size :, :] = jnp.zeros((8, c), f32)
        copies = jnp.concatenate([rooms[s, 8 - k : 8 - k + long, :] for k in range(3)], axis=1)
        rims = jnp.concatenate([weight[tap] for tap in taps], axis=1)
        rim = lax.dot_general(copies.astype(bf16), rims, NT, preferred_element_type=f32)
        rooms[s, 0:long, :] = rim
        at = lax.broadcasted_iota(jnp.int32, (size, c), 0)
        corner = jnp.where(at == 0, rooms[s, 0:1, :], 0.0) + jnp.where(
            at == size - 1, rooms[s, size + 1 : size + 2, :], 0.0
        )
        grads[s] = rooms[s, 1 : 1 + size, :] + 0.5 * corner


def exact(values):
    return [value.astype(bf16).astype(f32) for value in values]


def first_strips(cols, table, block, weight, *refs):
    outs, found, held, held_weight = refs[:4], *refs[4:7]
    strips, columns, rows, near, arrived = refs[7:12]
    size = block.shape[0]
    pairs = [
        (table, near),
        (block.at[0], rows.at[0]),
        (block.at[size - 1], rows.at[1]),
        (block.at[:, pl.ds(0, 16), :], columns.at[0]),
        (block.at[:, pl.ds(size - 16, 16), :], columns.at[1]),
        (block, held),
        (weight, held_weight),
    ]
    copies = [
        pltpu.make_async_copy(source, target, arrived.at[k])
        for k, (source, target) in enumerate(pairs)
    ]
    for copy in copies:
        copy.start()
    for copy in copies[:5]:
        copy.wait()
    write_links(near, cols, found)
    strips[0] = rows[0].astype(f32)
    strips[2] = rows[1].astype(f32)
    strips[3] = columns[0].astype(f32)[:, 0, :]
    strips[1] = columns[1].astype(f32)[:, 15, :]
    send_strips(found, strips, outs)
    for copy in copies[5:]:
        copy.wait()


def first_bulk(block, weight, shifted, pre, hidden, slope, pairs, lower, upper):
    count, size, lanes = pre.shape
    c = lanes // 2
    for i in range(count):
        pairs[i, :, 0:c] = block[2 * i]
        pairs[i, :, c:] = block[2 * i + 1]
    fill_columns(shifted, pairs)
    bulk_conv(shifted, weight, lower, upper, pre, False)
    for i in range(count):
        value, rate = gelu_both(pre[i])
        hidden[i] = value.astype(bf16)
        slope[i] = rate.astype(bf16)


def first_edges(found, *refs):
    received, weight, blocks = refs[:4], refs[4], refs[5:9]
    outs, hidden, slope, halo = refs[9:13], refs[13:17], refs[17:21], refs[21]
    rooms, strips, long = refs[22:28], refs[28], refs[29]
    take_strips(found, received, halo)
    terms = halo_terms(halo_windows(halo, long), weight)
    edges = add_strips(load_edges(*blocks), terms, rooms)
    both = [gelu_both(edge) for edge in edges]
    values = exact([value for value, _ in both])
    for k in range(4):
        hidden[k][...] = values[k]
        slope[k][...] = both[k][1]
    edge_strips(values, strips)
    send_strips(found, strips, outs)


def second_bulk(hidden, left, right, top, bottom, weight, cotangent, *refs):
    shifted, pre, out_field, delta, pairs, lower, upper = refs
    count, size, lanes = pre.shape
    c = lanes // 2
    pairs[...] = hidden[...].astype(f32)
    lay_edges(pairs, left, right, top, bottom)
    fill_columns(shifted, pairs)
    bulk_conv(shifted, weight, lower, upper, pre, False)
    for i in range(count):
        for parity in range(2):
            part = slice(parity * c, (parity + 1) * c)
            value, rate = gelu_both(pre[i, :, part])
            out_field[i, :, part] = value.astype(bf16)
            delta[i, :, part] = (cotangent[2 * i + parity].astype(f32) * rate).astype(bf16)


def second_edges(found, *refs):
    received, weight, blocks, wanted = refs[:4], refs[4], refs[5:9], refs[9:13]
    outs, out_field, delta, halo = refs[13:17], refs[17:21], refs[21:25], refs[25]
    rooms, strips, long, grads = refs[26:32], refs[32], refs[33], refs[34]
    half, depth = blocks[0].shape[:2]
    take_strips(found, received, halo)
    terms = halo_terms(halo_windows(halo, long), weight)
    edges = add_strips(load_edges(*blocks), terms, rooms)
    cots = []
    for ref, at in ((wanted[0], 0), (wanted[1], 16 - depth)):
        block = ref[...].astype(f32)
        block = block.reshape((half, 2) + block.shape[1:])[:, :, at : at + depth, :]
        cots.append(jnp.concatenate([block[:, 0], block[:, 1]], axis=-1))
    cots += [wanted[2][0].astype(f32), wanted[3][0].astype(f32)]
    both = [gelu_both(edge) for edge in edges]
    deltas = exact([cot * rate for cot, (_, rate) in zip(cots, both)])
    for k in range(4):
        out_field[k][...] = both[k][0]
        delta[k][...] = deltas[k]
    edge_strips(deltas, strips)
    halo_grads(strips, weight, long, grads)
    send_strips(found, grads, outs)


def second_back(*refs):
    bulk_delta, delta_edges, halo = refs[0], refs[1:5], refs[5]
    shifted, weight, bulk_slope = refs[6:9]
    grad_weight, grad_hidden, delta_first = refs[9:12]
    pairs, delta, lower, upper, moved, strips, long = refs[12:19]
    count = pairs.shape[0]
    pairs[...] = bulk_delta[...].astype(f32)
    lay_edges(pairs, *delta_edges)
    delta[...] = pairs[...].astype(bf16)
    bulk_weight_grad(shifted, delta, grad_weight)
    edge_strips([ref[...] for ref in delta_edges], strips)
    halo_weight_grad(halo_windows(halo, long), strips, grad_weight)
    fill_columns(moved, pairs)
    bulk_conv(moved, weight, lower, upper, grad_hidden, True)
    for i in range(count):
        delta_first[i] = (grad_hidden[i] * bulk_slope[i].astype(f32)).astype(bf16)


def first_back(found, *refs):
    received, blocks, slope, bulk_delta = refs[:4], refs[4:8], refs[8:12], refs[12]
    halo, shifted, other_grad = refs[13:16]
    delta, edges_out, kept, given = refs[16], refs[17:21], refs[21], refs[22]
    rooms, strips, long, back, pairs, grad_weight = refs[23:29], *refs[29:34]
    take_strips(found, received, back)
    edges = add_strips(load_edges(*blocks), [back[s] for s in range(4)], rooms)
    deltas = exact([edge * rate[...] for edge, rate in zip(edges, slope)])
    for k in range(4):
        edges_out[k][...] = deltas[k]
    edge_strips(deltas, strips)
    pairs[...] = bulk_delta[...].astype(f32)
    lay_edges(pairs, *deltas)
    delta[...] = pairs[...].astype(bf16)
    bulk_weight_grad(shifted, delta, grad_weight)
    halo_weight_grad(halo_windows(halo, long), strips, grad_weight)
    core = lax.axis_index("tile") & 1
    for tap in range(grad_weight.shape[0]):
        one, two = grad_weight[tap], other_grad[tap]
        kept[tap] = jnp.where(core == 0, one, two)
        given[tap] = jnp.where(core == 0, two, one).astype(bf16)


def first_returns(found, *refs):
    edges, weight, outs = refs[:4], refs[4], refs[5:9]
    strips, long, grads = refs[9:12]
    edge_strips([edge[...] for edge in edges], strips)
    halo_grads(strips, weight, long, grads)
    send_strips(found, grads, outs)


def last_bulk(delta, weight, bulk_out, *refs):
    out_edges, interior, out_field, pairs, moved, lower, upper = refs[:4], *refs[4:10]
    count, size, lanes = pairs.shape
    c = lanes // 2
    pairs[...] = bulk_out[...].astype(f32)
    lay_edges(pairs, *out_edges)
    for i in range(count):
        out_field[2 * i] = pairs[i, :, 0:c].astype(bf16)
        out_field[2 * i + 1] = pairs[i, :, c:].astype(bf16)
    pairs[...] = delta[...].astype(f32)
    fill_columns(moved, pairs)
    bulk_conv(moved, weight, lower, upper, interior, True)


def last_edges(found, *refs):
    received, interior, grad = refs[:4], refs[4], refs[5]
    rooms, back, pairs = refs[6:12], refs[12], refs[13]
    count, size, lanes = interior.shape
    c = lanes // 2
    take_strips(found, received, back)
    edges = (
        interior[:, 0:8, :],
        interior[:, size - 8 :, :],
        interior[0, :, 0:c],
        interior[count - 1, :, c:],
    )
    edges = add_strips(edges, [back[s] for s in range(4)], rooms)
    pairs[...] = interior[...]
    lay_edges(pairs, *edges)
    for i in range(count):
        grad[2 * i] = pairs[i, :, 0:c].astype(bf16)
        grad[2 * i + 1] = pairs[i, :, c:].astype(bf16)


def call(kernel, name, ins, outs, scratch, cost=0, room=16 << 20):
    whole = pl.BlockSpec(memory_space=pltpu.VMEM)
    return pl.pallas_call(
        kernel,
        name=name,
        grid=(1,),
        in_specs=[spec or whole for _, spec in ins],
        out_specs=[whole] * len(outs),
        out_shape=outs,
        scratch_shapes=scratch,
        compiler_params=pltpu.CompilerParams(vmem_limit_bytes=room),
        cost_estimate=pl.CostEstimate(flops=cost, bytes_accessed=2 << 20, transcendentals=0),
    )(*[array for array, _ in ins])


def flip_swap(block, mask_ens, mask_tile):
    ens, tile = lax.axis_size("ens"), lax.axis_size("tile")
    route = [
        (e * tile + t, (e ^ mask_ens) * tile + (t ^ mask_tile))
        for e in range(ens)
        for t in range(tile)
    ]
    return lax.ppermute(block, ("ens", "tile"), route)


def seat_of():
    return lax.axis_index("ens") * 2 + (lax.axis_index("tile") >> 1 & 1)


def share_out(kept, given, own, *sent):
    rows = own.shape[0]
    seat = seat_of()
    quarter = lambda at: pl.ds(pl.multiple_of(at * rows, rows), rows)
    add = lambda at: kept[quarter(at), :] + given[quarter(at), :].astype(f32)
    own[...] = add(seat)
    for k, block in enumerate(sent):
        block[...] = add(seat ^ (k + 1)).astype(bf16)


def add_up(count, loads, base, *refs):
    got, riders = refs[:count], refs[count : count + loads]
    total, loaded, came = refs[count + loads], refs[count + loads + 1 :][:loads], refs[count + 2 * loads + 1 :]
    rows = base.shape[0]
    terms = [base[...].astype(f32)] + [block[0:rows].astype(f32) for block in got]
    while len(terms) > 1:
        terms = [terms[i] + terms[i + 1] for i in range(0, len(terms), 2)]
    total[...] = terms[0].astype(bf16)
    for block, rider in zip(loaded, riders):
        block[0:rows] = terms[0].astype(bf16)
        block[rows:] = rider[...]
    for block, place in zip([block for block in got if block.shape[0] > rows], came):
        place[...] = block[rows:]


def summed_part(kept, given, riders, ways, beside):
    tiles = lax.axis_size("tile")
    rows, lanes = kept.shape[0] // 4, kept.shape[1]
    groups, bit = [], 4
    while bit < tiles:
        groups.append([bit, 2 * bit, 3 * bit] if 2 * bit < tiles else [bit])
        bit *= 4
    S = jax.ShapeDtypeStruct
    given, riders = lax.optimization_barrier((flip_swap(given, 0, 1), riders))
    base, *sent = call(
        share_out,
        "share_out",
        [(kept, None), (given, None)],
        [S((rows, lanes), f32)] + [S((rows, lanes), bf16)] * 3,
        [],
    )
    got = [flip_swap(block, k >> 1, (k & 1) << 1) for k, block in zip((1, 2, 3), sent)]
    carried, coming = {}, []
    for n, masks in enumerate(groups + [[]]):
        aboard = {}
        for mask in masks:
            way = tuple(t ^ mask for t in range(tiles))
            if way in ways:
                aboard[mask] = ways.index(way)
        loads = [riders[k] for k in aboard.values()]
        found = call(
            functools.partial(add_up, len(got), len(loads)),
            "add_up",
            [(block, None) for block in (base, *got, *loads)],
            [S((rows, lanes), bf16)]
            + [S((rows + load.shape[0], lanes), bf16) for load in loads]
            + [S(riders[k].shape, bf16) for k in coming],
            [],
        )
        if n == 0:
            found, beside = lax.optimization_barrier((found, beside))
        base, loaded = found[0], dict(zip(aboard, found[1 : 1 + len(loads)]))
        carried.update(zip(coming, found[1 + len(loads) :]))
        got = [flip_swap(loaded.get(mask, base), 0, mask) for mask in masks]
        coming = list(aboard.values())
    for k, way in enumerate(ways):
        if k not in carried:
            carried[k] = lax.ppermute(riders[k], "tile", list(enumerate(way)))
    return base, [carried[k] for k in range(len(ways))], beside


def gather_quarters(part):
    seat = seat_of()
    whole = jnp.zeros((4,) + part.shape, part.dtype)
    whole = lax.dynamic_update_index_in_dim(whole, part, seat, 0)
    for k in (1, 2, 3):
        got = flip_swap(part, k >> 1, (k & 1) << 1)
        whole = lax.dynamic_update_index_in_dim(whole, got, seat ^ k, 0)
    return whole.reshape(-1, part.shape[-1])


def both_grads(half, other, first, second):
    core = lax.axis_index("tile") & 1
    one, two = half[...].astype(f32), other[...].astype(f32)
    first[...] = jnp.where(core == 0, one, two)
    second[...] = jnp.where(core == 0, two, one)


def local(fields, weight_first, weight_second, neighbours, cotangent):
    block, wanted = fields[0, 0], cotangent[0, 0]
    size, c = block.shape[0], block.shape[-1]
    half = size // 2
    count = lax.axis_size("tile")
    cols = max(4, count // 8)
    shape = weight_first.shape
    one, two = weight_first.reshape(9, c, c), weight_second.reshape(9, c, c)
    flops = 2 * size * size * 9 * c * c

    S = jax.ShapeDtypeStruct
    sent = [S((size, c), bf16)] * 4
    halo = S((4, size, c), f32)
    edge = [S((half, 8, 2 * c), f32)] * 2 + [S((size, c), f32)] * 2
    pairs = lambda kind: S((half, size, 2 * c), kind)
    shifted = S(((half + 1) * size, 6 * c), bf16)
    V = lambda leaf: pltpu.VMEM(leaf.shape, leaf.dtype)
    ahead = [pltpu.VMEM((6 * c, 2 * c), bf16)] * 2
    back = [pltpu.VMEM((2 * c, 6 * c), bf16)] * 2
    rooms = [V(leaf) for leaf in edge] + [pltpu.VMEM((size, c), f32)] * 2
    long = pltpu.VMEM((4, size + 16, c), f32)
    whole = lambda arrays: [(array, None) for array in arrays]

    def edge_blocks(array):
        last = size // 8 - 1
        return [
            (array, pl.BlockSpec((half, 8, 2 * c), lambda step: (0, 0, 0))),
            (array, pl.BlockSpec((half, 8, 2 * c), lambda step: (0, last, 0))),
            (array, pl.BlockSpec((1, size, c), lambda step: (0, 0, 0))),
            (array, pl.BlockSpec((1, size, c), lambda step: (half - 1, 0, 1))),
        ]

    def image_edges(array):
        last = size // 16 - 1
        return [
            (array, pl.BlockSpec((size, 16, c), lambda step: (0, 0, 0))),
            (array, pl.BlockSpec((size, 16, c), lambda step: (0, last, 0))),
            (array, pl.BlockSpec((1, size, c), lambda step: (0, 0, 0))),
            (array, pl.BlockSpec((1, size, c), lambda step: (size - 1, 0, 0))),
        ]

    far = pl.BlockSpec(memory_space=pl.ANY)
    stay = lambda array: (pltpu.with_memory_space_constraint(array, pltpu.HBM), far)
    *strips, found, block, one = call(
        functools.partial(first_strips, cols),
        "first_strips",
        [stay(neighbours.T), stay(block), stay(one)],
        sent + [S((8, 8, 128), jnp.int32), S(block.shape, bf16), S(one.shape, bf16)],
        [V(halo), pltpu.VMEM((2, size, 16, c), bf16), pltpu.VMEM((2, size, c), bf16)]
        + [pltpu.SMEM(neighbours.shape[::-1], jnp.int32), pltpu.SemaphoreType.DMA((7,))],
    )
    links = (found, None)
    strips = swap_all(strips, cols)
    shifted_one, pre_one, hidden, slope = call(
        first_bulk,
        "first_bulk",
        whole([block, one]),
        [shifted, pairs(f32), pairs(bf16), pairs(bf16)],
        [V(pairs(bf16))] + ahead,
        flops,
    )
    found = call(
        first_edges,
        "first_edges",
        [links] + whole(strips) + [(one, None)] + edge_blocks(pre_one),
        sent + edge + edge + [halo],
        rooms + [V(halo), long],
    )
    strips, hidden_edges, slope_edges, halo_one = found[:4], found[4:8], found[8:12], found[12]
    strips = swap_all(strips, cols)
    shifted_two, pre_two, out_bulk, delta_bulk = call(
        second_bulk,
        "second_bulk",
        whole([hidden, *hidden_edges, two, wanted]),
        [shifted, pairs(f32), pairs(bf16), pairs(bf16)],
        [V(pairs(f32))] + ahead,
        flops,
    )
    found = call(
        second_edges,
        "second_edges",
        [links] + whole(strips) + [(two, None)] + edge_blocks(pre_two) + image_edges(wanted),
        sent + edge + edge + [halo],
        rooms + [V(halo), long, V(halo)],
    )
    strips, out_edges, delta_edges, halo_two = found[:4], found[4:8], found[8:12], found[12]
    strips = swap_all(strips, cols)
    grad_two, grad_hidden, delta_one = call(
        second_back,
        "second_back",
        whole(
            [delta_bulk, *delta_edges, halo_two, shifted_two, two, slope]
        ),
        [S((9, c, c), f32), pairs(f32), pairs(bf16)],
        [V(pairs(f32)), V(pairs(bf16))] + back + [V(shifted), V(halo), long],
        2 * flops,
    )
    found = call(
        first_back,
        "first_back",
        [links]
        + whole(strips)
        + edge_blocks(grad_hidden)
        + whole([*slope_edges, delta_one, halo_one, shifted_one, grad_two]),
        [pairs(bf16)] + edge + [S((9, c, c), f32), S((9, c, c), bf16)],
        rooms + [V(halo), long, V(halo), V(pairs(f32)), pltpu.VMEM((9, c, c), f32)],
        flops,
    )
    delta_one, delta_edges, kept, given = found[0], found[1:5], *found[5:]
    strips = call(
        first_returns,
        "first_returns",
        [links] + whole([*delta_edges, one]),
        sent,
        [V(halo), long, V(halo)],
    )
    interior, out_field = call(
        last_bulk,
        "last_bulk",
        whole([delta_one, one, out_bulk, *out_edges]),
        [pairs(f32), S(block.shape, bf16)],
        [V(pairs(f32)), V(shifted)] + back,
        flops,
    )
    part, strips, interior = summed_part(
        kept.reshape(9 * c, c), given.reshape(9 * c, c), strips, routes(cols), interior
    )
    part, strips = lax.optimization_barrier((part, strips))
    (grad_block,) = call(
        last_edges,
        "last_edges",
        [links] + whole([*strips, interior]),
        [S(block.shape, bf16)],
        rooms + [V(halo), V(pairs(f32))],
    )
    half_grads = gather_quarters(part)
    half_grads, grad_block = lax.optimization_barrier((half_grads, grad_block))
    grads = call(
        both_grads,
        "both_grads",
        whole([half_grads, flip_swap(half_grads, 0, 1)]),
        [S((9 * c, c), f32)] * 2,
        [],
    )
    grad_first, grad_second = (grad.reshape(shape) for grad in grads)
    return (out_field[None, None], grad_block[None, None], grad_first, grad_second)


def solution(mesh):
    placed = (P("ens", "tile", None, None, None), P(), P(), P(), P("ens", "tile", None, None, None))
    return jax.shard_map(
        local,
        mesh=mesh,
        in_specs=placed,
        out_specs=(
            P("ens", "tile", None, None, None),
            P("ens", "tile", None, None, None),
            P(),
            P(),
        ),
        check_vma=False,
    )
```

```python
import functools

import jax
import jax.numpy as jnp
from jax import lax
from jax.experimental import pallas as pl
from jax.experimental.pallas import tpu as pltpu
from jax.sharding import PartitionSpec as P

root_half = 0.7071067811865476
inv_root_tau = 0.3989422804014327
bf16, f32 = jnp.bfloat16, jnp.float32
NT = (((1,), (1,)), ((), ()))
TN = (((0,), (0,)), ((), ()))


def gelu_both(pre):
    bell = 0.5 * (1.0 + lax.erf(pre * root_half))
    return pre * bell, bell + pre * jnp.exp(-0.5 * pre * pre) * inv_root_tau


def partners(index, count, cols):
    odd, row_odd = index & 1, (index // cols) & 1
    return [
        (index + cols * (2 * row_odd - 1) + count) % count,
        (index + cols * (1 - 2 * row_odd) + count) % count,
        (index - 1 + 2 * odd + count) % count,
        (index + 1 - 2 * odd + count) % count,
    ]


def write_links(table, cols, found):
    count = lax.axis_size("tile")
    me = lax.axis_index("tile")
    for k, other in enumerate(partners(me, count, cols)):
        side, back = jnp.int32(0), jnp.int32(0)
        for s in range(1, 4):
            side = jnp.where(table[s, me] == other, s, side)
            back = jnp.where(table[s, other] == me, s, back)
        turn = jnp.where((side >= 2) == (back >= 2), 1, 0)
        found[k] = jnp.full(found.shape[1:], side, jnp.int32)
        found[4 + k] = jnp.full(found.shape[1:], turn, jnp.int32)


def send_strips(found, strips, outs):
    _, size, c = strips.shape
    at_row = lax.broadcasted_iota(jnp.int32, (size, size), 0)
    at_col = lax.broadcasted_iota(jnp.int32, (size, size), 1)
    for k, out in enumerate(outs):
        turn = found[4 + k][0:1, 0:size] == 1
        order = (at_col == jnp.where(turn, size - 1 - at_row, at_row)).astype(f32).astype(bf16)
        side = found[k][None]
        chosen = jnp.zeros((size // 8, 8, c), f32)
        for s in range(4):
            chosen = jnp.where(side == s, strips[s].reshape(chosen.shape), chosen)
        chosen = chosen.reshape(size, c).astype(bf16)
        out[...] = jnp.dot(order, chosen, preferred_element_type=f32).astype(bf16)


def take_strips(found, received, strips):
    _, size, c = strips.shape
    blocks = [block[...].astype(f32).reshape(size // 8, 8, c) for block in received]
    for s in range(4):
        taken = blocks[0]
        for k in range(1, 4):
            taken = jnp.where(found[k][None] == s, blocks[k], taken)
        strips[s] = taken.reshape(size, c)


def routes(cols):
    count = lax.axis_size("tile")
    return list(zip(*[partners(p, count, cols) for p in range(count)]))


def swap_all(blocks, cols):
    return [
        lax.ppermute(block, "tile", list(enumerate(way)))
        for block, way in zip(blocks, routes(cols))
    ]


def fill_columns(shifted, pairs):
    count, size, lanes = pairs.shape
    c = lanes // 2
    at = lax.broadcasted_iota(jnp.int32, (size, c), 0)
    first, last = at == 0, at == size - 1
    shifted[0:size, 0 : 3 * c] = jnp.zeros((size, 3 * c), bf16)
    shifted[count * size :, 3 * c :] = jnp.zeros((size, 3 * c), bf16)
    for i in range(count):
        for parity, row, lane in ((1, (i + 1) * size, 0), (0, i * size, 3 * c)):
            value = pairs[i, :, parity * c : (parity + 1) * c].astype(f32)
            before = jnp.where(first, 0.0, pltpu.roll(value, 1, 0))
            after = jnp.where(last, 0.0, pltpu.roll(value, size - 1, 0))
            shifted[row : row + size, lane : lane + c] = before.astype(bf16)
            shifted[row : row + size, lane + c : lane + 2 * c] = value.astype(bf16)
            shifted[row : row + size, lane + 2 * c : lane + 3 * c] = after.astype(bf16)


def blocks_of_pairs(tap, lower, upper, c):
    for b in range(3):
        for half, parity, target, a in (
            (lower, 0, 0, 0),
            (lower, 0, 1, None),
            (lower, 1, 0, 1),
            (lower, 1, 1, 0),
            (upper, 0, 0, 2),
            (upper, 0, 1, 1),
            (upper, 1, 0, None),
            (upper, 1, 1, 2),
        ):
            yield half, (parity * 3 + b) * c, target * c, tap(a, b) if a is not None else None


def bulk_conv(shifted, weight, lower, upper, out, backward):
    c = weight.shape[-1]
    count, size, lanes = out.shape
    if backward:
        tap = lambda a, b: weight[(2 - a) * 3 + 2 - b]
    else:
        tap = lambda a, b: weight[a * 3 + b]
    for half, depth, target, block in blocks_of_pairs(tap, lower, upper, c):
        if block is None:
            block = jnp.zeros((c, c), bf16)
        if backward:
            half[target : target + c, depth : depth + c] = block
        else:
            half[depth : depth + c, target : target + c] = block
    rows = count * size
    dims = NT if backward else (((1,), (0,)), ((), ()))
    total = lax.dot_general(
        shifted[0:rows, :], lower[...], dims, preferred_element_type=f32
    ) + lax.dot_general(shifted[size : size + rows, :], upper[...], dims, preferred_element_type=f32)
    out[...] = total.reshape(count, size, lanes)


def bulk_weight_grad(shifted, delta, out):
    count, size, lanes = delta.shape
    c = lanes // 2
    rows = count * size
    flat = delta[...].reshape(rows, lanes)
    low = lax.dot_general(shifted[0:rows, :], flat, TN, preferred_element_type=f32)
    high = lax.dot_general(shifted[size : size + rows, :], flat, TN, preferred_element_type=f32)
    for b in range(3):
        here, there = b * c, (3 + b) * c
        out[b] = low[here : here + c, 0:c] + low[there : there + c, c:]
        out[3 + b] = low[there : there + c, 0:c] + high[here : here + c, c:]
        out[6 + b] = high[here : here + c, 0:c] + high[there : there + c, c:]


def load_edges(left, right, top, bottom):
    return left[...], right[...], top[0], bottom[0]


def to_pairs(strip, room):
    room[...] = strip
    half = strip.shape[0] // 2
    return jnp.concatenate(
        [room[pl.ds(0, half, stride=2), :], room[pl.ds(1, half, stride=2), :]], axis=1
    )


def add_strips(edges, strips, rooms):
    left, right, top, bottom = edges
    t, r, b, l = strips
    c = t.shape[1]
    half, depth, size = left.shape[0], left.shape[1], t.shape[0]
    at = lax.broadcasted_iota(jnp.int32, left.shape, 1)
    left_room, right_room, top_room, bottom_room, strip_a, strip_b = rooms
    left_room[...] = left + jnp.where(at == 0, to_pairs(l, strip_a)[:, None, :], 0.0)
    right_room[...] = right + jnp.where(at == depth - 1, to_pairs(r, strip_b)[:, None, :], 0.0)
    left_room[0, :, 0:c] += t[0:depth]
    left_room[half - 1, :, c:] += b[0:depth]
    right_room[0, :, 0:c] += t[size - depth :]
    right_room[half - 1, :, c:] += b[size - depth :]
    top_room[...] = top + t
    bottom_room[...] = bottom + b
    top_room[0:depth] = left_room[0, :, 0:c]
    top_room[size - depth :] = right_room[0, :, 0:c]
    bottom_room[0:depth] = left_room[half - 1, :, c:]
    bottom_room[size - depth :] = right_room[half - 1, :, c:]
    return left_room[...], right_room[...], top_room[...], bottom_room[...]


def edge_strips(edges, strips):
    left, right, top, bottom = edges
    c = top.shape[1]
    half = left.shape[0]
    strips[0] = top
    strips[2] = bottom
    for side, column in ((1, right[:, -1, :]), (3, left[:, 0, :])):
        strips[side, pl.ds(0, half, stride=2), :] = column[:, 0:c]
        strips[side, pl.ds(1, half, stride=2), :] = column[:, c:]


def lay_edges(pairs, left, right, top, bottom):
    depth = left.shape[1]
    size = pairs.shape[1]
    c = top.shape[-1]
    pairs[:, 0:depth, :] = left[...]
    pairs[:, size - depth :, :] = right[...]
    pairs[0, :, 0:c] = top[...]
    pairs[pairs.shape[0] - 1, :, c:] = bottom[...]


def halo_windows(strips, rooms):
    size = strips.shape[1]
    top, right, bottom, left = (strips[s] for s in range(4))
    zero = jnp.zeros_like(top[0:1])
    ends = [
        (0.5 * (top[0:1] + left[0:1]), 0.5 * (top[size - 1 :] + right[0:1])),
        (zero, zero),
        (0.5 * (left[size - 1 :] + bottom[0:1]), 0.5 * (bottom[size - 1 :] + right[size - 1 :])),
        (zero, zero),
    ]
    windows = []
    for s, (strip, (before, after)) in enumerate(zip((top, right, bottom, left), ends)):
        rooms[s, 7:8, :] = before
        rooms[s, 8 : 8 + size, :] = strip
        rooms[s, 8 + size : 9 + size, :] = after
        windows.append(
            jnp.concatenate([rooms[s, 7 + k : 7 + k + size, :] for k in range(3)], axis=1).astype(
                bf16
            )
        )
    return windows


side_taps = ((0, 1, 2), (2, 5, 8), (6, 7, 8), (0, 3, 6))


def halo_terms(windows, weight):
    return [
        jnp.dot(
            window,
            jnp.concatenate([weight[tap] for tap in taps], axis=0),
            preferred_element_type=f32,
        )
        for window, taps in zip(windows, side_taps)
    ]


def halo_weight_grad(windows, strips, out):
    c = out.shape[-1]
    for s, (window, taps) in enumerate(zip(windows, side_taps)):
        term = lax.dot_general(window, strips[s].astype(bf16), TN, preferred_element_type=f32)
        for k, tap in enumerate(taps):
            out[tap] += term[k * c : (k + 1) * c]


def halo_grads(strips, weight, rooms, grads):
    size, c = strips.shape[1:]
    long = size + 8
    for s, taps in enumerate(side_taps):
        rooms[s, 0:8, :] = jnp.zeros((8, c), f32)
        rooms[s, 8 : 8 + size, :] = strips[s]
        rooms[s, 8 + size :, :] = jnp.zeros((8, c), f32)
        copies = jnp.concatenate([rooms[s, 8 - k : 8 - k + long, :] for k in range(3)], axis=1)
        rims = jnp.concatenate([weight[tap] for tap in taps], axis=1)
        rim = lax.dot_general(copies.astype(bf16), rims, NT, preferred_element_type=f32)
        rooms[s, 0:long, :] = rim
        at = lax.broadcasted_iota(jnp.int32, (size, c), 0)
        corner = jnp.where(at == 0, rooms[s, 0:1, :], 0.0) + jnp.where(
            at == size - 1, rooms[s, size + 1 : size + 2, :], 0.0
        )
        grads[s] = rooms[s, 1 : 1 + size, :] + 0.5 * corner


def exact(values):
    return [value.astype(bf16).astype(f32) for value in values]


def first_strips(cols, table, block, weight, *refs):
    outs, found, held, held_weight = refs[:4], *refs[4:7]
    strips, columns, rows, near, arrived = refs[7:12]
    size = block.shape[0]
    pairs = [
        (table, near),
        (block.at[0], rows.at[0]),
        (block.at[size - 1], rows.at[1]),
        (block.at[:, pl.ds(0, 16), :], columns.at[0]),
        (block.at[:, pl.ds(size - 16, 16), :], columns.at[1]),
        (block, held),
        (weight, held_weight),
    ]
    copies = [
        pltpu.make_async_copy(source, target, arrived.at[k])
        for k, (source, target) in enumerate(pairs)
    ]
    for copy in copies:
        copy.start()
    copies[0].wait()
    write_links(near, cols, found)
    for copy in copies[1:5]:
        copy.wait()
    strips[0] = rows[0].astype(f32)
    strips[2] = rows[1].astype(f32)
    strips[3] = columns[0].astype(f32)[:, 0, :]
    strips[1] = columns[1].astype(f32)[:, 15, :]
    send_strips(found, strips, outs)
    for copy in copies[5:]:
        copy.wait()


def first_bulk(block, weight, shifted, pre, hidden, slope, pairs, lower, upper):
    count, size, lanes = pre.shape
    c = lanes // 2
    for i in range(count):
        pairs[i, :, 0:c] = block[2 * i]
        pairs[i, :, c:] = block[2 * i + 1]
    fill_columns(shifted, pairs)
    bulk_conv(shifted, weight, lower, upper, pre, False)
    for i in range(count):
        value, rate = gelu_both(pre[i])
        hidden[i] = value.astype(bf16)
        slope[i] = rate.astype(bf16)


def first_edges(found, *refs):
    received, weight, blocks = refs[:4], refs[4], refs[5:9]
    outs, hidden, slope, halo = refs[9:13], refs[13:17], refs[17:21], refs[21]
    rooms, strips, long = refs[22:28], refs[28], refs[29]
    take_strips(found, received, halo)
    terms = halo_terms(halo_windows(halo, long), weight)
    edges = add_strips(load_edges(*blocks), terms, rooms)
    both = [gelu_both(edge) for edge in edges]
    values = exact([value for value, _ in both])
    for k in range(4):
        hidden[k][...] = values[k]
        slope[k][...] = both[k][1]
    edge_strips(values, strips)
    send_strips(found, strips, outs)


def second_bulk(hidden, left, right, top, bottom, weight, cotangent, *refs):
    shifted, pre, out_field, delta, pairs, lower, upper = refs
    count, size, lanes = pre.shape
    c = lanes // 2
    pairs[...] = hidden[...].astype(f32)
    lay_edges(pairs, left, right, top, bottom)
    fill_columns(shifted, pairs)
    bulk_conv(shifted, weight, lower, upper, pre, False)
    for i in range(count):
        for parity in range(2):
            part = slice(parity * c, (parity + 1) * c)
            value, rate = gelu_both(pre[i, :, part])
            out_field[i, :, part] = value.astype(bf16)
            delta[i, :, part] = (cotangent[2 * i + parity].astype(f32) * rate).astype(bf16)


def second_edges(found, *refs):
    received, weight, blocks, wanted = refs[:4], refs[4], refs[5:9], refs[9:13]
    outs, out_field, delta, halo = refs[13:17], refs[17:21], refs[21:25], refs[25]
    rooms, strips, long, grads = refs[26:32], refs[32], refs[33], refs[34]
    half, depth = blocks[0].shape[:2]
    take_strips(found, received, halo)
    terms = halo_terms(halo_windows(halo, long), weight)
    edges = add_strips(load_edges(*blocks), terms, rooms)
    cots = []
    for ref, at in ((wanted[0], 0), (wanted[1], 16 - depth)):
        block = ref[...].astype(f32)
        block = block.reshape((half, 2) + block.shape[1:])[:, :, at : at + depth, :]
        cots.append(jnp.concatenate([block[:, 0], block[:, 1]], axis=-1))
    cots += [wanted[2][0].astype(f32), wanted[3][0].astype(f32)]
    both = [gelu_both(edge) for edge in edges]
    deltas = exact([cot * rate for cot, (_, rate) in zip(cots, both)])
    for k in range(4):
        out_field[k][...] = both[k][0]
        delta[k][...] = deltas[k]
    edge_strips(deltas, strips)
    halo_grads(strips, weight, long, grads)
    send_strips(found, grads, outs)


def second_back(*refs):
    bulk_delta, delta_edges, halo = refs[0], refs[1:5], refs[5]
    shifted, weight, bulk_slope = refs[6:9]
    grad_weight, grad_hidden, delta_first = refs[9:12]
    pairs, delta, lower, upper, moved, strips, long = refs[12:19]
    count = pairs.shape[0]
    pairs[...] = bulk_delta[...].astype(f32)
    lay_edges(pairs, *delta_edges)
    delta[...] = pairs[...].astype(bf16)
    bulk_weight_grad(shifted, delta, grad_weight)
    edge_strips([ref[...] for ref in delta_edges], strips)
    halo_weight_grad(halo_windows(halo, long), strips, grad_weight)
    fill_columns(moved, pairs)
    bulk_conv(moved, weight, lower, upper, grad_hidden, True)
    for i in range(count):
        delta_first[i] = (grad_hidden[i] * bulk_slope[i].astype(f32)).astype(bf16)


def first_back(found, *refs):
    received, blocks, slope, bulk_delta = refs[:4], refs[4:8], refs[8:12], refs[12]
    halo, shifted, other_grad = refs[13:16]
    delta, edges_out, kept, given = refs[16], refs[17:21], refs[21], refs[22]
    rooms, strips, long, back, pairs, grad_weight = refs[23:29], *refs[29:34]
    take_strips(found, received, back)
    edges = add_strips(load_edges(*blocks), [back[s] for s in range(4)], rooms)
    deltas = exact([edge * rate[...] for edge, rate in zip(edges, slope)])
    for k in range(4):
        edges_out[k][...] = deltas[k]
    edge_strips(deltas, strips)
    pairs[...] = bulk_delta[...].astype(f32)
    lay_edges(pairs, *deltas)
    delta[...] = pairs[...].astype(bf16)
    bulk_weight_grad(shifted, delta, grad_weight)
    halo_weight_grad(halo_windows(halo, long), strips, grad_weight)
    core = lax.axis_index("tile") & 1
    for tap in range(grad_weight.shape[0]):
        one, two = grad_weight[tap], other_grad[tap]
        kept[tap] = jnp.where(core == 0, one, two)
        given[tap] = jnp.where(core == 0, two, one).astype(bf16)


def first_returns(found, *refs):
    edges, weight, outs = refs[:4], refs[4], refs[5:9]
    strips, long, grads = refs[9:12]
    edge_strips([edge[...] for edge in edges], strips)
    halo_grads(strips, weight, long, grads)
    send_strips(found, grads, outs)


def last_bulk(delta, weight, bulk_out, *refs):
    out_edges, interior, out_field, pairs, moved, lower, upper = refs[:4], *refs[4:10]
    count, size, lanes = pairs.shape
    c = lanes // 2
    pairs[...] = bulk_out[...].astype(f32)
    lay_edges(pairs, *out_edges)
    for i in range(count):
        out_field[2 * i] = pairs[i, :, 0:c].astype(bf16)
        out_field[2 * i + 1] = pairs[i, :, c:].astype(bf16)
    pairs[...] = delta[...].astype(f32)
    fill_columns(moved, pairs)
    bulk_conv(moved, weight, lower, upper, interior, True)


def last_edges(found, *refs):
    received, interior, grad = refs[:4], refs[4], refs[5]
    rooms, back, pairs = refs[6:12], refs[12], refs[13]
    count, size, lanes = interior.shape
    c = lanes // 2
    take_strips(found, received, back)
    edges = (
        interior[:, 0:8, :],
        interior[:, size - 8 :, :],
        interior[0, :, 0:c],
        interior[count - 1, :, c:],
    )
    edges = add_strips(edges, [back[s] for s in range(4)], rooms)
    pairs[...] = interior[...]
    lay_edges(pairs, *edges)
    for i in range(count):
        grad[2 * i] = pairs[i, :, 0:c].astype(bf16)
        grad[2 * i + 1] = pairs[i, :, c:].astype(bf16)


def call(kernel, name, ins, outs, scratch, cost=0, room=16 << 20):
    whole = pl.BlockSpec(memory_space=pltpu.VMEM)
    return pl.pallas_call(
        kernel,
        name=name,
        grid=(1,),
        in_specs=[spec or whole for _, spec in ins],
        out_specs=[whole] * len(outs),
        out_shape=outs,
        scratch_shapes=scratch,
        compiler_params=pltpu.CompilerParams(vmem_limit_bytes=room),
        cost_estimate=pl.CostEstimate(flops=cost, bytes_accessed=2 << 20, transcendentals=0),
    )(*[array for array, _ in ins])


def flip_swap(block, mask_ens, mask_tile):
    ens, tile = lax.axis_size("ens"), lax.axis_size("tile")
    route = [
        (e * tile + t, (e ^ mask_ens) * tile + (t ^ mask_tile))
        for e in range(ens)
        for t in range(tile)
    ]
    return lax.ppermute(block, ("ens", "tile"), route)


def seat_of():
    return lax.axis_index("ens") * 2 + (lax.axis_index("tile") >> 1 & 1)


def share_out(kept, given, own, *sent):
    rows = own.shape[0]
    seat = seat_of()
    quarter = lambda at: pl.ds(pl.multiple_of(at * rows, rows), rows)
    add = lambda at: kept[quarter(at), :] + given[quarter(at), :].astype(f32)
    own[...] = add(seat)
    for k, block in enumerate(sent):
        block[...] = add(seat ^ (3, 2, 1)[k]).astype(bf16)


def add_up(count, loads, base, *refs):
    got, riders = refs[:count], refs[count : count + loads]
    total, loaded, came = refs[count + loads], refs[count + loads + 1 :][:loads], refs[count + 2 * loads + 1 :]
    rows = base.shape[0]
    terms = [base[...].astype(f32)] + [block[0:rows].astype(f32) for block in got]
    while len(terms) > 1:
        terms = [terms[i] + terms[i + 1] for i in range(0, len(terms), 2)]
    total[...] = terms[0].astype(bf16)
    for block, rider in zip(loaded, riders):
        block[0:rows] = terms[0].astype(bf16)
        block[rows:] = rider[...]
    for block, place in zip([block for block in got if block.shape[0] > rows], came):
        place[...] = block[rows:]


def summed_part(kept, given, riders, ways, beside):
    tiles = lax.axis_size("tile")
    rows, lanes = kept.shape[0] // 4, kept.shape[1]
    groups, bit = [], 4
    while bit < tiles:
        groups.append([3 * bit, 2 * bit, bit] if 2 * bit < tiles else [bit])
        bit *= 4
    S = jax.ShapeDtypeStruct
    given, riders = lax.optimization_barrier((flip_swap(given, 0, 1), riders))
    base, *sent = call(
        share_out,
        "share_out",
        [(kept, None), (given, None)],
        [S((rows, lanes), f32)] + [S((rows, lanes), bf16)] * 3,
        [],
    )
    got = [flip_swap(block, k >> 1, (k & 1) << 1) for k, block in zip((3, 2, 1), sent)]
    carried, coming = {}, []
    for n, masks in enumerate(groups + [[]]):
        aboard = {}
        for mask in masks:
            way = tuple(t ^ mask for t in range(tiles))
            if way in ways:
                aboard[mask] = ways.index(way)
        loads = [riders[k] for k in aboard.values()]
        found = call(
            functools.partial(add_up, len(got), len(loads)),
            "add_up",
            [(block, None) for block in (base, *got, *loads)],
            [S((rows, lanes), bf16)]
            + [S((rows + load.shape[0], lanes), bf16) for load in loads]
            + [S(riders[k].shape, bf16) for k in coming],
            [],
        )
        if n == 0:
            found, beside = lax.optimization_barrier((found, beside))
        base, loaded = found[0], dict(zip(aboard, found[1 : 1 + len(loads)]))
        carried.update(zip(coming, found[1 + len(loads) :]))
        got = [flip_swap(loaded.get(mask, base), 0, mask) for mask in masks]
        coming = list(aboard.values())
    for k, way in enumerate(ways):
        if k not in carried:
            carried[k] = lax.ppermute(riders[k], "tile", list(enumerate(way)))
    return base, [carried[k] for k in range(len(ways))], beside


def gather_quarters(part):
    return [part] + [flip_swap(part, k >> 1, (k & 1) << 1) for k in (1, 2, 3)]


def both_grads(*refs):
    mine, others, first, second = refs[:4], refs[4:8], refs[8], refs[9]
    rows = mine[0].shape[0]
    core, seat = lax.axis_index("tile") & 1, seat_of()
    for k in range(4):
        place = pl.ds(pl.multiple_of((seat ^ k) * rows, rows), rows)
        one, two = mine[k][...].astype(f32), others[k][...].astype(f32)
        first[place, :] = jnp.where(core == 0, one, two)
        second[place, :] = jnp.where(core == 0, two, one)


def local(fields, weight_first, weight_second, neighbours, cotangent):
    block, wanted = fields[0, 0], cotangent[0, 0]
    size, c = block.shape[0], block.shape[-1]
    half = size // 2
    count = lax.axis_size("tile")
    cols = max(4, count // 8)
    shape = weight_first.shape
    one, two = weight_first.reshape(9, c, c), weight_second.reshape(9, c, c)
    flops = 2 * size * size * 9 * c * c

    S = jax.ShapeDtypeStruct
    sent = [S((size, c), bf16)] * 4
    halo = S((4, size, c), f32)
    edge = [S((half, 8, 2 * c), f32)] * 2 + [S((size, c), f32)] * 2
    pairs = lambda kind: S((half, size, 2 * c), kind)
    shifted = S(((half + 1) * size, 6 * c), bf16)
    V = lambda leaf: pltpu.VMEM(leaf.shape, leaf.dtype)
    ahead = [pltpu.VMEM((6 * c, 2 * c), bf16)] * 2
    back = [pltpu.VMEM((2 * c, 6 * c), bf16)] * 2
    rooms = [V(leaf) for leaf in edge] + [pltpu.VMEM((size, c), f32)] * 2
    long = pltpu.VMEM((4, size + 16, c), f32)
    whole = lambda arrays: [(array, None) for array in arrays]

    def edge_blocks(array):
        last = size // 8 - 1
        return [
            (array, pl.BlockSpec((half, 8, 2 * c), lambda step: (0, 0, 0))),
            (array, pl.BlockSpec((half, 8, 2 * c), lambda step: (0, last, 0))),
            (array, pl.BlockSpec((1, size, c), lambda step: (0, 0, 0))),
            (array, pl.BlockSpec((1, size, c), lambda step: (half - 1, 0, 1))),
        ]

    def image_edges(array):
        last = size // 16 - 1
        return [
            (array, pl.BlockSpec((size, 16, c), lambda step: (0, 0, 0))),
            (array, pl.BlockSpec((size, 16, c), lambda step: (0, last, 0))),
            (array, pl.BlockSpec((1, size, c), lambda step: (0, 0, 0))),
            (array, pl.BlockSpec((1, size, c), lambda step: (size - 1, 0, 0))),
        ]

    far = pl.BlockSpec(memory_space=pl.ANY)
    stay = lambda array: (pltpu.with_memory_space_constraint(array, pltpu.HBM), far)
    *strips, found, block, one = call(
        functools.partial(first_strips, cols),
        "first_strips",
        [stay(neighbours.T), stay(block), stay(one)],
        sent + [S((8, 8, 128), jnp.int32), S(block.shape, bf16), S(one.shape, bf16)],
        [V(halo), pltpu.VMEM((2, size, 16, c), bf16), pltpu.VMEM((2, size, c), bf16)]
        + [pltpu.SMEM(neighbours.shape[::-1], jnp.int32), pltpu.SemaphoreType.DMA((7,))],
    )
    links = (found, None)
    strips = swap_all(strips, cols)
    shifted_one, pre_one, hidden, slope = call(
        first_bulk,
        "first_bulk",
        whole([block, one]),
        [shifted, pairs(f32), pairs(bf16), pairs(bf16)],
        [V(pairs(bf16))] + ahead,
        flops,
    )
    found = call(
        first_edges,
        "first_edges",
        [links] + whole(strips) + [(one, None)] + edge_blocks(pre_one),
        sent + edge + edge + [halo],
        rooms + [V(halo), long],
    )
    strips, hidden_edges, slope_edges, halo_one = found[:4], found[4:8], found[8:12], found[12]
    strips = swap_all(strips, cols)
    shifted_two, pre_two, out_bulk, delta_bulk = call(
        second_bulk,
        "second_bulk",
        whole([hidden, *hidden_edges, two, wanted]),
        [shifted, pairs(f32), pairs(bf16), pairs(bf16)],
        [V(pairs(f32))] + ahead,
        flops,
    )
    found = call(
        second_edges,
        "second_edges",
        [links] + whole(strips) + [(two, None)] + edge_blocks(pre_two) + image_edges(wanted),
        sent + edge + edge + [halo],
        rooms + [V(halo), long, V(halo)],
    )
    strips, out_edges, delta_edges, halo_two = found[:4], found[4:8], found[8:12], found[12]
    strips = swap_all(strips, cols)
    grad_two, grad_hidden, delta_one = call(
        second_back,
        "second_back",
        whole(
            [delta_bulk, *delta_edges, halo_two, shifted_two, two, slope]
        ),
        [S((9, c, c), f32), pairs(f32), pairs(bf16)],
        [V(pairs(f32)), V(pairs(bf16))] + back + [V(shifted), V(halo), long],
        2 * flops,
    )
    found = call(
        first_back,
        "first_back",
        [links]
        + whole(strips)
        + edge_blocks(grad_hidden)
        + whole([*slope_edges, delta_one, halo_one, shifted_one, grad_two]),
        [pairs(bf16)] + edge + [S((9, c, c), f32), S((9, c, c), bf16)],
        rooms + [V(halo), long, V(halo), V(pairs(f32)), pltpu.VMEM((9, c, c), f32)],
        flops,
    )
    delta_one, delta_edges, kept, given = found[0], found[1:5], *found[5:]
    strips = call(
        first_returns,
        "first_returns",
        [links] + whole([*delta_edges, one]),
        sent,
        [V(halo), long, V(halo)],
    )
    interior, out_field = call(
        last_bulk,
        "last_bulk",
        whole([delta_one, one, out_bulk, *out_edges]),
        [pairs(f32), S(block.shape, bf16)],
        [V(pairs(f32)), V(shifted)] + back,
        flops,
    )
    part, strips, interior = summed_part(
        kept.reshape(9 * c, c), given.reshape(9 * c, c), strips, routes(cols), interior
    )
    part, strips = lax.optimization_barrier((part, strips))
    (grad_block,) = call(
        last_edges,
        "last_edges",
        [links] + whole([*strips, interior]),
        [S(block.shape, bf16)],
        rooms + [V(halo), V(pairs(f32))],
    )
    quarters = gather_quarters(part)
    others = [flip_swap(quarter, 0, 1) for quarter in quarters]
    others, grad_block = lax.optimization_barrier((others, grad_block))
    grads = call(
        both_grads,
        "both_grads",
        whole([*quarters, *others]),
        [S((9 * c, c), f32)] * 2,
        [],
    )
    grad_first, grad_second = (grad.reshape(shape) for grad in grads)
    return (out_field[None, None], grad_block[None, None], grad_first, grad_second)


def solution(mesh):
    placed = (P("ens", "tile", None, None, None), P(), P(), P(), P("ens", "tile", None, None, None))
    return jax.shard_map(
        local,
        mesh=mesh,
        in_specs=placed,
        out_specs=(
            P("ens", "tile", None, None, None),
            P("ens", "tile", None, None, None),
            P(),
            P(),
        ),
        check_vma=False,
    )
```

```python
import functools

import jax
import jax.numpy as jnp
from jax import lax
from jax.experimental import pallas as pl
from jax.experimental.pallas import tpu as pltpu
from jax.sharding import PartitionSpec as P

root_half = 0.7071067811865476
inv_root_tau = 0.3989422804014327
bf16, f32 = jnp.bfloat16, jnp.float32
NT = (((1,), (1,)), ((), ()))
TN = (((0,), (0,)), ((), ()))


def gelu_both(pre):
    bell = 0.5 * (1.0 + lax.erf(pre * root_half))
    return pre * bell, bell + pre * jnp.exp(-0.5 * pre * pre) * inv_root_tau


def partners(index, count, cols):
    odd, row_odd = index & 1, (index // cols) & 1
    return [
        (index + cols * (2 * row_odd - 1) + count) % count,
        (index + cols * (1 - 2 * row_odd) + count) % count,
        (index - 1 + 2 * odd + count) % count,
        (index + 1 - 2 * odd + count) % count,
    ]


def write_links(table, cols, found):
    count = lax.axis_size("tile")
    me = lax.axis_index("tile")
    for k, other in enumerate(partners(me, count, cols)):
        side, back = jnp.int32(0), jnp.int32(0)
        for s in range(1, 4):
            side = jnp.where(table[s, me] == other, s, side)
            back = jnp.where(table[s, other] == me, s, back)
        turn = jnp.where((side >= 2) == (back >= 2), 1, 0)
        found[k] = jnp.full(found.shape[1:], side, jnp.int32)
        found[4 + k] = jnp.full(found.shape[1:], turn, jnp.int32)
        found[8 + k] = jnp.full(found.shape[1:], back, jnp.int32)


def masked(found, block):
    wide = jnp.concatenate([found] * (block.shape[-1] // found.shape[-1]), axis=1)
    return wide[None]


def choose(found, strips):
    _, size, c = strips.shape
    chosen = strips[0].reshape(size // 8, 8, c)
    for s in range(1, 4):
        here = masked(found, chosen) == s
        chosen = jnp.where(here, strips[s].reshape(chosen.shape), chosen)
    return chosen.reshape(size, c)


def send_strips(found, strips, outs):
    _, size, lanes = strips.shape
    c = outs[0].shape[-1]
    at_row = lax.broadcasted_iota(jnp.int32, (size, size), 0)
    at_col = lax.broadcasted_iota(jnp.int32, (size, size), 1)
    for k, out in enumerate(outs):
        turn = found[4 + k][0:1, 0:size] == 1
        order = (at_col == jnp.where(turn, size - 1 - at_row, at_row)).astype(f32).astype(bf16)
        chosen = choose(found[k], strips).astype(bf16)
        turned = jnp.dot(order, chosen, preferred_element_type=f32).astype(bf16)
        for part in range(lanes // c):
            out[part * size : (part + 1) * size] = turned[:, part * c : (part + 1) * c]


def take_strips(found, received, strips, last=False):
    _, size, c = strips.shape
    blocks = []
    for block in received:
        row = block.shape[0] - size if last else 0
        blocks.append(block[row : row + size].astype(f32).reshape(size // 8, 8, c))
    for s in range(4):
        taken = blocks[0]
        for k in range(1, 4):
            taken = jnp.where(found[k][None] == s, blocks[k], taken)
        strips[s] = taken.reshape(size, c)


def routes(cols):
    count = lax.axis_size("tile")
    return list(zip(*[partners(p, count, cols) for p in range(count)]))


def swap_all(blocks, cols):
    return [
        lax.ppermute(block, "tile", list(enumerate(way)))
        for block, way in zip(blocks, routes(cols))
    ]


def fill_columns(shifted, pairs):
    count, size, lanes = pairs.shape
    c = lanes // 2
    at = lax.broadcasted_iota(jnp.int32, (size, c), 0)
    first, last = at == 0, at == size - 1
    shifted[0:size, 0 : 3 * c] = jnp.zeros((size, 3 * c), bf16)
    shifted[count * size :, 3 * c :] = jnp.zeros((size, 3 * c), bf16)
    for i in range(count):
        for parity, row, lane in ((1, (i + 1) * size, 0), (0, i * size, 3 * c)):
            value = pairs[i, :, parity * c : (parity + 1) * c].astype(f32)
            before = jnp.where(first, 0.0, pltpu.roll(value, 1, 0))
            after = jnp.where(last, 0.0, pltpu.roll(value, size - 1, 0))
            shifted[row : row + size, lane : lane + c] = before.astype(bf16)
            shifted[row : row + size, lane + c : lane + 2 * c] = value.astype(bf16)
            shifted[row : row + size, lane + 2 * c : lane + 3 * c] = after.astype(bf16)


def blocks_of_pairs(tap, lower, upper, c):
    for b in range(3):
        for half, parity, target, a in (
            (lower, 0, 0, 0),
            (lower, 0, 1, None),
            (lower, 1, 0, 1),
            (lower, 1, 1, 0),
            (upper, 0, 0, 2),
            (upper, 0, 1, 1),
            (upper, 1, 0, None),
            (upper, 1, 1, 2),
        ):
            yield half, (parity * 3 + b) * c, target * c, tap(a, b) if a is not None else None


def bulk_conv(shifted, weight, lower, upper, out, backward):
    c = weight.shape[-1]
    count, size, lanes = out.shape
    if backward:
        tap = lambda a, b: weight[(2 - a) * 3 + 2 - b]
    else:
        tap = lambda a, b: weight[a * 3 + b]
    for half, depth, target, block in blocks_of_pairs(tap, lower, upper, c):
        if block is None:
            block = jnp.zeros((c, c), bf16)
        if backward:
            half[target : target + c, depth : depth + c] = block
        else:
            half[depth : depth + c, target : target + c] = block
    rows = count * size
    dims = NT if backward else (((1,), (0,)), ((), ()))
    total = lax.dot_general(
        shifted[0:rows, :], lower[...], dims, preferred_element_type=f32
    ) + lax.dot_general(shifted[size : size + rows, :], upper[...], dims, preferred_element_type=f32)
    out[...] = total.reshape(count, size, lanes)


def bulk_weight_grad(shifted, delta, out):
    count, size, lanes = delta.shape
    c = lanes // 2
    rows = count * size
    flat = delta[...].reshape(rows, lanes)
    low = lax.dot_general(shifted[0:rows, :], flat, TN, preferred_element_type=f32)
    high = lax.dot_general(shifted[size : size + rows, :], flat, TN, preferred_element_type=f32)
    for b in range(3):
        here, there = b * c, (3 + b) * c
        out[b] = low[here : here + c, 0:c] + low[there : there + c, c:]
        out[3 + b] = low[there : there + c, 0:c] + high[here : here + c, c:]
        out[6 + b] = high[here : here + c, 0:c] + high[there : there + c, c:]


def load_edges(left, right, top, bottom):
    return left[...], right[...], top[0], bottom[0]


def to_pairs(strip, room):
    room[...] = strip
    half = strip.shape[0] // 2
    return jnp.concatenate(
        [room[pl.ds(0, half, stride=2), :], room[pl.ds(1, half, stride=2), :]], axis=1
    )


def add_strips(edges, strips, rooms):
    left, right, top, bottom = edges
    t, r, b, l = strips
    c = t.shape[1]
    half, depth, size = left.shape[0], left.shape[1], t.shape[0]
    at = lax.broadcasted_iota(jnp.int32, left.shape, 1)
    left_room, right_room, top_room, bottom_room, strip_a, strip_b = rooms
    left_room[...] = left + jnp.where(at == 0, to_pairs(l, strip_a)[:, None, :], 0.0)
    right_room[...] = right + jnp.where(at == depth - 1, to_pairs(r, strip_b)[:, None, :], 0.0)
    left_room[0, :, 0:c] += t[0:depth]
    left_room[half - 1, :, c:] += b[0:depth]
    right_room[0, :, 0:c] += t[size - depth :]
    right_room[half - 1, :, c:] += b[size - depth :]
    top_room[...] = top + t
    bottom_room[...] = bottom + b
    top_room[0:depth] = left_room[0, :, 0:c]
    top_room[size - depth :] = right_room[0, :, 0:c]
    bottom_room[0:depth] = left_room[half - 1, :, c:]
    bottom_room[size - depth :] = right_room[half - 1, :, c:]
    return left_room[...], right_room[...], top_room[...], bottom_room[...]


def edge_strips(edges, strips):
    left, right, top, bottom = edges
    c = top.shape[1]
    half = left.shape[0]
    strips[0] = top
    strips[2] = bottom
    for side, column in ((1, right[:, -1, :]), (3, left[:, 0, :])):
        strips[side, pl.ds(0, half, stride=2), :] = column[:, 0:c]
        strips[side, pl.ds(1, half, stride=2), :] = column[:, c:]


def lay_edges(pairs, left, right, top, bottom):
    depth = left.shape[1]
    size = pairs.shape[1]
    c = top.shape[-1]
    pairs[:, 0:depth, :] = left[...]
    pairs[:, size - depth :, :] = right[...]
    pairs[0, :, 0:c] = top[...]
    pairs[pairs.shape[0] - 1, :, c:] = bottom[...]


def halo_windows(strips, rooms):
    size = strips.shape[1]
    top, right, bottom, left = (strips[s] for s in range(4))
    zero = jnp.zeros_like(top[0:1])
    ends = [
        (0.5 * (top[0:1] + left[0:1]), 0.5 * (top[size - 1 :] + right[0:1])),
        (zero, zero),
        (0.5 * (left[size - 1 :] + bottom[0:1]), 0.5 * (bottom[size - 1 :] + right[size - 1 :])),
        (zero, zero),
    ]
    windows = []
    for s, (strip, (before, after)) in enumerate(zip((top, right, bottom, left), ends)):
        rooms[s, 7:8, :] = before
        rooms[s, 8 : 8 + size, :] = strip
        rooms[s, 8 + size : 9 + size, :] = after
        windows.append(
            jnp.concatenate([rooms[s, 7 + k : 7 + k + size, :] for k in range(3)], axis=1).astype(
                bf16
            )
        )
    return windows


def rim_ends(strips, rooms, ends):
    size = strips.shape[1]
    last = size - 1
    ne, nw = rooms[0, 8 + size : 9 + size, :], rooms[0, 7:8, :]
    se, sw = rooms[2, 8 + size : 9 + size, :], rooms[2, 7:8, :]
    across = lambda at: (strips[3, at : at + 1, :], strips[1, at : at + 1, :])
    along = lambda at: (strips[0, at : at + 1, :], strips[2, at : at + 1, :])
    ends[...] = jnp.zeros_like(ends)
    for side, rows in enumerate(
        (
            ((nw, ne), across(0), across(1)),
            ((ne, se), along(last), along(last - 1)),
            ((sw, se), across(last), across(last - 1)),
            ((nw, sw), along(0), along(1)),
        )
    ):
        for depth, (before, after) in enumerate(rows):
            for turned, pair in enumerate(((before, after), (after, before))):
                ends[side, turned, 2 * depth : 2 * depth + 1, :] = pair[0]
                ends[side, turned, 2 * depth + 1 : 2 * depth + 2, :] = pair[1]


def rim_weight_grad(found, own, near, carried, grads, room, out):
    _, size, c = own.shape
    windows, deltas = [], []
    for k in range(4):
        ends = carried[k][2 * size :].astype(f32)
        rows = (
            choose(found[k], own),
            near[k][0:size].astype(f32),
            near[k][size : 2 * size].astype(f32),
        )
        for depth, row in enumerate(rows):
            room[depth, 7:8, :] = ends[2 * depth : 2 * depth + 1]
            room[depth, 8 : 8 + size, :] = row
            room[depth, 8 + size : 9 + size, :] = ends[2 * depth + 1 : 2 * depth + 2]
        part = [
            [room[d, 7 + b : 7 + b + size, :].reshape(size // 8, 8, c) for b in range(3)]
            for d in range(3)
        ]
        turned = found[4 + k][None] == 1
        back = found[8 + k][None]
        swap = lambda here, one, two: (jnp.where(here, two, one), jnp.where(here, one, two))
        for d in range(3):
            part[d][0], part[d][2] = swap(turned, part[d][0], part[d][2])
        for b in range(3):
            inward = (back == 1) | (back == 2)
            part[0][b], part[2][b] = swap(inward, part[0][b], part[2][b])
        for a, b in ((0, 1), (0, 2), (1, 2)):
            upright = (back & 1) == 1
            part[a][b], part[b][a] = swap(upright, part[a][b], part[b][a])
        windows.append(
            jnp.concatenate(
                [part[a][b].reshape(size, c).astype(bf16) for a in range(3) for b in range(3)],
                axis=1,
            )
        )
        delta = choose(found[k], grads).astype(bf16).astype(f32)
        deltas.append((delta * carried[k][size : 2 * size].astype(f32)).astype(bf16))
    term = lax.dot_general(
        jnp.concatenate(windows, axis=0),
        jnp.concatenate(deltas, axis=0),
        TN,
        preferred_element_type=f32,
    )
    for tap in range(9):
        out[tap] += term[tap * c : (tap + 1) * c]


side_taps = ((0, 1, 2), (2, 5, 8), (6, 7, 8), (0, 3, 6))


def halo_terms(windows, weight):
    return [
        jnp.dot(
            window,
            jnp.concatenate([weight[tap] for tap in taps], axis=0),
            preferred_element_type=f32,
        )
        for window, taps in zip(windows, side_taps)
    ]


def halo_weight_grad(windows, strips, out):
    c = out.shape[-1]
    for s, (window, taps) in enumerate(zip(windows, side_taps)):
        term = lax.dot_general(window, strips[s].astype(bf16), TN, preferred_element_type=f32)
        for k, tap in enumerate(taps):
            out[tap] += term[k * c : (k + 1) * c]


def halo_grads(strips, weight, rooms, grads):
    size, c = strips.shape[1:]
    long = size + 8
    for s, taps in enumerate(side_taps):
        rooms[s, 0:8, :] = jnp.zeros((8, c), f32)
        rooms[s, 8 : 8 + size, :] = strips[s]
        rooms[s, 8 + size :, :] = jnp.zeros((8, c), f32)
        copies = jnp.concatenate([rooms[s, 8 - k : 8 - k + long, :] for k in range(3)], axis=1)
        rims = jnp.concatenate([weight[tap] for tap in taps], axis=1)
        rim = lax.dot_general(copies.astype(bf16), rims, NT, preferred_element_type=f32)
        rooms[s, 0:long, :] = rim
        at = lax.broadcasted_iota(jnp.int32, (size, c), 0)
        corner = jnp.where(at == 0, rooms[s, 0:1, :], 0.0) + jnp.where(
            at == size - 1, rooms[s, size + 1 : size + 2, :], 0.0
        )
        grads[s] = rooms[s, 1 : 1 + size, :] + 0.5 * corner


def exact(values):
    return [value.astype(bf16).astype(f32) for value in values]


def first_strips(cols, table, block, weight, *refs):
    outs, found, held, held_weight, own = refs[:4], *refs[4:8]
    strips, columns, rows, near, arrived = refs[8:13]
    size, c = own.shape[1:]
    pairs = [
        (table, near),
        (block.at[pl.ds(0, 2)], rows.at[0]),
        (block.at[pl.ds(size - 2, 2)], rows.at[1]),
        (block.at[:, pl.ds(0, 16), :], columns.at[0]),
        (block.at[:, pl.ds(size - 16, 16), :], columns.at[1]),
        (block, held),
        (weight, held_weight),
    ]
    copies = [
        pltpu.make_async_copy(source, target, arrived.at[k])
        for k, (source, target) in enumerate(pairs)
    ]
    for copy in copies:
        copy.start()
    copies[0].wait()
    write_links(near, cols, found)
    for copy in copies[1:5]:
        copy.wait()
    left, right = columns[0].astype(f32), columns[1].astype(f32)
    for side, edge, second in (
        (0, rows[0, 0].astype(f32), rows[0, 1].astype(f32)),
        (1, right[:, 15, :], right[:, 14, :]),
        (2, rows[1, 1].astype(f32), rows[1, 0].astype(f32)),
        (3, left[:, 0, :], left[:, 1, :]),
    ):
        own[side] = edge
        strips[side, :, 0:c] = edge
        strips[side, :, c:] = second
    send_strips(found, strips, outs)
    for copy in copies[5:]:
        copy.wait()


def first_bulk(block, weight, shifted, pre, hidden, slope, pairs, lower, upper):
    count, size, lanes = pre.shape
    c = lanes // 2
    for i in range(count):
        pairs[i, :, 0:c] = block[2 * i]
        pairs[i, :, c:] = block[2 * i + 1]
    fill_columns(shifted, pairs)
    bulk_conv(shifted, weight, lower, upper, pre, False)
    for i in range(count):
        value, rate = gelu_both(pre[i])
        hidden[i] = value.astype(bf16)
        slope[i] = rate.astype(bf16)


def first_edges(found, *refs):
    received, weight, blocks = refs[:4], refs[4], refs[5:9]
    outs, hidden, slope, halo = refs[9:13], refs[13:17], refs[17:21], refs[21]
    rooms, strips, long, ends, narrow = refs[22:28], *refs[28:32]
    size, c = halo.shape[1:]
    take_strips(found, received, halo)
    terms = halo_terms(halo_windows(halo, long), weight)
    edges = add_strips(load_edges(*blocks), terms, rooms)
    both = [gelu_both(edge) for edge in edges]
    values = exact([value for value, _ in both])
    for k in range(4):
        hidden[k][...] = values[k]
        slope[k][...] = both[k][1]
    for k, edges in enumerate((values, [rate for _, rate in both])):
        edge_strips(edges, narrow)
        strips[:, :, k * c : (k + 1) * c] = narrow[...]
    rim_ends(halo, long, ends)
    send_strips(found, strips, outs)
    for k, out in enumerate(outs):
        straight = choose(found[k], ends.at[:, 0])
        turned = choose(found[k], ends.at[:, 1])
        here = jnp.concatenate([found[4 + k]] * 2, axis=0) == 1
        out[2 * size :] = jnp.where(here, turned, straight).astype(bf16)


def second_bulk(hidden, left, right, top, bottom, weight, cotangent, *refs):
    shifted, pre, out_field, delta, pairs, lower, upper = refs
    count, size, lanes = pre.shape
    c = lanes // 2
    pairs[...] = hidden[...].astype(f32)
    lay_edges(pairs, left, right, top, bottom)
    fill_columns(shifted, pairs)
    bulk_conv(shifted, weight, lower, upper, pre, False)
    for i in range(count):
        for parity in range(2):
            part = slice(parity * c, (parity + 1) * c)
            value, rate = gelu_both(pre[i, :, part])
            out_field[i, :, part] = value.astype(bf16)
            delta[i, :, part] = (cotangent[2 * i + parity].astype(f32) * rate).astype(bf16)


def second_edges(found, *refs):
    received, weight, blocks, wanted = refs[:4], refs[4], refs[5:9], refs[9:13]
    outs, out_field, delta, halo, grads = refs[13:17], refs[17:21], refs[21:25], *refs[25:27]
    rooms, strips, long = refs[27:33], refs[33], refs[34]
    half, depth = blocks[0].shape[:2]
    take_strips(found, received, halo)
    terms = halo_terms(halo_windows(halo, long), weight)
    edges = add_strips(load_edges(*blocks), terms, rooms)
    cots = []
    for ref, at in ((wanted[0], 0), (wanted[1], 16 - depth)):
        block = ref[...].astype(f32)
        block = block.reshape((half, 2) + block.shape[1:])[:, :, at : at + depth, :]
        cots.append(jnp.concatenate([block[:, 0], block[:, 1]], axis=-1))
    cots += [wanted[2][0].astype(f32), wanted[3][0].astype(f32)]
    both = [gelu_both(edge) for edge in edges]
    deltas = exact([cot * rate for cot, (_, rate) in zip(cots, both)])
    for k in range(4):
        out_field[k][...] = both[k][0]
        delta[k][...] = deltas[k]
    edge_strips(deltas, strips)
    halo_grads(strips, weight, long, grads)
    send_strips(found, grads, outs)


def second_back(*refs):
    bulk_delta, delta_edges, halo = refs[0], refs[1:5], refs[5]
    shifted, weight, bulk_slope = refs[6:9]
    grad_weight, grad_hidden, delta_first = refs[9:12]
    pairs, delta, lower, upper, moved, strips, long = refs[12:19]
    count = pairs.shape[0]
    pairs[...] = bulk_delta[...].astype(f32)
    lay_edges(pairs, *delta_edges)
    delta[...] = pairs[...].astype(bf16)
    bulk_weight_grad(shifted, delta, grad_weight)
    edge_strips([ref[...] for ref in delta_edges], strips)
    halo_weight_grad(halo_windows(halo, long), strips, grad_weight)
    fill_columns(moved, pairs)
    bulk_conv(moved, weight, lower, upper, grad_hidden, True)
    for i in range(count):
        delta_first[i] = (grad_hidden[i] * bulk_slope[i].astype(f32)).astype(bf16)


def first_grads(found, *refs):
    blocks, slope, bulk_delta, halo, shifted, other_grad = refs[:4], refs[4:8], *refs[8:12]
    own, near, carried, grads = refs[12], refs[13:17], refs[17:21], refs[21]
    delta, kept, given = refs[22:25]
    pairs, strips, long, grad_weight, room = refs[25:30]
    edges = [edge * rate[...] for edge, rate in zip(load_edges(*blocks), slope)]
    pairs[...] = bulk_delta[...].astype(f32)
    lay_edges(pairs, *edges)
    delta[...] = pairs[...].astype(bf16)
    bulk_weight_grad(shifted, delta, grad_weight)
    edge_strips(edges, strips)
    halo_weight_grad(halo_windows(halo, long), strips, grad_weight)
    rim_weight_grad(found, own, near, carried, grads, room, grad_weight)
    core = lax.axis_index("tile") & 1
    for tap in range(grad_weight.shape[0]):
        one, two = grad_weight[tap], other_grad[tap]
        kept[tap] = jnp.where(core == 0, one, two)
        given[tap] = jnp.where(core == 0, two, one).astype(bf16)


def first_back(found, *refs):
    received, weight, blocks, slope = refs[:4], refs[4], refs[5:9], refs[9:13]
    outs, delta = refs[13:17], refs[17:21]
    rooms, strips, long, grads, back = refs[21:27], *refs[27:31]
    take_strips(found, received, back, True)
    edges = add_strips(load_edges(*blocks), [back[s] for s in range(4)], rooms)
    deltas = exact([edge * rate[...] for edge, rate in zip(edges, slope)])
    for k in range(4):
        delta[k][...] = deltas[k]
    edge_strips(deltas, strips)
    halo_grads(strips, weight, long, grads)
    send_strips(found, grads, outs)


def last_bulk(delta, weight, bulk_out, *refs):
    delta_edges, out_edges, interior, out_field = refs[:4], refs[4:8], *refs[8:10]
    pairs, moved, lower, upper = refs[10:14]
    count, size, lanes = pairs.shape
    c = lanes // 2
    pairs[...] = bulk_out[...].astype(f32)
    lay_edges(pairs, *out_edges)
    for i in range(count):
        out_field[2 * i] = pairs[i, :, 0:c].astype(bf16)
        out_field[2 * i + 1] = pairs[i, :, c:].astype(bf16)
    pairs[...] = delta[...].astype(f32)
    lay_edges(pairs, *delta_edges)
    fill_columns(moved, pairs)
    bulk_conv(moved, weight, lower, upper, interior, True)


def last_edges(found, *refs):
    received, interior, grad = refs[:4], refs[4], refs[5]
    rooms, back, pairs = refs[6:12], refs[12], refs[13]
    count, size, lanes = interior.shape
    c = lanes // 2
    take_strips(found, received, back, True)
    edges = (
        interior[:, 0:8, :],
        interior[:, size - 8 :, :],
        interior[0, :, 0:c],
        interior[count - 1, :, c:],
    )
    edges = add_strips(edges, [back[s] for s in range(4)], rooms)
    pairs[...] = interior[...]
    lay_edges(pairs, *edges)
    for i in range(count):
        grad[2 * i] = pairs[i, :, 0:c].astype(bf16)
        grad[2 * i + 1] = pairs[i, :, c:].astype(bf16)


def call(kernel, name, ins, outs, scratch, cost=0, room=16 << 20):
    whole = pl.BlockSpec(memory_space=pltpu.VMEM)
    return pl.pallas_call(
        kernel,
        name=name,
        grid=(1,),
        in_specs=[spec or whole for _, spec in ins],
        out_specs=[whole] * len(outs),
        out_shape=outs,
        scratch_shapes=scratch,
        compiler_params=pltpu.CompilerParams(vmem_limit_bytes=room),
        cost_estimate=pl.CostEstimate(flops=cost, bytes_accessed=2 << 20, transcendentals=0),
    )(*[array for array, _ in ins])


def flip_swap(block, mask_ens, mask_tile):
    ens, tile = lax.axis_size("ens"), lax.axis_size("tile")
    route = [
        (e * tile + t, (e ^ mask_ens) * tile + (t ^ mask_tile))
        for e in range(ens)
        for t in range(tile)
    ]
    return lax.ppermute(block, ("ens", "tile"), route)


def seat_of():
    return lax.axis_index("tile") >> 2 & 3


def share_out(loads, kept, given, *refs):
    riders, own, sent = refs[: sum(loads)], refs[sum(loads)], refs[sum(loads) + 1 :]
    rows = own.shape[0]
    seat = seat_of()
    quarter = lambda at: pl.ds(pl.multiple_of(at * rows, rows), rows)
    add = lambda at: kept[quarter(at), :] + given[quarter(at), :].astype(f32)
    own[...] = add(seat)
    taken = 0
    for k, block in enumerate(sent):
        block[0:rows] = add(seat ^ (3 - k)).astype(bf16)
        if loads[k]:
            block[rows:] = riders[taken][...]
            taken += 1


def add_up(count, loads, base, *refs):
    got, riders, total = refs[:count], refs[count : count + loads], refs[count + loads]
    loaded = refs[count + loads + 1 :]
    rows = base.shape[0]
    terms = [base[...].astype(f32)] + [block[0:rows].astype(f32) for block in got]
    while len(terms) > 1:
        terms = [terms[i] + terms[i + 1] for i in range(0, len(terms), 2)]
    total[...] = terms[0].astype(bf16)
    for block, rider in zip(loaded, riders):
        block[0:rows] = terms[0].astype(bf16)
        block[rows:] = rider[...]


def line_masks():
    return [12, 8, 4]


def aboard(ways):
    tiles = lax.axis_size("tile")
    line = [tuple(t ^ mask for t in range(tiles)) for mask in line_masks()]
    return [ways.index(way) if way in ways else None for way in line]


def swap_line(blocks, riders, ways):
    riding = aboard(ways)
    got = [flip_swap(block, 0, mask) for block, mask in zip(blocks, line_masks())]
    came = [
        got[riding.index(k)] if k in riding else lax.ppermute(rider, "tile", list(enumerate(way)))
        for k, (rider, way) in enumerate(zip(riders, ways))
    ]
    return got, came


def scatter_line(kept, given, riders, ways):
    rows, lanes = kept.shape[0] // 4, kept.shape[1]
    S = jax.ShapeDtypeStruct
    given, riders = lax.optimization_barrier((flip_swap(given, 0, 1), riders))
    loads = [k is not None for k in aboard(ways)]
    taken = [riders[k] for k in aboard(ways) if k is not None]
    own, *sent = call(
        functools.partial(share_out, loads),
        "share_out",
        [(block, None) for block in (kept, given, *taken)],
        [S((rows, lanes), f32)]
        + [S((rows + load * riders[0].shape[0], lanes), bf16) for load in loads],
        [],
    )
    got, came = swap_line(sent, riders, ways)
    return own, got, came


def sum_rest(own, got, riders, ways):
    tiles = lax.axis_size("tile")
    groups, bit = [[(1, 2), (1, 0), (0, 2)]], 16
    while bit < tiles:
        groups.append([(0, 3 * bit), (0, 2 * bit), (0, bit)] if 2 * bit < tiles else [(0, bit)])
        bit *= 4
    S = jax.ShapeDtypeStruct
    riding = aboard(ways)
    for masks in groups + [None]:
        taken = [riders[k] for k in riding if k is not None] if masks is None else []
        own, *loaded = call(
            functools.partial(add_up, len(got), len(taken)),
            "add_up",
            [(block, None) for block in (own, *got, *taken)],
            [S(own.shape, bf16)]
            + [S((own.shape[0] + rider.shape[0], own.shape[1]), bf16) for rider in taken],
            [],
        )
        if masks is not None:
            got = [flip_swap(own, *mask) for mask in masks]
    return own, [own if k is None else loaded.pop(0) for k in riding]


def stack(*refs):
    rows = refs[0].shape[0]
    for k in range(4):
        refs[4][k] = refs[k][0:rows]


def both_grads(mine, others, first, second):
    rows = mine.shape[1]
    core, seat = lax.axis_index("tile") & 1, seat_of()
    for k in range(4):
        place = pl.ds(pl.multiple_of((seat ^ k) * rows, rows), rows)
        one, two = mine[k].astype(f32), others[k].astype(f32)
        first[place, :] = jnp.where(core == 0, one, two)
        second[place, :] = jnp.where(core == 0, two, one)


def local(fields, weight_first, weight_second, neighbours, cotangent):
    block, wanted = fields[0, 0], cotangent[0, 0]
    size, c = block.shape[0], block.shape[-1]
    half = size // 2
    count = lax.axis_size("tile")
    cols = max(4, count // 8)
    shape = weight_first.shape
    one, two = weight_first.reshape(9, c, c), weight_second.reshape(9, c, c)
    flops = 2 * size * size * 9 * c * c

    S = jax.ShapeDtypeStruct
    sent = [S((size, c), bf16)] * 4
    halo = S((4, size, c), f32)
    edge = [S((half, 8, 2 * c), f32)] * 2 + [S((size, c), f32)] * 2
    pairs = lambda kind: S((half, size, 2 * c), kind)
    shifted = S(((half + 1) * size, 6 * c), bf16)
    V = lambda leaf: pltpu.VMEM(leaf.shape, leaf.dtype)
    ahead = [pltpu.VMEM((6 * c, 2 * c), bf16)] * 2
    back = [pltpu.VMEM((2 * c, 6 * c), bf16)] * 2
    rooms = [V(leaf) for leaf in edge] + [pltpu.VMEM((size, c), f32)] * 2
    long = pltpu.VMEM((4, size + 16, c), f32)
    whole = lambda arrays: [(array, None) for array in arrays]

    def edge_blocks(array):
        last = size // 8 - 1
        return [
            (array, pl.BlockSpec((half, 8, 2 * c), lambda step: (0, 0, 0))),
            (array, pl.BlockSpec((half, 8, 2 * c), lambda step: (0, last, 0))),
            (array, pl.BlockSpec((1, size, c), lambda step: (0, 0, 0))),
            (array, pl.BlockSpec((1, size, c), lambda step: (half - 1, 0, 1))),
        ]

    def image_edges(array):
        last = size // 16 - 1
        return [
            (array, pl.BlockSpec((size, 16, c), lambda step: (0, 0, 0))),
            (array, pl.BlockSpec((size, 16, c), lambda step: (0, last, 0))),
            (array, pl.BlockSpec((1, size, c), lambda step: (0, 0, 0))),
            (array, pl.BlockSpec((1, size, c), lambda step: (size - 1, 0, 0))),
        ]

    wide = pltpu.VMEM((4, size, 2 * c), f32)
    far = pl.BlockSpec(memory_space=pl.ANY)
    stay = lambda array: (pltpu.with_memory_space_constraint(array, pltpu.HBM), far)
    *strips, found, block, one, own = call(
        functools.partial(first_strips, cols),
        "first_strips",
        [stay(neighbours.T), stay(block), stay(one)],
        [S((2 * size, c), bf16)] * 4
        + [S((12, 8, 128), jnp.int32), S(block.shape, bf16), S(one.shape, bf16), halo],
        [wide, pltpu.VMEM((2, size, 16, c), bf16), pltpu.VMEM((2, 2, size, c), bf16)]
        + [pltpu.SMEM(neighbours.shape[::-1], jnp.int32), pltpu.SemaphoreType.DMA((7,))],
    )
    links = (found, None)
    near = swap_all(strips, cols)
    shifted_one, pre_one, hidden, slope = call(
        first_bulk,
        "first_bulk",
        whole([block, one]),
        [shifted, pairs(f32), pairs(bf16), pairs(bf16)],
        [V(pairs(bf16))] + ahead,
        flops,
    )
    found = call(
        first_edges,
        "first_edges",
        [links] + whole(near) + [(one, None)] + edge_blocks(pre_one),
        [S((2 * size + 16, c), bf16)] * 4 + edge + edge + [halo],
        rooms + [wide, long, pltpu.VMEM((4, 2, 16, c), f32), V(halo)],
    )
    strips, hidden_edges, slope_edges, halo_one = found[:4], found[4:8], found[8:12], found[12]
    carried = swap_all(strips, cols)
    shifted_two, pre_two, out_bulk, delta_bulk = call(
        second_bulk,
        "second_bulk",
        whole([hidden, *hidden_edges, two, wanted]),
        [shifted, pairs(f32), pairs(bf16), pairs(bf16)],
        [V(pairs(f32))] + ahead,
        flops,
    )
    found = call(
        second_edges,
        "second_edges",
        [links] + whole(carried) + [(two, None)] + edge_blocks(pre_two) + image_edges(wanted),
        sent + edge + edge + [halo, halo],
        rooms + [V(halo), long],
    )
    strips, out_edges, delta_edges, halo_two, grads = found[:4], found[4:8], found[8:12], *found[12:]
    grad_two, grad_hidden, delta_one = call(
        second_back,
        "second_back",
        whole([delta_bulk, *delta_edges, halo_two, shifted_two, two, slope]),
        [S((9, c, c), f32), pairs(f32), pairs(bf16)],
        [V(pairs(f32)), V(pairs(bf16))] + back + [V(shifted), V(halo), long],
        2 * flops,
    )
    delta_one, kept, given = call(
        first_grads,
        "first_grads",
        [links]
        + edge_blocks(grad_hidden)
        + whole([*slope_edges, delta_one, halo_one, shifted_one, grad_two])
        + whole([own, *near, *carried, grads]),
        [pairs(bf16), S((9, c, c), f32), S((9, c, c), bf16)],
        [V(pairs(f32)), V(halo), long, pltpu.VMEM((9, c, c), f32)]
        + [pltpu.VMEM((3, size + 16, c), f32)],
        flops,
    )
    ways = routes(cols)
    quarter, got, strips = scatter_line(
        kept.reshape(9 * c, c), given.reshape(9 * c, c), strips, ways
    )
    found = call(
        first_back,
        "first_back",
        [links] + whole(strips) + [(one, None)] + edge_blocks(grad_hidden) + whole(slope_edges),
        sent + edge,
        rooms + [V(halo), long, V(halo), V(halo)],
    )
    strips, delta_edges = found[:4], found[4:8]
    interior, out_field = call(
        last_bulk,
        "last_bulk",
        whole([delta_one, one, out_bulk, *delta_edges, *out_edges]),
        [pairs(f32), S(block.shape, bf16)],
        [V(pairs(f32)), V(shifted)] + back,
        flops,
    )
    quarter, blocks = sum_rest(quarter, got, strips, ways)
    quarter, blocks, strips, interior = lax.optimization_barrier(
        (quarter, blocks, strips, interior)
    )
    got, strips = lax.optimization_barrier(swap_line(blocks, strips, ways))
    (grad_block,) = call(
        last_edges,
        "last_edges",
        [links] + whole([*strips, interior]),
        [S(block.shape, bf16)],
        rooms + [V(halo), V(pairs(f32))],
    )
    quarters = [quarter, *got[::-1]]
    (stacked,) = call(stack, "stack", whole(quarters), [S((4, *quarter.shape), bf16)], [])
    others, grad_block = lax.optimization_barrier((flip_swap(stacked, 0, 1), grad_block))
    grads = call(
        both_grads,
        "both_grads",
        whole([stacked, others]),
        [S((9 * c, c), f32)] * 2,
        [],
    )
    grad_first, grad_second = (grad.reshape(shape) for grad in grads)
    return (out_field[None, None], grad_block[None, None], grad_first, grad_second)


def solution(mesh):
    placed = (P("ens", "tile", None, None, None), P(), P(), P(), P("ens", "tile", None, None, None))
    return jax.shard_map(
        local,
        mesh=mesh,
        in_specs=placed,
        out_specs=(
            P("ens", "tile", None, None, None),
            P("ens", "tile", None, None, None),
            P(),
            P(),
        ),
        check_vma=False,
    )
```

```python
import functools

import jax
import jax.numpy as jnp
from jax import lax
from jax.experimental import pallas as pl
from jax.experimental.pallas import tpu as pltpu
from jax.sharding import PartitionSpec as P

root_half = 0.7071067811865476
inv_root_tau = 0.3989422804014327
bf16, f32 = jnp.bfloat16, jnp.float32
NT = (((1,), (1,)), ((), ()))
TN = (((0,), (0,)), ((), ()))


def gelu_both(pre):
    bell = 0.5 * (1.0 + lax.erf(pre * root_half))
    return pre * bell, bell + pre * jnp.exp(-0.5 * pre * pre) * inv_root_tau


def partners(index, count, cols):
    odd, row_odd = index & 1, (index // cols) & 1
    return [
        (index + cols * (2 * row_odd - 1) + count) % count,
        (index - 1 + 2 * odd + count) % count,
        (index + cols * (1 - 2 * row_odd) + count) % count,
        (index + 1 - 2 * odd + count) % count,
    ]


def write_links(table, cols, found):
    count = lax.axis_size("tile")
    me = lax.axis_index("tile")
    for k, other in enumerate(partners(me, count, cols)):
        side, back = jnp.int32(0), jnp.int32(0)
        for s in range(1, 4):
            side = jnp.where(table[s, me] == other, s, side)
            back = jnp.where(table[s, other] == me, s, back)
        turn = jnp.where((side >= 2) == (back >= 2), 1, 0)
        found[k] = jnp.full(found.shape[1:], side, jnp.int32)
        found[4 + k] = jnp.full(found.shape[1:], turn, jnp.int32)
        found[8 + k] = jnp.full(found.shape[1:], back, jnp.int32)


def masked(found, block):
    wide = jnp.concatenate([found] * (block.shape[-1] // found.shape[-1]), axis=1)
    return wide[None]


def choose(found, strips):
    _, size, c = strips.shape
    chosen = strips[0].reshape(size // 8, 8, c)
    for s in range(1, 4):
        here = masked(found, chosen) == s
        chosen = jnp.where(here, strips[s].reshape(chosen.shape), chosen)
    return chosen.reshape(size, c)


def send_strips(found, strips, outs):
    _, size, lanes = strips.shape
    c = outs[0].shape[-1]
    at_row = lax.broadcasted_iota(jnp.int32, (size, size), 0)
    at_col = lax.broadcasted_iota(jnp.int32, (size, size), 1)
    for k, out in enumerate(outs):
        turn = found[4 + k][0:1, 0:size] == 1
        order = (at_col == jnp.where(turn, size - 1 - at_row, at_row)).astype(f32).astype(bf16)
        chosen = choose(found[k], strips).astype(bf16)
        turned = jnp.dot(order, chosen, preferred_element_type=f32).astype(bf16)
        for part in range(lanes // c):
            out[part * size : (part + 1) * size] = turned[:, part * c : (part + 1) * c]


def take_strips(found, received, strips, last=False):
    _, size, c = strips.shape
    blocks = []
    for block in received:
        row = block.shape[0] - size if last else 0
        blocks.append(block[row : row + size].astype(f32).reshape(size // 8, 8, c))
    for s in range(4):
        taken = blocks[0]
        for k in range(1, 4):
            taken = jnp.where(found[k][None] == s, blocks[k], taken)
        strips[s] = taken.reshape(size, c)


def routes(cols):
    count = lax.axis_size("tile")
    return list(zip(*[partners(p, count, cols) for p in range(count)]))


def swap_all(blocks, cols):
    return [
        lax.ppermute(block, "tile", list(enumerate(way)))
        for block, way in zip(blocks, routes(cols))
    ]


def fill_columns(shifted, pairs):
    count, size, lanes = pairs.shape
    c = lanes // 2
    at = lax.broadcasted_iota(jnp.int32, (size, c), 0)
    first, last = at == 0, at == size - 1
    shifted[0:size, 0 : 3 * c] = jnp.zeros((size, 3 * c), bf16)
    shifted[count * size :, 3 * c :] = jnp.zeros((size, 3 * c), bf16)
    for i in range(count):
        for parity, row, lane in ((1, (i + 1) * size, 0), (0, i * size, 3 * c)):
            value = pairs[i, :, parity * c : (parity + 1) * c].astype(f32)
            before = jnp.where(first, 0.0, pltpu.roll(value, 1, 0))
            after = jnp.where(last, 0.0, pltpu.roll(value, size - 1, 0))
            shifted[row : row + size, lane : lane + c] = before.astype(bf16)
            shifted[row : row + size, lane + c : lane + 2 * c] = value.astype(bf16)
            shifted[row : row + size, lane + 2 * c : lane + 3 * c] = after.astype(bf16)


def blocks_of_pairs(tap, lower, upper, c):
    for b in range(3):
        for half, parity, target, a in (
            (lower, 0, 0, 0),
            (lower, 0, 1, None),
            (lower, 1, 0, 1),
            (lower, 1, 1, 0),
            (upper, 0, 0, 2),
            (upper, 0, 1, 1),
            (upper, 1, 0, None),
            (upper, 1, 1, 2),
        ):
            yield half, (parity * 3 + b) * c, target * c, tap(a, b) if a is not None else None


def bulk_conv(shifted, weight, lower, upper, out, backward):
    c = weight.shape[-1]
    count, size, lanes = out.shape
    if backward:
        tap = lambda a, b: weight[(2 - a) * 3 + 2 - b]
    else:
        tap = lambda a, b: weight[a * 3 + b]
    for half, depth, target, block in blocks_of_pairs(tap, lower, upper, c):
        if block is None:
            block = jnp.zeros((c, c), bf16)
        if backward:
            half[target : target + c, depth : depth + c] = block
        else:
            half[depth : depth + c, target : target + c] = block
    rows = count * size
    dims = NT if backward else (((1,), (0,)), ((), ()))
    total = lax.dot_general(
        shifted[0:rows, :], lower[...], dims, preferred_element_type=f32
    ) + lax.dot_general(shifted[size : size + rows, :], upper[...], dims, preferred_element_type=f32)
    out[...] = total.reshape(count, size, lanes)


def bulk_weight_grad(shifted, delta, out):
    count, size, lanes = delta.shape
    c = lanes // 2
    rows = count * size
    flat = delta[...].reshape(rows, lanes)
    low = lax.dot_general(shifted[0:rows, :], flat, TN, preferred_element_type=f32)
    high = lax.dot_general(shifted[size : size + rows, :], flat, TN, preferred_element_type=f32)
    for b in range(3):
        here, there = b * c, (3 + b) * c
        out[b] = low[here : here + c, 0:c] + low[there : there + c, c:]
        out[3 + b] = low[there : there + c, 0:c] + high[here : here + c, c:]
        out[6 + b] = high[here : here + c, 0:c] + high[there : there + c, c:]


def load_edges(left, right, top, bottom):
    return left[...], right[...], top[0], bottom[0]


def to_pairs(strip, room):
    room[...] = strip
    half = strip.shape[0] // 2
    return jnp.concatenate(
        [room[pl.ds(0, half, stride=2), :], room[pl.ds(1, half, stride=2), :]], axis=1
    )


def add_strips(edges, strips, rooms):
    left, right, top, bottom = edges
    t, r, b, l = strips
    c = t.shape[1]
    half, depth, size = left.shape[0], left.shape[1], t.shape[0]
    at = lax.broadcasted_iota(jnp.int32, left.shape, 1)
    left_room, right_room, top_room, bottom_room, strip_a, strip_b = rooms
    left_room[...] = left + jnp.where(at == 0, to_pairs(l, strip_a)[:, None, :], 0.0)
    right_room[...] = right + jnp.where(at == depth - 1, to_pairs(r, strip_b)[:, None, :], 0.0)
    left_room[0, :, 0:c] += t[0:depth]
    left_room[half - 1, :, c:] += b[0:depth]
    right_room[0, :, 0:c] += t[size - depth :]
    right_room[half - 1, :, c:] += b[size - depth :]
    top_room[...] = top + t
    bottom_room[...] = bottom + b
    top_room[0:depth] = left_room[0, :, 0:c]
    top_room[size - depth :] = right_room[0, :, 0:c]
    bottom_room[0:depth] = left_room[half - 1, :, c:]
    bottom_room[size - depth :] = right_room[half - 1, :, c:]
    return left_room[...], right_room[...], top_room[...], bottom_room[...]


def edge_strips(edges, strips):
    left, right, top, bottom = edges
    c = top.shape[1]
    half = left.shape[0]
    strips[0] = top
    strips[2] = bottom
    for side, column in ((1, right[:, -1, :]), (3, left[:, 0, :])):
        strips[side, pl.ds(0, half, stride=2), :] = column[:, 0:c]
        strips[side, pl.ds(1, half, stride=2), :] = column[:, c:]


def lay_edges(pairs, left, right, top, bottom):
    depth = left.shape[1]
    size = pairs.shape[1]
    c = top.shape[-1]
    pairs[:, 0:depth, :] = left[...]
    pairs[:, size - depth :, :] = right[...]
    pairs[0, :, 0:c] = top[...]
    pairs[pairs.shape[0] - 1, :, c:] = bottom[...]


def halo_windows(strips, rooms):
    size = strips.shape[1]
    top, right, bottom, left = (strips[s] for s in range(4))
    zero = jnp.zeros_like(top[0:1])
    ends = [
        (0.5 * (top[0:1] + left[0:1]), 0.5 * (top[size - 1 :] + right[0:1])),
        (zero, zero),
        (0.5 * (left[size - 1 :] + bottom[0:1]), 0.5 * (bottom[size - 1 :] + right[size - 1 :])),
        (zero, zero),
    ]
    windows = []
    for s, (strip, (before, after)) in enumerate(zip((top, right, bottom, left), ends)):
        rooms[s, 7:8, :] = before
        rooms[s, 8 : 8 + size, :] = strip
        rooms[s, 8 + size : 9 + size, :] = after
        windows.append(
            jnp.concatenate([rooms[s, 7 + k : 7 + k + size, :] for k in range(3)], axis=1).astype(
                bf16
            )
        )
    return windows


def rim_ends(strips, rooms, ends):
    size = strips.shape[1]
    last = size - 1
    ne, nw = rooms[0, 8 + size : 9 + size, :], rooms[0, 7:8, :]
    se, sw = rooms[2, 8 + size : 9 + size, :], rooms[2, 7:8, :]
    across = lambda at: (strips[3, at : at + 1, :], strips[1, at : at + 1, :])
    along = lambda at: (strips[0, at : at + 1, :], strips[2, at : at + 1, :])
    ends[...] = jnp.zeros_like(ends)
    for side, rows in enumerate(
        (
            ((nw, ne), across(0), across(1)),
            ((ne, se), along(last), along(last - 1)),
            ((sw, se), across(last), across(last - 1)),
            ((nw, sw), along(0), along(1)),
        )
    ):
        for depth, (before, after) in enumerate(rows):
            for turned, pair in enumerate(((before, after), (after, before))):
                ends[side, turned, 2 * depth : 2 * depth + 1, :] = pair[0]
                ends[side, turned, 2 * depth + 1 : 2 * depth + 2, :] = pair[1]


def rim_weight_grad(found, own, near, carried, grads, room, out):
    _, size, c = own.shape
    windows, deltas = [], []
    for k in range(4):
        ends = carried[k][2 * size :].astype(f32)
        rows = (
            choose(found[k], own),
            near[k][0:size].astype(f32),
            near[k][size : 2 * size].astype(f32),
        )
        for depth, row in enumerate(rows):
            room[depth, 7:8, :] = ends[2 * depth : 2 * depth + 1]
            room[depth, 8 : 8 + size, :] = row
            room[depth, 8 + size : 9 + size, :] = ends[2 * depth + 1 : 2 * depth + 2]
        part = [
            [room[d, 7 + b : 7 + b + size, :].reshape(size // 8, 8, c) for b in range(3)]
            for d in range(3)
        ]
        turned = found[4 + k][None] == 1
        back = found[8 + k][None]
        swap = lambda here, one, two: (jnp.where(here, two, one), jnp.where(here, one, two))
        for d in range(3):
            part[d][0], part[d][2] = swap(turned, part[d][0], part[d][2])
        for b in range(3):
            inward = (back == 1) | (back == 2)
            part[0][b], part[2][b] = swap(inward, part[0][b], part[2][b])
        for a, b in ((0, 1), (0, 2), (1, 2)):
            upright = (back & 1) == 1
            part[a][b], part[b][a] = swap(upright, part[a][b], part[b][a])
        windows.append(
            jnp.concatenate(
                [part[a][b].reshape(size, c).astype(bf16) for a in range(3) for b in range(3)],
                axis=1,
            )
        )
        delta = choose(found[k], grads).astype(bf16).astype(f32)
        deltas.append((delta * carried[k][size : 2 * size].astype(f32)).astype(bf16))
    term = lax.dot_general(
        jnp.concatenate(windows, axis=0),
        jnp.concatenate(deltas, axis=0),
        TN,
        preferred_element_type=f32,
    )
    for tap in range(9):
        out[tap] += term[tap * c : (tap + 1) * c]


side_taps = ((0, 1, 2), (2, 5, 8), (6, 7, 8), (0, 3, 6))


def halo_terms(windows, weight):
    return [
        jnp.dot(
            window,
            jnp.concatenate([weight[tap] for tap in taps], axis=0),
            preferred_element_type=f32,
        )
        for window, taps in zip(windows, side_taps)
    ]


def halo_weight_grad(windows, strips, out):
    c = out.shape[-1]
    for s, (window, taps) in enumerate(zip(windows, side_taps)):
        term = lax.dot_general(window, strips[s].astype(bf16), TN, preferred_element_type=f32)
        for k, tap in enumerate(taps):
            out[tap] += term[k * c : (k + 1) * c]


def halo_grads(strips, weight, rooms, grads):
    size, c = strips.shape[1:]
    long = size + 8
    for s, taps in enumerate(side_taps):
        rooms[s, 0:8, :] = jnp.zeros((8, c), f32)
        rooms[s, 8 : 8 + size, :] = strips[s]
        rooms[s, 8 + size :, :] = jnp.zeros((8, c), f32)
        copies = jnp.concatenate([rooms[s, 8 - k : 8 - k + long, :] for k in range(3)], axis=1)
        rims = jnp.concatenate([weight[tap] for tap in taps], axis=1)
        rim = lax.dot_general(copies.astype(bf16), rims, NT, preferred_element_type=f32)
        rooms[s, 0:long, :] = rim
        at = lax.broadcasted_iota(jnp.int32, (size, c), 0)
        corner = jnp.where(at == 0, rooms[s, 0:1, :], 0.0) + jnp.where(
            at == size - 1, rooms[s, size + 1 : size + 2, :], 0.0
        )
        grads[s] = rooms[s, 1 : 1 + size, :] + 0.5 * corner


def exact(values):
    return [value.astype(bf16).astype(f32) for value in values]


def first_strips(cols, table, block, weight, *refs):
    outs, found, held, held_weight, own = refs[:4], *refs[4:8]
    strips, columns, rows, near, arrived = refs[8:13]
    size, c = own.shape[1:]
    pairs = [
        (table, near),
        (block.at[pl.ds(0, 2)], rows.at[0]),
        (block.at[pl.ds(size - 2, 2)], rows.at[1]),
        (block.at[:, pl.ds(0, 16), :], columns.at[0]),
        (block.at[:, pl.ds(size - 16, 16), :], columns.at[1]),
        (block, held),
        (weight, held_weight),
    ]
    copies = [
        pltpu.make_async_copy(source, target, arrived.at[k])
        for k, (source, target) in enumerate(pairs)
    ]
    for copy in copies:
        copy.start()
    copies[0].wait()
    write_links(near, cols, found)
    for copy in copies[1:5]:
        copy.wait()
    left, right = columns[0].astype(f32), columns[1].astype(f32)
    for side, edge, second in (
        (0, rows[0, 0].astype(f32), rows[0, 1].astype(f32)),
        (1, right[:, 15, :], right[:, 14, :]),
        (2, rows[1, 1].astype(f32), rows[1, 0].astype(f32)),
        (3, left[:, 0, :], left[:, 1, :]),
    ):
        own[side] = edge
        strips[side, :, 0:c] = edge
        strips[side, :, c:] = second
    send_strips(found, strips, outs)
    for copy in copies[5:]:
        copy.wait()


def first_bulk(block, weight, shifted, pre, hidden, slope, pairs, lower, upper):
    count, size, lanes = pre.shape
    c = lanes // 2
    for i in range(count):
        pairs[i, :, 0:c] = block[2 * i]
        pairs[i, :, c:] = block[2 * i + 1]
    fill_columns(shifted, pairs)
    bulk_conv(shifted, weight, lower, upper, pre, False)
    for i in range(count):
        value, rate = gelu_both(pre[i])
        hidden[i] = value.astype(bf16)
        slope[i] = rate.astype(bf16)


def first_edges(found, *refs):
    received, weight, blocks = refs[:4], refs[4], refs[5:9]
    outs, hidden, slope, halo = refs[9:13], refs[13:17], refs[17:21], refs[21]
    rooms, strips, long, ends, narrow = refs[22:28], *refs[28:32]
    size, c = halo.shape[1:]
    take_strips(found, received, halo)
    terms = halo_terms(halo_windows(halo, long), weight)
    edges = add_strips(load_edges(*blocks), terms, rooms)
    both = [gelu_both(edge) for edge in edges]
    values = exact([value for value, _ in both])
    for k in range(4):
        hidden[k][...] = values[k]
        slope[k][...] = both[k][1]
    for k, edges in enumerate((values, [rate for _, rate in both])):
        edge_strips(edges, narrow)
        strips[:, :, k * c : (k + 1) * c] = narrow[...]
    rim_ends(halo, long, ends)
    send_strips(found, strips, outs)
    for k, out in enumerate(outs):
        straight = choose(found[k], ends.at[:, 0])
        turned = choose(found[k], ends.at[:, 1])
        here = jnp.concatenate([found[4 + k]] * 2, axis=0) == 1
        out[2 * size :] = jnp.where(here, turned, straight).astype(bf16)


def second_bulk(hidden, left, right, top, bottom, weight, cotangent, *refs):
    shifted, pre, out_field, delta, pairs, lower, upper = refs
    count, size, lanes = pre.shape
    c = lanes // 2
    pairs[...] = hidden[...].astype(f32)
    lay_edges(pairs, left, right, top, bottom)
    fill_columns(shifted, pairs)
    bulk_conv(shifted, weight, lower, upper, pre, False)
    for i in range(count):
        for parity in range(2):
            part = slice(parity * c, (parity + 1) * c)
            value, rate = gelu_both(pre[i, :, part])
            out_field[i, :, part] = value.astype(bf16)
            delta[i, :, part] = (cotangent[2 * i + parity].astype(f32) * rate).astype(bf16)


def second_edges(found, *refs):
    received, weight, blocks, wanted = refs[:4], refs[4], refs[5:9], refs[9:13]
    outs, out_field, delta, halo, grads = refs[13:17], refs[17:21], refs[21:25], *refs[25:27]
    rooms, strips, long = refs[27:33], refs[33], refs[34]
    half, depth = blocks[0].shape[:2]
    take_strips(found, received, halo)
    terms = halo_terms(halo_windows(halo, long), weight)
    edges = add_strips(load_edges(*blocks), terms, rooms)
    cots = []
    for ref, at in ((wanted[0], 0), (wanted[1], 16 - depth)):
        block = ref[...].astype(f32)
        block = block.reshape((half, 2) + block.shape[1:])[:, :, at : at + depth, :]
        cots.append(jnp.concatenate([block[:, 0], block[:, 1]], axis=-1))
    cots += [wanted[2][0].astype(f32), wanted[3][0].astype(f32)]
    both = [gelu_both(edge) for edge in edges]
    deltas = exact([cot * rate for cot, (_, rate) in zip(cots, both)])
    for k in range(4):
        out_field[k][...] = both[k][0]
        delta[k][...] = deltas[k]
    edge_strips(deltas, strips)
    halo_grads(strips, weight, long, grads)
    send_strips(found, grads, outs)


def second_back(*refs):
    bulk_delta, delta_edges, halo = refs[0], refs[1:5], refs[5]
    shifted, weight, bulk_slope = refs[6:9]
    grad_weight, grad_hidden, delta_first = refs[9:12]
    pairs, delta, lower, upper, moved, strips, long = refs[12:19]
    count = pairs.shape[0]
    pairs[...] = bulk_delta[...].astype(f32)
    lay_edges(pairs, *delta_edges)
    delta[...] = pairs[...].astype(bf16)
    bulk_weight_grad(shifted, delta, grad_weight)
    edge_strips([ref[...] for ref in delta_edges], strips)
    halo_weight_grad(halo_windows(halo, long), strips, grad_weight)
    fill_columns(moved, pairs)
    bulk_conv(moved, weight, lower, upper, grad_hidden, True)
    for i in range(count):
        delta_first[i] = (grad_hidden[i] * bulk_slope[i].astype(f32)).astype(bf16)


def first_grads(found, *refs):
    blocks, slope, bulk_delta, halo, shifted, other_grad = refs[:4], refs[4:8], *refs[8:12]
    own, near, carried, grads = refs[12], refs[13:17], refs[17:21], refs[21]
    delta, kept, given = refs[22:25]
    pairs, strips, long, grad_weight, room = refs[25:30]
    edges = [edge * rate[...] for edge, rate in zip(load_edges(*blocks), slope)]
    pairs[...] = bulk_delta[...].astype(f32)
    lay_edges(pairs, *edges)
    delta[...] = pairs[...].astype(bf16)
    bulk_weight_grad(shifted, delta, grad_weight)
    edge_strips(edges, strips)
    halo_weight_grad(halo_windows(halo, long), strips, grad_weight)
    rim_weight_grad(found, own, near, carried, grads, room, grad_weight)
    core = lax.axis_index("tile") & 1
    for tap in range(grad_weight.shape[0]):
        one, two = grad_weight[tap], other_grad[tap]
        kept[tap] = jnp.where(core == 0, one, two)
        given[tap] = jnp.where(core == 0, two, one).astype(bf16)


def first_back(found, *refs):
    received, weight, blocks, slope = refs[:4], refs[4], refs[5:9], refs[9:13]
    outs, delta = refs[13:17], refs[17:21]
    rooms, strips, long, grads, back = refs[21:27], *refs[27:31]
    take_strips(found, received, back, True)
    edges = add_strips(load_edges(*blocks), [back[s] for s in range(4)], rooms)
    deltas = exact([edge * rate[...] for edge, rate in zip(edges, slope)])
    for k in range(4):
        delta[k][...] = deltas[k]
    edge_strips(deltas, strips)
    halo_grads(strips, weight, long, grads)
    send_strips(found, grads, outs)


def last_bulk(delta, weight, bulk_out, *refs):
    delta_edges, out_edges, interior, out_field = refs[:4], refs[4:8], *refs[8:10]
    pairs, moved, lower, upper = refs[10:14]
    count, size, lanes = pairs.shape
    c = lanes // 2
    pairs[...] = bulk_out[...].astype(f32)
    lay_edges(pairs, *out_edges)
    for i in range(count):
        out_field[2 * i] = pairs[i, :, 0:c].astype(bf16)
        out_field[2 * i + 1] = pairs[i, :, c:].astype(bf16)
    pairs[...] = delta[...].astype(f32)
    lay_edges(pairs, *delta_edges)
    fill_columns(moved, pairs)
    bulk_conv(moved, weight, lower, upper, interior, True)


def last_edges(found, *refs):
    received, interior, grad = refs[:4], refs[4], refs[5]
    rooms, back, pairs = refs[6:12], refs[12], refs[13]
    count, size, lanes = interior.shape
    c = lanes // 2
    take_strips(found, received, back, True)
    edges = (
        interior[:, 0:8, :],
        interior[:, size - 8 :, :],
        interior[0, :, 0:c],
        interior[count - 1, :, c:],
    )
    edges = add_strips(edges, [back[s] for s in range(4)], rooms)
    pairs[...] = interior[...]
    lay_edges(pairs, *edges)
    for i in range(count):
        grad[2 * i] = pairs[i, :, 0:c].astype(bf16)
        grad[2 * i + 1] = pairs[i, :, c:].astype(bf16)


def call(kernel, name, ins, outs, scratch, cost=0, room=16 << 20):
    whole = pl.BlockSpec(memory_space=pltpu.VMEM)
    return pl.pallas_call(
        kernel,
        name=name,
        grid=(1,),
        in_specs=[spec or whole for _, spec in ins],
        out_specs=[whole] * len(outs),
        out_shape=outs,
        scratch_shapes=scratch,
        compiler_params=pltpu.CompilerParams(vmem_limit_bytes=room),
        cost_estimate=pl.CostEstimate(flops=cost, bytes_accessed=2 << 20, transcendentals=0),
    )(*[array for array, _ in ins])


def flip_swap(block, mask_ens, mask_tile):
    ens, tile = lax.axis_size("ens"), lax.axis_size("tile")
    route = [
        (e * tile + t, (e ^ mask_ens) * tile + (t ^ mask_tile))
        for e in range(ens)
        for t in range(tile)
    ]
    return lax.ppermute(block, ("ens", "tile"), route)


def seat_of():
    return lax.axis_index("tile") >> 2 & 3


def share_out(loads, kept, given, *refs):
    riders, own, sent = refs[: sum(loads)], refs[sum(loads)], refs[sum(loads) + 1 :]
    rows = own.shape[0]
    seat = seat_of()
    quarter = lambda at: pl.ds(pl.multiple_of(at * rows, rows), rows)
    add = lambda at: kept[quarter(at), :] + given[quarter(at), :].astype(f32)
    own[...] = add(seat)
    taken = 0
    for k, block in enumerate(sent):
        block[0:rows] = add(seat ^ (3 - k)).astype(bf16)
        if loads[k]:
            block[rows:] = riders[taken][...]
            taken += 1


def add_up(count, loads, base, *refs):
    got, riders, total = refs[:count], refs[count : count + loads], refs[count + loads]
    loaded = refs[count + loads + 1 :]
    rows = base.shape[0]
    terms = [base[...].astype(f32)] + [block[0:rows].astype(f32) for block in got]
    while len(terms) > 1:
        terms = [terms[i] + terms[i + 1] for i in range(0, len(terms), 2)]
    total[...] = terms[0].astype(bf16)
    for block, rider in zip(loaded, riders):
        block[0:rows] = terms[0].astype(bf16)
        block[rows:] = rider[...]


def line_masks():
    return [12, 8, 4]


def aboard(ways):
    tiles = lax.axis_size("tile")
    line = [tuple(t ^ mask for t in range(tiles)) for mask in line_masks()]
    return [ways.index(way) if way in ways else None for way in line]


def swap_line(blocks, riders, ways):
    riding = aboard(ways)
    got = [flip_swap(block, 0, mask) for block, mask in zip(blocks, line_masks())]
    came = [
        got[riding.index(k)] if k in riding else lax.ppermute(rider, "tile", list(enumerate(way)))
        for k, (rider, way) in enumerate(zip(riders, ways))
    ]
    return got, came


def scatter_line(kept, given, riders, ways):
    rows, lanes = kept.shape[0] // 4, kept.shape[1]
    S = jax.ShapeDtypeStruct
    given, riders = lax.optimization_barrier((flip_swap(given, 0, 1), riders))
    loads = [k is not None for k in aboard(ways)]
    taken = [riders[k] for k in aboard(ways) if k is not None]
    own, *sent = call(
        functools.partial(share_out, loads),
        "share_out",
        [(block, None) for block in (kept, given, *taken)],
        [S((rows, lanes), f32)]
        + [S((rows + load * riders[0].shape[0], lanes), bf16) for load in loads],
        [],
    )
    got, came = swap_line(sent, riders, ways)
    return own, got, came


def sum_rest(own, got, riders, ways):
    tiles = lax.axis_size("tile")
    groups, bit = [[(0, 2), (1, 0), (1, 2)]], 16
    while bit < tiles:
        groups.append([(0, 3 * bit), (0, 2 * bit), (0, bit)] if 2 * bit < tiles else [(0, bit)])
        bit *= 4
    S = jax.ShapeDtypeStruct
    riding = aboard(ways)
    for masks in groups + [None]:
        taken = [riders[k] for k in riding if k is not None] if masks is None else []
        own, *loaded = call(
            functools.partial(add_up, len(got), len(taken)),
            "add_up",
            [(block, None) for block in (own, *got, *taken)],
            [S(own.shape, bf16)]
            + [S((own.shape[0] + rider.shape[0], own.shape[1]), bf16) for rider in taken],
            [],
        )
        if masks is not None:
            got = [flip_swap(own, *mask) for mask in masks]
    return own, [own if k is None else loaded.pop(0) for k in riding]


def stack(*refs):
    rows = refs[0].shape[0]
    for k in range(4):
        refs[4][k] = refs[k][0:rows]


def both_grads(mine, others, first, second):
    rows = mine.shape[1]
    core, seat = lax.axis_index("tile") & 1, seat_of()
    for k in range(4):
        place = pl.ds(pl.multiple_of((seat ^ k) * rows, rows), rows)
        one, two = mine[k].astype(f32), others[k].astype(f32)
        first[place, :] = jnp.where(core == 0, one, two)
        second[place, :] = jnp.where(core == 0, two, one)


def local(fields, weight_first, weight_second, neighbours, cotangent):
    block, wanted = fields[0, 0], cotangent[0, 0]
    size, c = block.shape[0], block.shape[-1]
    half = size // 2
    count = lax.axis_size("tile")
    cols = max(4, count // 8)
    shape = weight_first.shape
    one, two = weight_first.reshape(9, c, c), weight_second.reshape(9, c, c)
    flops = 2 * size * size * 9 * c * c

    S = jax.ShapeDtypeStruct
    sent = [S((size, c), bf16)] * 4
    halo = S((4, size, c), f32)
    edge = [S((half, 8, 2 * c), f32)] * 2 + [S((size, c), f32)] * 2
    pairs = lambda kind: S((half, size, 2 * c), kind)
    shifted = S(((half + 1) * size, 6 * c), bf16)
    V = lambda leaf: pltpu.VMEM(leaf.shape, leaf.dtype)
    ahead = [pltpu.VMEM((6 * c, 2 * c), bf16)] * 2
    back = [pltpu.VMEM((2 * c, 6 * c), bf16)] * 2
    rooms = [V(leaf) for leaf in edge] + [pltpu.VMEM((size, c), f32)] * 2
    long = pltpu.VMEM((4, size + 16, c), f32)
    whole = lambda arrays: [(array, None) for array in arrays]

    def edge_blocks(array):
        last = size // 8 - 1
        return [
            (array, pl.BlockSpec((half, 8, 2 * c), lambda step: (0, 0, 0))),
            (array, pl.BlockSpec((half, 8, 2 * c), lambda step: (0, last, 0))),
            (array, pl.BlockSpec((1, size, c), lambda step: (0, 0, 0))),
            (array, pl.BlockSpec((1, size, c), lambda step: (half - 1, 0, 1))),
        ]

    def image_edges(array):
        last = size // 16 - 1
        return [
            (array, pl.BlockSpec((size, 16, c), lambda step: (0, 0, 0))),
            (array, pl.BlockSpec((size, 16, c), lambda step: (0, last, 0))),
            (array, pl.BlockSpec((1, size, c), lambda step: (0, 0, 0))),
            (array, pl.BlockSpec((1, size, c), lambda step: (size - 1, 0, 0))),
        ]

    wide = pltpu.VMEM((4, size, 2 * c), f32)
    far = pl.BlockSpec(memory_space=pl.ANY)
    stay = lambda array: (pltpu.with_memory_space_constraint(array, pltpu.HBM), far)
    *strips, found, block, one, own = call(
        functools.partial(first_strips, cols),
        "first_strips",
        [stay(neighbours.T), stay(block), stay(one)],
        [S((2 * size, c), bf16)] * 4
        + [S((12, 8, 128), jnp.int32), S(block.shape, bf16), S(one.shape, bf16), halo],
        [wide, pltpu.VMEM((2, size, 16, c), bf16), pltpu.VMEM((2, 2, size, c), bf16)]
        + [pltpu.SMEM(neighbours.shape[::-1], jnp.int32), pltpu.SemaphoreType.DMA((7,))],
    )
    links = (found, None)
    near = swap_all(strips, cols)
    shifted_one, pre_one, hidden, slope = call(
        first_bulk,
        "first_bulk",
        whole([block, one]),
        [shifted, pairs(f32), pairs(bf16), pairs(bf16)],
        [V(pairs(bf16))] + ahead,
        flops,
    )
    found = call(
        first_edges,
        "first_edges",
        [links] + whole(near) + [(one, None)] + edge_blocks(pre_one),
        [S((2 * size + 16, c), bf16)] * 4 + edge + edge + [halo],
        rooms + [wide, long, pltpu.VMEM((4, 2, 16, c), f32), V(halo)],
    )
    strips, hidden_edges, slope_edges, halo_one = found[:4], found[4:8], found[8:12], found[12]
    carried = swap_all(strips, cols)
    shifted_two, pre_two, out_bulk, delta_bulk = call(
        second_bulk,
        "second_bulk",
        whole([hidden, *hidden_edges, two, wanted]),
        [shifted, pairs(f32), pairs(bf16), pairs(bf16)],
        [V(pairs(f32))] + ahead,
        flops,
    )
    found = call(
        second_edges,
        "second_edges",
        [links] + whole(carried) + [(two, None)] + edge_blocks(pre_two) + image_edges(wanted),
        sent + edge + edge + [halo, halo],
        rooms + [V(halo), long],
    )
    strips, out_edges, delta_edges, halo_two, grads = found[:4], found[4:8], found[8:12], *found[12:]
    grad_two, grad_hidden, delta_one = call(
        second_back,
        "second_back",
        whole([delta_bulk, *delta_edges, halo_two, shifted_two, two, slope]),
        [S((9, c, c), f32), pairs(f32), pairs(bf16)],
        [V(pairs(f32)), V(pairs(bf16))] + back + [V(shifted), V(halo), long],
        2 * flops,
    )
    delta_one, kept, given = call(
        first_grads,
        "first_grads",
        [links]
        + edge_blocks(grad_hidden)
        + whole([*slope_edges, delta_one, halo_one, shifted_one, grad_two])
        + whole([own, *near, *carried, grads]),
        [pairs(bf16), S((9, c, c), f32), S((9, c, c), bf16)],
        [V(pairs(f32)), V(halo), long, pltpu.VMEM((9, c, c), f32)]
        + [pltpu.VMEM((3, size + 16, c), f32)],
        flops,
    )
    ways = routes(cols)
    quarter, got, strips = scatter_line(
        kept.reshape(9 * c, c), given.reshape(9 * c, c), strips, ways
    )
    found = call(
        first_back,
        "first_back",
        [links] + whole(strips) + [(one, None)] + edge_blocks(grad_hidden) + whole(slope_edges),
        sent + edge,
        rooms + [V(halo), long, V(halo), V(halo)],
    )
    strips, delta_edges = found[:4], found[4:8]
    interior, out_field = call(
        last_bulk,
        "last_bulk",
        whole([delta_one, one, out_bulk, *delta_edges, *out_edges]),
        [pairs(f32), S(block.shape, bf16)],
        [V(pairs(f32)), V(shifted)] + back,
        flops,
    )
    quarter, blocks = sum_rest(quarter, got, strips, ways)
    quarter, blocks, strips, interior = lax.optimization_barrier(
        (quarter, blocks, strips, interior)
    )
    got, strips = lax.optimization_barrier(swap_line(blocks, strips, ways))
    (grad_block,) = call(
        last_edges,
        "last_edges",
        [links] + whole([*strips, interior]),
        [S(block.shape, bf16)],
        rooms + [V(halo), V(pairs(f32))],
    )
    quarters = [quarter, *got[::-1]]
    (stacked,) = call(stack, "stack", whole(quarters), [S((4, *quarter.shape), bf16)], [])
    others, grad_block = lax.optimization_barrier((flip_swap(stacked, 0, 1), grad_block))
    grads = call(
        both_grads,
        "both_grads",
        whole([stacked, others]),
        [S((9 * c, c), f32)] * 2,
        [],
    )
    grad_first, grad_second = (grad.reshape(shape) for grad in grads)
    return (out_field[None, None], grad_block[None, None], grad_first, grad_second)


def solution(mesh):
    placed = (P("ens", "tile", None, None, None), P(), P(), P(), P("ens", "tile", None, None, None))
    return jax.shard_map(
        local,
        mesh=mesh,
        in_specs=placed,
        out_specs=(
            P("ens", "tile", None, None, None),
            P("ens", "tile", None, None, None),
            P(),
            P(),
        ),
        check_vma=False,
    )
```

```python
import functools

import jax
import jax.numpy as jnp
from jax import lax
from jax.experimental import pallas as pl
from jax.experimental.pallas import tpu as pltpu
from jax.sharding import PartitionSpec as P

root_half = 0.7071067811865476
inv_root_tau = 0.3989422804014327
bf16, f32 = jnp.bfloat16, jnp.float32
NT = (((1,), (1,)), ((), ()))
TN = (((0,), (0,)), ((), ()))


def gelu_both(pre):
    bell = 0.5 * (1.0 + lax.erf(pre * root_half))
    return pre * bell, bell + pre * jnp.exp(-0.5 * pre * pre) * inv_root_tau


def partners(index, count, cols):
    odd, row_odd = index & 1, (index // cols) & 1
    return [
        (index + cols * (2 * row_odd - 1) + count) % count,
        (index - 1 + 2 * odd + count) % count,
        (index + cols * (1 - 2 * row_odd) + count) % count,
        (index + 1 - 2 * odd + count) % count,
    ]


def write_links(table, cols, found):
    count = lax.axis_size("tile")
    me = lax.axis_index("tile")
    for k, other in enumerate(partners(me, count, cols)):
        side, back = jnp.int32(0), jnp.int32(0)
        for s in range(1, 4):
            side = jnp.where(table[s, me] == other, s, side)
            back = jnp.where(table[s, other] == me, s, back)
        turn = jnp.where((side >= 2) == (back >= 2), 1, 0)
        found[k] = jnp.full(found.shape[1:], side, jnp.int32)
        found[4 + k] = jnp.full(found.shape[1:], turn, jnp.int32)
        found[8 + k] = jnp.full(found.shape[1:], back, jnp.int32)


def masked(found, block):
    wide = jnp.concatenate([found] * (block.shape[-1] // found.shape[-1]), axis=1)
    return wide[None]


def choose(found, strips):
    _, size, c = strips.shape
    chosen = strips[0].reshape(size // 8, 8, c)
    for s in range(1, 4):
        here = masked(found, chosen) == s
        chosen = jnp.where(here, strips[s].reshape(chosen.shape), chosen)
    return chosen.reshape(size, c)


def send_strips(found, strips, outs):
    _, size, lanes = strips.shape
    c = outs[0].shape[-1]
    at_row = lax.broadcasted_iota(jnp.int32, (size, size), 0)
    at_col = lax.broadcasted_iota(jnp.int32, (size, size), 1)
    for k, out in enumerate(outs):
        turn = found[4 + k][0:1, 0:size] == 1
        order = (at_col == jnp.where(turn, size - 1 - at_row, at_row)).astype(f32).astype(bf16)
        chosen = choose(found[k], strips).astype(bf16)
        turned = jnp.dot(order, chosen, preferred_element_type=f32).astype(bf16)
        for part in range(lanes // c):
            out[part * size : (part + 1) * size] = turned[:, part * c : (part + 1) * c]


def take_strips(found, received, strips, last=False):
    _, size, c = strips.shape
    blocks = []
    for block in received:
        row = block.shape[0] - size if last else 0
        blocks.append(block[row : row + size].astype(f32).reshape(size // 8, 8, c))
    for s in range(4):
        taken = blocks[0]
        for k in range(1, 4):
            taken = jnp.where(found[k][None] == s, blocks[k], taken)
        strips[s] = taken.reshape(size, c)


def routes(cols):
    count = lax.axis_size("tile")
    return list(zip(*[partners(p, count, cols) for p in range(count)]))


def swap_all(blocks, cols):
    return [
        lax.ppermute(block, "tile", list(enumerate(way)))
        for block, way in zip(blocks, routes(cols))
    ]


def fill_columns(shifted, pairs):
    count, size, lanes = pairs.shape
    c = lanes // 2
    at = lax.broadcasted_iota(jnp.int32, (size, c), 0)
    first, last = at == 0, at == size - 1
    shifted[0:size, 0 : 3 * c] = jnp.zeros((size, 3 * c), bf16)
    shifted[count * size :, 3 * c :] = jnp.zeros((size, 3 * c), bf16)
    for i in range(count):
        for parity, row, lane in ((1, (i + 1) * size, 0), (0, i * size, 3 * c)):
            value = pairs[i, :, parity * c : (parity + 1) * c].astype(f32)
            before = jnp.where(first, 0.0, pltpu.roll(value, 1, 0))
            after = jnp.where(last, 0.0, pltpu.roll(value, size - 1, 0))
            shifted[row : row + size, lane : lane + c] = before.astype(bf16)
            shifted[row : row + size, lane + c : lane + 2 * c] = value.astype(bf16)
            shifted[row : row + size, lane + 2 * c : lane + 3 * c] = after.astype(bf16)


def blocks_of_pairs(tap, lower, upper, c):
    for b in range(3):
        for half, parity, target, a in (
            (lower, 0, 0, 0),
            (lower, 0, 1, None),
            (lower, 1, 0, 1),
            (lower, 1, 1, 0),
            (upper, 0, 0, 2),
            (upper, 0, 1, 1),
            (upper, 1, 0, None),
            (upper, 1, 1, 2),
        ):
            yield half, (parity * 3 + b) * c, target * c, tap(a, b) if a is not None else None


def bulk_conv(shifted, weight, lower, upper, out, backward):
    c = weight.shape[-1]
    count, size, lanes = out.shape
    if backward:
        tap = lambda a, b: weight[(2 - a) * 3 + 2 - b]
    else:
        tap = lambda a, b: weight[a * 3 + b]
    for half, depth, target, block in blocks_of_pairs(tap, lower, upper, c):
        if block is None:
            block = jnp.zeros((c, c), bf16)
        if backward:
            half[target : target + c, depth : depth + c] = block
        else:
            half[depth : depth + c, target : target + c] = block
    rows = count * size
    dims = NT if backward else (((1,), (0,)), ((), ()))
    total = lax.dot_general(
        shifted[0:rows, :], lower[...], dims, preferred_element_type=f32
    ) + lax.dot_general(shifted[size : size + rows, :], upper[...], dims, preferred_element_type=f32)
    out[...] = total.reshape(count, size, lanes)


def bulk_weight_grad(shifted, delta, out):
    count, size, lanes = delta.shape
    c = lanes // 2
    rows = count * size
    flat = delta[...].reshape(rows, lanes)
    low = lax.dot_general(shifted[0:rows, :], flat, TN, preferred_element_type=f32)
    high = lax.dot_general(shifted[size : size + rows, :], flat, TN, preferred_element_type=f32)
    for b in range(3):
        here, there = b * c, (3 + b) * c
        out[b] = low[here : here + c, 0:c] + low[there : there + c, c:]
        out[3 + b] = low[there : there + c, 0:c] + high[here : here + c, c:]
        out[6 + b] = high[here : here + c, 0:c] + high[there : there + c, c:]


def load_edges(left, right, top, bottom):
    return left[...], right[...], top[0], bottom[0]


def to_pairs(strip, room):
    room[...] = strip
    half = strip.shape[0] // 2
    return jnp.concatenate(
        [room[pl.ds(0, half, stride=2), :], room[pl.ds(1, half, stride=2), :]], axis=1
    )


def add_strips(edges, strips, rooms):
    left, right, top, bottom = edges
    t, r, b, l = strips
    c = t.shape[1]
    half, depth, size = left.shape[0], left.shape[1], t.shape[0]
    at = lax.broadcasted_iota(jnp.int32, left.shape, 1)
    left_room, right_room, top_room, bottom_room, strip_a, strip_b = rooms
    left_room[...] = left + jnp.where(at == 0, to_pairs(l, strip_a)[:, None, :], 0.0)
    right_room[...] = right + jnp.where(at == depth - 1, to_pairs(r, strip_b)[:, None, :], 0.0)
    left_room[0, :, 0:c] += t[0:depth]
    left_room[half - 1, :, c:] += b[0:depth]
    right_room[0, :, 0:c] += t[size - depth :]
    right_room[half - 1, :, c:] += b[size - depth :]
    top_room[...] = top + t
    bottom_room[...] = bottom + b
    top_room[0:depth] = left_room[0, :, 0:c]
    top_room[size - depth :] = right_room[0, :, 0:c]
    bottom_room[0:depth] = left_room[half - 1, :, c:]
    bottom_room[size - depth :] = right_room[half - 1, :, c:]
    return left_room[...], right_room[...], top_room[...], bottom_room[...]


def edge_strips(edges, strips):
    left, right, top, bottom = edges
    c = top.shape[1]
    half = left.shape[0]
    strips[0] = top
    strips[2] = bottom
    for side, column in ((1, right[:, -1, :]), (3, left[:, 0, :])):
        strips[side, pl.ds(0, half, stride=2), :] = column[:, 0:c]
        strips[side, pl.ds(1, half, stride=2), :] = column[:, c:]


def lay_edges(pairs, left, right, top, bottom):
    depth = left.shape[1]
    size = pairs.shape[1]
    c = top.shape[-1]
    pairs[:, 0:depth, :] = left[...]
    pairs[:, size - depth :, :] = right[...]
    pairs[0, :, 0:c] = top[...]
    pairs[pairs.shape[0] - 1, :, c:] = bottom[...]


def halo_windows(strips, rooms):
    size = strips.shape[1]
    top, right, bottom, left = (strips[s] for s in range(4))
    zero = jnp.zeros_like(top[0:1])
    ends = [
        (0.5 * (top[0:1] + left[0:1]), 0.5 * (top[size - 1 :] + right[0:1])),
        (zero, zero),
        (0.5 * (left[size - 1 :] + bottom[0:1]), 0.5 * (bottom[size - 1 :] + right[size - 1 :])),
        (zero, zero),
    ]
    windows = []
    for s, (strip, (before, after)) in enumerate(zip((top, right, bottom, left), ends)):
        rooms[s, 7:8, :] = before
        rooms[s, 8 : 8 + size, :] = strip
        rooms[s, 8 + size : 9 + size, :] = after
        windows.append(
            jnp.concatenate([rooms[s, 7 + k : 7 + k + size, :] for k in range(3)], axis=1).astype(
                bf16
            )
        )
    return windows


def rim_ends(strips, rooms, ends):
    size = strips.shape[1]
    last = size - 1
    ne, nw = rooms[0, 8 + size : 9 + size, :], rooms[0, 7:8, :]
    se, sw = rooms[2, 8 + size : 9 + size, :], rooms[2, 7:8, :]
    across = lambda at: (strips[3, at : at + 1, :], strips[1, at : at + 1, :])
    along = lambda at: (strips[0, at : at + 1, :], strips[2, at : at + 1, :])
    ends[...] = jnp.zeros_like(ends)
    for side, rows in enumerate(
        (
            ((nw, ne), across(0), across(1)),
            ((ne, se), along(last), along(last - 1)),
            ((sw, se), across(last), across(last - 1)),
            ((nw, sw), along(0), along(1)),
        )
    ):
        for depth, (before, after) in enumerate(rows):
            for turned, pair in enumerate(((before, after), (after, before))):
                ends[side, turned, 2 * depth : 2 * depth + 1, :] = pair[0]
                ends[side, turned, 2 * depth + 1 : 2 * depth + 2, :] = pair[1]


def rim_weight_grad(found, own, near, carried, grads, room, out):
    _, size, c = own.shape
    windows, deltas = [], []
    for k in range(4):
        ends = carried[k][2 * size :].astype(f32)
        rows = (
            choose(found[k], own),
            near[k][0:size].astype(f32),
            near[k][size : 2 * size].astype(f32),
        )
        for depth, row in enumerate(rows):
            room[depth, 7:8, :] = ends[2 * depth : 2 * depth + 1]
            room[depth, 8 : 8 + size, :] = row
            room[depth, 8 + size : 9 + size, :] = ends[2 * depth + 1 : 2 * depth + 2]
        part = [
            [room[d, 7 + b : 7 + b + size, :].reshape(size // 8, 8, c) for b in range(3)]
            for d in range(3)
        ]
        turned = found[4 + k][None] == 1
        back = found[8 + k][None]
        swap = lambda here, one, two: (jnp.where(here, two, one), jnp.where(here, one, two))
        for d in range(3):
            part[d][0], part[d][2] = swap(turned, part[d][0], part[d][2])
        for b in range(3):
            inward = (back == 1) | (back == 2)
            part[0][b], part[2][b] = swap(inward, part[0][b], part[2][b])
        for a, b in ((0, 1), (0, 2), (1, 2)):
            upright = (back & 1) == 1
            part[a][b], part[b][a] = swap(upright, part[a][b], part[b][a])
        windows.append(
            jnp.concatenate(
                [part[a][b].reshape(size, c).astype(bf16) for a in range(3) for b in range(3)],
                axis=1,
            )
        )
        delta = choose(found[k], grads).astype(bf16).astype(f32)
        deltas.append((delta * carried[k][size : 2 * size].astype(f32)).astype(bf16))
    term = lax.dot_general(
        jnp.concatenate(windows, axis=0),
        jnp.concatenate(deltas, axis=0),
        TN,
        preferred_element_type=f32,
    )
    for tap in range(9):
        out[tap] += term[tap * c : (tap + 1) * c]


side_taps = ((0, 1, 2), (2, 5, 8), (6, 7, 8), (0, 3, 6))


def halo_terms(windows, weight):
    return [
        jnp.dot(
            window,
            jnp.concatenate([weight[tap] for tap in taps], axis=0),
            preferred_element_type=f32,
        )
        for window, taps in zip(windows, side_taps)
    ]


def halo_weight_grad(windows, strips, out):
    c = out.shape[-1]
    for s, (window, taps) in enumerate(zip(windows, side_taps)):
        term = lax.dot_general(window, strips[s].astype(bf16), TN, preferred_element_type=f32)
        for k, tap in enumerate(taps):
            out[tap] += term[k * c : (k + 1) * c]


def halo_grads(strips, weight, rooms, grads):
    size, c = strips.shape[1:]
    long = size + 8
    for s, taps in enumerate(side_taps):
        rooms[s, 0:8, :] = jnp.zeros((8, c), f32)
        rooms[s, 8 : 8 + size, :] = strips[s]
        rooms[s, 8 + size :, :] = jnp.zeros((8, c), f32)
        copies = jnp.concatenate([rooms[s, 8 - k : 8 - k + long, :] for k in range(3)], axis=1)
        rims = jnp.concatenate([weight[tap] for tap in taps], axis=1)
        rim = lax.dot_general(copies.astype(bf16), rims, NT, preferred_element_type=f32)
        rooms[s, 0:long, :] = rim
        at = lax.broadcasted_iota(jnp.int32, (size, c), 0)
        corner = jnp.where(at == 0, rooms[s, 0:1, :], 0.0) + jnp.where(
            at == size - 1, rooms[s, size + 1 : size + 2, :], 0.0
        )
        grads[s] = rooms[s, 1 : 1 + size, :] + 0.5 * corner


def exact(values):
    return [value.astype(bf16).astype(f32) for value in values]


def first_strips(cols, table, block, weight, *refs):
    outs, found, held, held_weight, own = refs[:4], *refs[4:8]
    strips, columns, rows, near, arrived = refs[8:13]
    size, c = own.shape[1:]
    pairs = [
        (table, near),
        (block.at[pl.ds(0, 2)], rows.at[0]),
        (block.at[pl.ds(size - 2, 2)], rows.at[1]),
        (block.at[:, pl.ds(0, 16), :], columns.at[0]),
        (block.at[:, pl.ds(size - 16, 16), :], columns.at[1]),
        (block, held),
        (weight, held_weight),
    ]
    copies = [
        pltpu.make_async_copy(source, target, arrived.at[k])
        for k, (source, target) in enumerate(pairs)
    ]
    for copy in copies:
        copy.start()
    copies[0].wait()
    write_links(near, cols, found)
    for copy in copies[1:5]:
        copy.wait()
    left, right = columns[0].astype(f32), columns[1].astype(f32)
    for side, edge, second in (
        (0, rows[0, 0].astype(f32), rows[0, 1].astype(f32)),
        (1, right[:, 15, :], right[:, 14, :]),
        (2, rows[1, 1].astype(f32), rows[1, 0].astype(f32)),
        (3, left[:, 0, :], left[:, 1, :]),
    ):
        own[side] = edge
        strips[side, :, 0:c] = edge
        strips[side, :, c:] = second
    send_strips(found, strips, outs)
    for copy in copies[5:]:
        copy.wait()


def first_bulk(block, weight, shifted, pre, hidden, slope, pairs, lower, upper):
    count, size, lanes = pre.shape
    c = lanes // 2
    for i in range(count):
        pairs[i, :, 0:c] = block[2 * i]
        pairs[i, :, c:] = block[2 * i + 1]
    fill_columns(shifted, pairs)
    bulk_conv(shifted, weight, lower, upper, pre, False)
    for i in range(count):
        value, rate = gelu_both(pre[i])
        hidden[i] = value.astype(bf16)
        slope[i] = rate.astype(bf16)


def first_edges(found, *refs):
    received, weight, blocks = refs[:4], refs[4], refs[5:9]
    outs, hidden, slope, halo = refs[9:13], refs[13:17], refs[17:21], refs[21]
    rooms, strips, long, ends, narrow = refs[22:28], *refs[28:32]
    size, c = halo.shape[1:]
    take_strips(found, received, halo)
    terms = halo_terms(halo_windows(halo, long), weight)
    edges = add_strips(load_edges(*blocks), terms, rooms)
    both = [gelu_both(edge) for edge in edges]
    values = exact([value for value, _ in both])
    for k in range(4):
        hidden[k][...] = values[k]
        slope[k][...] = both[k][1]
    for k, edges in enumerate((values, [rate for _, rate in both])):
        edge_strips(edges, narrow)
        strips[:, :, k * c : (k + 1) * c] = narrow[...]
    rim_ends(halo, long, ends)
    send_strips(found, strips, outs)
    for k, out in enumerate(outs):
        straight = choose(found[k], ends.at[:, 0])
        turned = choose(found[k], ends.at[:, 1])
        here = jnp.concatenate([found[4 + k]] * 2, axis=0) == 1
        out[2 * size :] = jnp.where(here, turned, straight).astype(bf16)


def second_bulk(hidden, left, right, top, bottom, weight, cotangent, *refs):
    shifted, pre, out_field, delta, pairs, lower, upper = refs
    count, size, lanes = pre.shape
    c = lanes // 2
    pairs[...] = hidden[...].astype(f32)
    lay_edges(pairs, left, right, top, bottom)
    fill_columns(shifted, pairs)
    bulk_conv(shifted, weight, lower, upper, pre, False)
    for i in range(count):
        for parity in range(2):
            part = slice(parity * c, (parity + 1) * c)
            value, rate = gelu_both(pre[i, :, part])
            out_field[i, :, part] = value.astype(bf16)
            delta[i, :, part] = (cotangent[2 * i + parity].astype(f32) * rate).astype(bf16)


def second_edges(found, *refs):
    received, weight, blocks, wanted = refs[:4], refs[4], refs[5:9], refs[9:13]
    outs, out_field, delta, halo, grads = refs[13:17], refs[17:21], refs[21:25], *refs[25:27]
    rooms, strips, long = refs[27:33], refs[33], refs[34]
    half, depth = blocks[0].shape[:2]
    take_strips(found, received, halo)
    terms = halo_terms(halo_windows(halo, long), weight)
    edges = add_strips(load_edges(*blocks), terms, rooms)
    cots = []
    for ref, at in ((wanted[0], 0), (wanted[1], 16 - depth)):
        block = ref[...].astype(f32)
        block = block.reshape((half, 2) + block.shape[1:])[:, :, at : at + depth, :]
        cots.append(jnp.concatenate([block[:, 0], block[:, 1]], axis=-1))
    cots += [wanted[2][0].astype(f32), wanted[3][0].astype(f32)]
    both = [gelu_both(edge) for edge in edges]
    deltas = exact([cot * rate for cot, (_, rate) in zip(cots, both)])
    for k in range(4):
        out_field[k][...] = both[k][0]
        delta[k][...] = deltas[k]
    edge_strips(deltas, strips)
    halo_grads(strips, weight, long, grads)
    send_strips(found, grads, outs)


def second_back(*refs):
    bulk_delta, delta_edges, halo = refs[0], refs[1:5], refs[5]
    shifted, weight, bulk_slope = refs[6:9]
    grad_weight, grad_hidden, delta_first = refs[9:12]
    pairs, delta, lower, upper, moved, strips, long = refs[12:19]
    count = pairs.shape[0]
    pairs[...] = bulk_delta[...].astype(f32)
    lay_edges(pairs, *delta_edges)
    delta[...] = pairs[...].astype(bf16)
    bulk_weight_grad(shifted, delta, grad_weight)
    edge_strips([ref[...] for ref in delta_edges], strips)
    halo_weight_grad(halo_windows(halo, long), strips, grad_weight)
    fill_columns(moved, pairs)
    bulk_conv(moved, weight, lower, upper, grad_hidden, True)
    for i in range(count):
        delta_first[i] = (grad_hidden[i] * bulk_slope[i].astype(f32)).astype(bf16)


def first_grads(found, *refs):
    blocks, slope, bulk_delta, halo, shifted, other_grad = refs[:4], refs[4:8], *refs[8:12]
    own, near, carried, grads = refs[12], refs[13:17], refs[17:21], refs[21]
    delta, kept, given = refs[22:25]
    pairs, strips, long, grad_weight, room = refs[25:30]
    edges = [edge * rate[...] for edge, rate in zip(load_edges(*blocks), slope)]
    pairs[...] = bulk_delta[...].astype(f32)
    lay_edges(pairs, *edges)
    delta[...] = pairs[...].astype(bf16)
    bulk_weight_grad(shifted, delta, grad_weight)
    edge_strips(edges, strips)
    halo_weight_grad(halo_windows(halo, long), strips, grad_weight)
    rim_weight_grad(found, own, near, carried, grads, room, grad_weight)
    core = lax.axis_index("tile") & 1
    for tap in range(grad_weight.shape[0]):
        one, two = grad_weight[tap], other_grad[tap]
        kept[tap] = jnp.where(core == 0, one, two)
        given[tap] = jnp.where(core == 0, two, one).astype(bf16)


def first_back(found, *refs):
    received, weight, blocks, slope = refs[:4], refs[4], refs[5:9], refs[9:13]
    outs, delta = refs[13:17], refs[17:21]
    rooms, strips, long, grads, back = refs[21:27], *refs[27:31]
    take_strips(found, received, back, True)
    edges = add_strips(load_edges(*blocks), [back[s] for s in range(4)], rooms)
    deltas = exact([edge * rate[...] for edge, rate in zip(edges, slope)])
    for k in range(4):
        delta[k][...] = deltas[k]
    edge_strips(deltas, strips)
    halo_grads(strips, weight, long, grads)
    send_strips(found, grads, outs)


def last_bulk(delta, weight, bulk_out, *refs):
    delta_edges, out_edges, interior, out_field = refs[:4], refs[4:8], *refs[8:10]
    pairs, moved, lower, upper = refs[10:14]
    count, size, lanes = pairs.shape
    c = lanes // 2
    pairs[...] = bulk_out[...].astype(f32)
    lay_edges(pairs, *out_edges)
    for i in range(count):
        out_field[2 * i] = pairs[i, :, 0:c].astype(bf16)
        out_field[2 * i + 1] = pairs[i, :, c:].astype(bf16)
    pairs[...] = delta[...].astype(f32)
    lay_edges(pairs, *delta_edges)
    fill_columns(moved, pairs)
    bulk_conv(moved, weight, lower, upper, interior, True)


def last_edges(found, *refs):
    received, interior, grad = refs[:4], refs[4], refs[5]
    rooms, back, pairs = refs[6:12], refs[12], refs[13]
    count, size, lanes = interior.shape
    c = lanes // 2
    take_strips(found, received, back, True)
    edges = (
        interior[:, 0:8, :],
        interior[:, size - 8 :, :],
        interior[0, :, 0:c],
        interior[count - 1, :, c:],
    )
    edges = add_strips(edges, [back[s] for s in range(4)], rooms)
    pairs[...] = interior[...]
    lay_edges(pairs, *edges)
    for i in range(count):
        grad[2 * i] = pairs[i, :, 0:c].astype(bf16)
        grad[2 * i + 1] = pairs[i, :, c:].astype(bf16)


def call(kernel, name, ins, outs, scratch, cost=0, room=16 << 20):
    whole = pl.BlockSpec(memory_space=pltpu.VMEM)
    return pl.pallas_call(
        kernel,
        name=name,
        grid=(1,),
        in_specs=[spec or whole for _, spec in ins],
        out_specs=[whole] * len(outs),
        out_shape=outs,
        scratch_shapes=scratch,
        compiler_params=pltpu.CompilerParams(vmem_limit_bytes=room),
        cost_estimate=pl.CostEstimate(flops=cost, bytes_accessed=2 << 20, transcendentals=0),
    )(*[array for array, _ in ins])


def flip_swap(block, mask_ens, mask_tile):
    ens, tile = lax.axis_size("ens"), lax.axis_size("tile")
    route = [
        (e * tile + t, (e ^ mask_ens) * tile + (t ^ mask_tile))
        for e in range(ens)
        for t in range(tile)
    ]
    return lax.ppermute(block, ("ens", "tile"), route)


def seat_of():
    return lax.axis_index("tile") >> 2 & 3


def share_out(loads, kept, given, *refs):
    riders, own, sent = refs[: sum(loads)], refs[sum(loads)], refs[sum(loads) + 1 :]
    rows = own.shape[0]
    seat = seat_of()
    quarter = lambda at: pl.ds(pl.multiple_of(at * rows, rows), rows)
    add = lambda at: kept[quarter(at), :] + given[quarter(at), :].astype(f32)
    own[...] = add(seat)
    taken = 0
    for k, block in enumerate(sent):
        block[0:rows] = add(seat ^ (k + 1)).astype(bf16)
        if loads[k]:
            block[rows:] = riders[taken][...]
            taken += 1


def add_up(count, loads, base, *refs):
    got, riders, total = refs[:count], refs[count : count + loads], refs[count + loads]
    loaded = refs[count + loads + 1 :]
    rows = base.shape[0]
    terms = [base[...].astype(f32)] + [block[0:rows].astype(f32) for block in got]
    while len(terms) > 1:
        terms = [terms[i] + terms[i + 1] for i in range(0, len(terms), 2)]
    total[...] = terms[0].astype(bf16)
    for block, rider in zip(loaded, riders):
        block[0:rows] = terms[0].astype(bf16)
        block[rows:] = rider[...]


def line_masks():
    return [4, 8, 12]


def aboard(ways):
    tiles = lax.axis_size("tile")
    line = [tuple(t ^ mask for t in range(tiles)) for mask in line_masks()]
    return [ways.index(way) if way in ways else None for way in line]


def swap_line(blocks, riders, ways):
    riding = aboard(ways)
    got = [flip_swap(block, 0, mask) for block, mask in zip(blocks, line_masks())]
    came = [
        got[riding.index(k)] if k in riding else lax.ppermute(rider, "tile", list(enumerate(way)))
        for k, (rider, way) in enumerate(zip(riders, ways))
    ]
    return got, came


def scatter_line(kept, given, riders, ways):
    rows, lanes = kept.shape[0] // 4, kept.shape[1]
    S = jax.ShapeDtypeStruct
    given, riders = lax.optimization_barrier((flip_swap(given, 0, 1), riders))
    loads = [k is not None for k in aboard(ways)]
    taken = [riders[k] for k in aboard(ways) if k is not None]
    own, *sent = call(
        functools.partial(share_out, loads),
        "share_out",
        [(block, None) for block in (kept, given, *taken)],
        [S((rows, lanes), f32)]
        + [S((rows + load * riders[0].shape[0], lanes), bf16) for load in loads],
        [],
    )
    got, came = swap_line(sent, riders, ways)
    return own, got, came


def sum_rest(own, got, riders, ways):
    tiles = lax.axis_size("tile")
    groups, bit = [[(0, 2), (1, 0), (1, 2)]], 16
    while bit < tiles:
        groups.append([(0, 3 * bit), (0, 2 * bit), (0, bit)] if 2 * bit < tiles else [(0, bit)])
        bit *= 4
    S = jax.ShapeDtypeStruct
    riding = aboard(ways)
    for masks in groups + [None]:
        taken = [riders[k] for k in riding if k is not None] if masks is None else []
        own, *loaded = call(
            functools.partial(add_up, len(got), len(taken)),
            "add_up",
            [(block, None) for block in (own, *got, *taken)],
            [S(own.shape, bf16)]
            + [S((own.shape[0] + rider.shape[0], own.shape[1]), bf16) for rider in taken],
            [],
        )
        if masks is not None:
            got = [flip_swap(own, *mask) for mask in masks]
    return own, [own if k is None else loaded.pop(0) for k in riding]


def stack(*refs):
    rows = refs[0].shape[0]
    for k in range(4):
        refs[4][k] = refs[k][0:rows]


def both_grads(mine, others, first, second):
    rows = mine.shape[1]
    core, seat = lax.axis_index("tile") & 1, seat_of()
    for k in range(4):
        place = pl.ds(pl.multiple_of((seat ^ k) * rows, rows), rows)
        one, two = mine[k].astype(f32), others[k].astype(f32)
        first[place, :] = jnp.where(core == 0, one, two)
        second[place, :] = jnp.where(core == 0, two, one)


def local(fields, weight_first, weight_second, neighbours, cotangent):
    block, wanted = fields[0, 0], cotangent[0, 0]
    size, c = block.shape[0], block.shape[-1]
    half = size // 2
    count = lax.axis_size("tile")
    cols = max(4, count // 8)
    shape = weight_first.shape
    one, two = weight_first.reshape(9, c, c), weight_second.reshape(9, c, c)
    flops = 2 * size * size * 9 * c * c

    S = jax.ShapeDtypeStruct
    sent = [S((size, c), bf16)] * 4
    halo = S((4, size, c), f32)
    edge = [S((half, 8, 2 * c), f32)] * 2 + [S((size, c), f32)] * 2
    pairs = lambda kind: S((half, size, 2 * c), kind)
    shifted = S(((half + 1) * size, 6 * c), bf16)
    V = lambda leaf: pltpu.VMEM(leaf.shape, leaf.dtype)
    ahead = [pltpu.VMEM((6 * c, 2 * c), bf16)] * 2
    back = [pltpu.VMEM((2 * c, 6 * c), bf16)] * 2
    rooms = [V(leaf) for leaf in edge] + [pltpu.VMEM((size, c), f32)] * 2
    long = pltpu.VMEM((4, size + 16, c), f32)
    whole = lambda arrays: [(array, None) for array in arrays]

    def edge_blocks(array):
        last = size // 8 - 1
        return [
            (array, pl.BlockSpec((half, 8, 2 * c), lambda step: (0, 0, 0))),
            (array, pl.BlockSpec((half, 8, 2 * c), lambda step: (0, last, 0))),
            (array, pl.BlockSpec((1, size, c), lambda step: (0, 0, 0))),
            (array, pl.BlockSpec((1, size, c), lambda step: (half - 1, 0, 1))),
        ]

    def image_edges(array):
        last = size // 16 - 1
        return [
            (array, pl.BlockSpec((size, 16, c), lambda step: (0, 0, 0))),
            (array, pl.BlockSpec((size, 16, c), lambda step: (0, last, 0))),
            (array, pl.BlockSpec((1, size, c), lambda step: (0, 0, 0))),
            (array, pl.BlockSpec((1, size, c), lambda step: (size - 1, 0, 0))),
        ]

    wide = pltpu.VMEM((4, size, 2 * c), f32)
    far = pl.BlockSpec(memory_space=pl.ANY)
    stay = lambda array: (pltpu.with_memory_space_constraint(array, pltpu.HBM), far)
    *strips, found, block, one, own = call(
        functools.partial(first_strips, cols),
        "first_strips",
        [stay(neighbours.T), stay(block), stay(one)],
        [S((2 * size, c), bf16)] * 4
        + [S((12, 8, 128), jnp.int32), S(block.shape, bf16), S(one.shape, bf16), halo],
        [wide, pltpu.VMEM((2, size, 16, c), bf16), pltpu.VMEM((2, 2, size, c), bf16)]
        + [pltpu.SMEM(neighbours.shape[::-1], jnp.int32), pltpu.SemaphoreType.DMA((7,))],
    )
    links = (found, None)
    near = swap_all(strips, cols)
    shifted_one, pre_one, hidden, slope = call(
        first_bulk,
        "first_bulk",
        whole([block, one]),
        [shifted, pairs(f32), pairs(bf16), pairs(bf16)],
        [V(pairs(bf16))] + ahead,
        flops,
    )
    found = call(
        first_edges,
        "first_edges",
        [links] + whole(near) + [(one, None)] + edge_blocks(pre_one),
        [S((2 * size + 16, c), bf16)] * 4 + edge + edge + [halo],
        rooms + [wide, long, pltpu.VMEM((4, 2, 16, c), f32), V(halo)],
    )
    strips, hidden_edges, slope_edges, halo_one = found[:4], found[4:8], found[8:12], found[12]
    carried = swap_all(strips, cols)
    shifted_two, pre_two, out_bulk, delta_bulk = call(
        second_bulk,
        "second_bulk",
        whole([hidden, *hidden_edges, two, wanted]),
        [shifted, pairs(f32), pairs(bf16), pairs(bf16)],
        [V(pairs(f32))] + ahead,
        flops,
    )
    found = call(
        second_edges,
        "second_edges",
        [links] + whole(carried) + [(two, None)] + edge_blocks(pre_two) + image_edges(wanted),
        sent + edge + edge + [halo, halo],
        rooms + [V(halo), long],
    )
    strips, out_edges, delta_edges, halo_two, grads = found[:4], found[4:8], found[8:12], *found[12:]
    grad_two, grad_hidden, delta_one = call(
        second_back,
        "second_back",
        whole([delta_bulk, *delta_edges, halo_two, shifted_two, two, slope]),
        [S((9, c, c), f32), pairs(f32), pairs(bf16)],
        [V(pairs(f32)), V(pairs(bf16))] + back + [V(shifted), V(halo), long],
        2 * flops,
    )
    delta_one, kept, given = call(
        first_grads,
        "first_grads",
        [links]
        + edge_blocks(grad_hidden)
        + whole([*slope_edges, delta_one, halo_one, shifted_one, grad_two])
        + whole([own, *near, *carried, grads]),
        [pairs(bf16), S((9, c, c), f32), S((9, c, c), bf16)],
        [V(pairs(f32)), V(halo), long, pltpu.VMEM((9, c, c), f32)]
        + [pltpu.VMEM((3, size + 16, c), f32)],
        flops,
    )
    ways = routes(cols)
    quarter, got, strips = scatter_line(
        kept.reshape(9 * c, c), given.reshape(9 * c, c), strips, ways
    )
    found = call(
        first_back,
        "first_back",
        [links] + whole(strips) + [(one, None)] + edge_blocks(grad_hidden) + whole(slope_edges),
        sent + edge,
        rooms + [V(halo), long, V(halo), V(halo)],
    )
    strips, delta_edges = found[:4], found[4:8]
    interior, out_field = call(
        last_bulk,
        "last_bulk",
        whole([delta_one, one, out_bulk, *delta_edges, *out_edges]),
        [pairs(f32), S(block.shape, bf16)],
        [V(pairs(f32)), V(shifted)] + back,
        flops,
    )
    quarter, blocks = sum_rest(quarter, got, strips, ways)
    quarter, blocks, strips, interior = lax.optimization_barrier(
        (quarter, blocks, strips, interior)
    )
    got, strips = lax.optimization_barrier(swap_line(blocks, strips, ways))
    (grad_block,) = call(
        last_edges,
        "last_edges",
        [links] + whole([*strips, interior]),
        [S(block.shape, bf16)],
        rooms + [V(halo), V(pairs(f32))],
    )
    quarters = [quarter, *got]
    (stacked,) = call(stack, "stack", whole(quarters), [S((4, *quarter.shape), bf16)], [])
    others, grad_block = lax.optimization_barrier((flip_swap(stacked, 0, 1), grad_block))
    grads = call(
        both_grads,
        "both_grads",
        whole([stacked, others]),
        [S((9 * c, c), f32)] * 2,
        [],
    )
    grad_first, grad_second = (grad.reshape(shape) for grad in grads)
    return (out_field[None, None], grad_block[None, None], grad_first, grad_second)


def solution(mesh):
    placed = (P("ens", "tile", None, None, None), P(), P(), P(), P("ens", "tile", None, None, None))
    return jax.shard_map(
        local,
        mesh=mesh,
        in_specs=placed,
        out_specs=(
            P("ens", "tile", None, None, None),
            P("ens", "tile", None, None, None),
            P(),
            P(),
        ),
        check_vma=False,
    )
```

```python
import functools

import jax
import jax.numpy as jnp
from jax import lax
from jax.experimental import pallas as pl
from jax.experimental.pallas import tpu as pltpu
from jax.sharding import PartitionSpec as P

root_half = 0.7071067811865476
inv_root_tau = 0.3989422804014327
bf16, f32 = jnp.bfloat16, jnp.float32
NT = (((1,), (1,)), ((), ()))
TN = (((0,), (0,)), ((), ()))


def gelu_both(pre):
    bell = 0.5 * (1.0 + lax.erf(pre * root_half))
    return pre * bell, bell + pre * jnp.exp(-0.5 * pre * pre) * inv_root_tau


def partners(index, count, cols):
    odd, row_odd = index & 1, (index // cols) & 1
    return [
        (index + cols * (2 * row_odd - 1) + count) % count,
        (index - 1 + 2 * odd + count) % count,
        (index + cols * (1 - 2 * row_odd) + count) % count,
        (index + 1 - 2 * odd + count) % count,
    ]


def write_links(table, cols, found):
    count = lax.axis_size("tile")
    me = lax.axis_index("tile")
    for k, other in enumerate(partners(me, count, cols)):
        side, back = jnp.int32(0), jnp.int32(0)
        for s in range(1, 4):
            side = jnp.where(table[s, me] == other, s, side)
            back = jnp.where(table[s, other] == me, s, back)
        turn = jnp.where((side >= 2) == (back >= 2), 1, 0)
        found[k] = jnp.full(found.shape[1:], side, jnp.int32)
        found[4 + k] = jnp.full(found.shape[1:], turn, jnp.int32)
        found[8 + k] = jnp.full(found.shape[1:], back, jnp.int32)


def masked(found, block):
    wide = jnp.concatenate([found] * (block.shape[-1] // found.shape[-1]), axis=1)
    return wide[None]


def choose(found, strips):
    _, size, c = strips.shape
    chosen = strips[0].reshape(size // 8, 8, c)
    for s in range(1, 4):
        here = masked(found, chosen) == s
        chosen = jnp.where(here, strips[s].reshape(chosen.shape), chosen)
    return chosen.reshape(size, c)


def send_strips(found, strips, outs):
    _, size, lanes = strips.shape
    c = outs[0].shape[-1]
    at_row = lax.broadcasted_iota(jnp.int32, (size, size), 0)
    at_col = lax.broadcasted_iota(jnp.int32, (size, size), 1)
    for k, out in enumerate(outs):
        turn = found[4 + k][0:1, 0:size] == 1
        order = (at_col == jnp.where(turn, size - 1 - at_row, at_row)).astype(f32).astype(bf16)
        chosen = choose(found[k], strips).astype(bf16)
        turned = jnp.dot(order, chosen, preferred_element_type=f32).astype(bf16)
        for part in range(lanes // c):
            out[part * size : (part + 1) * size] = turned[:, part * c : (part + 1) * c]


def take_strips(found, received, strips, last=False):
    _, size, c = strips.shape
    blocks = []
    for block in received:
        row = block.shape[0] - size if last else 0
        blocks.append(block[row : row + size].astype(f32).reshape(size // 8, 8, c))
    for s in range(4):
        taken = blocks[0]
        for k in range(1, 4):
            taken = jnp.where(found[k][None] == s, blocks[k], taken)
        strips[s] = taken.reshape(size, c)


def routes(cols):
    count = lax.axis_size("tile")
    return list(zip(*[partners(p, count, cols) for p in range(count)]))


def swap_all(blocks, cols):
    return [
        lax.ppermute(block, "tile", list(enumerate(way)))
        for block, way in zip(blocks, routes(cols))
    ]


def fill_columns(shifted, pairs):
    count, size, lanes = pairs.shape
    c = lanes // 2
    at = lax.broadcasted_iota(jnp.int32, (size, c), 0)
    first, last = at == 0, at == size - 1
    shifted[0:size, 0 : 3 * c] = jnp.zeros((size, 3 * c), bf16)
    shifted[count * size :, 3 * c :] = jnp.zeros((size, 3 * c), bf16)
    for i in range(count):
        for parity, row, lane in ((1, (i + 1) * size, 0), (0, i * size, 3 * c)):
            value = pairs[i, :, parity * c : (parity + 1) * c].astype(f32)
            before = jnp.where(first, 0.0, pltpu.roll(value, 1, 0))
            after = jnp.where(last, 0.0, pltpu.roll(value, size - 1, 0))
            shifted[row : row + size, lane : lane + c] = before.astype(bf16)
            shifted[row : row + size, lane + c : lane + 2 * c] = value.astype(bf16)
            shifted[row : row + size, lane + 2 * c : lane + 3 * c] = after.astype(bf16)


def blocks_of_pairs(tap, lower, upper, c):
    for b in range(3):
        for half, parity, target, a in (
            (lower, 0, 0, 0),
            (lower, 0, 1, None),
            (lower, 1, 0, 1),
            (lower, 1, 1, 0),
            (upper, 0, 0, 2),
            (upper, 0, 1, 1),
            (upper, 1, 0, None),
            (upper, 1, 1, 2),
        ):
            yield half, (parity * 3 + b) * c, target * c, tap(a, b) if a is not None else None


def bulk_conv(shifted, weight, lower, upper, out, backward):
    c = weight.shape[-1]
    count, size, lanes = out.shape
    if backward:
        tap = lambda a, b: weight[(2 - a) * 3 + 2 - b]
    else:
        tap = lambda a, b: weight[a * 3 + b]
    for half, depth, target, block in blocks_of_pairs(tap, lower, upper, c):
        if block is None:
            block = jnp.zeros((c, c), bf16)
        if backward:
            half[target : target + c, depth : depth + c] = block
        else:
            half[depth : depth + c, target : target + c] = block
    rows = count * size
    dims = NT if backward else (((1,), (0,)), ((), ()))
    total = lax.dot_general(
        shifted[0:rows, :], lower[...], dims, preferred_element_type=f32
    ) + lax.dot_general(shifted[size : size + rows, :], upper[...], dims, preferred_element_type=f32)
    out[...] = total.reshape(count, size, lanes)


def bulk_weight_grad(shifted, delta, out):
    count, size, lanes = delta.shape
    c = lanes // 2
    rows = count * size
    flat = delta[...].reshape(rows, lanes)
    low = lax.dot_general(shifted[0:rows, :], flat, TN, preferred_element_type=f32)
    high = lax.dot_general(shifted[size : size + rows, :], flat, TN, preferred_element_type=f32)
    for b in range(3):
        here, there = b * c, (3 + b) * c
        out[b] = low[here : here + c, 0:c] + low[there : there + c, c:]
        out[3 + b] = low[there : there + c, 0:c] + high[here : here + c, c:]
        out[6 + b] = high[here : here + c, 0:c] + high[there : there + c, c:]


def load_edges(left, right, top, bottom):
    return left[...], right[...], top[0], bottom[0]


def to_pairs(strip, room):
    room[...] = strip
    half = strip.shape[0] // 2
    return jnp.concatenate(
        [room[pl.ds(0, half, stride=2), :], room[pl.ds(1, half, stride=2), :]], axis=1
    )


def add_strips(edges, strips, rooms):
    left, right, top, bottom = edges
    t, r, b, l = strips
    c = t.shape[1]
    half, depth, size = left.shape[0], left.shape[1], t.shape[0]
    at = lax.broadcasted_iota(jnp.int32, left.shape, 1)
    left_room, right_room, top_room, bottom_room, strip_a, strip_b = rooms
    left_room[...] = left + jnp.where(at == 0, to_pairs(l, strip_a)[:, None, :], 0.0)
    right_room[...] = right + jnp.where(at == depth - 1, to_pairs(r, strip_b)[:, None, :], 0.0)
    left_room[0, :, 0:c] += t[0:depth]
    left_room[half - 1, :, c:] += b[0:depth]
    right_room[0, :, 0:c] += t[size - depth :]
    right_room[half - 1, :, c:] += b[size - depth :]
    top_room[...] = top + t
    bottom_room[...] = bottom + b
    top_room[0:depth] = left_room[0, :, 0:c]
    top_room[size - depth :] = right_room[0, :, 0:c]
    bottom_room[0:depth] = left_room[half - 1, :, c:]
    bottom_room[size - depth :] = right_room[half - 1, :, c:]
    return left_room[...], right_room[...], top_room[...], bottom_room[...]


def edge_strips(edges, strips):
    left, right, top, bottom = edges
    c = top.shape[1]
    half = left.shape[0]
    strips[0] = top
    strips[2] = bottom
    for side, column in ((1, right[:, -1, :]), (3, left[:, 0, :])):
        strips[side, pl.ds(0, half, stride=2), :] = column[:, 0:c]
        strips[side, pl.ds(1, half, stride=2), :] = column[:, c:]


def lay_edges(pairs, left, right, top, bottom):
    depth = left.shape[1]
    size = pairs.shape[1]
    c = top.shape[-1]
    pairs[:, 0:depth, :] = left[...]
    pairs[:, size - depth :, :] = right[...]
    pairs[0, :, 0:c] = top[...]
    pairs[pairs.shape[0] - 1, :, c:] = bottom[...]


def halo_windows(strips, rooms):
    size = strips.shape[1]
    top, right, bottom, left = (strips[s] for s in range(4))
    zero = jnp.zeros_like(top[0:1])
    ends = [
        (0.5 * (top[0:1] + left[0:1]), 0.5 * (top[size - 1 :] + right[0:1])),
        (zero, zero),
        (0.5 * (left[size - 1 :] + bottom[0:1]), 0.5 * (bottom[size - 1 :] + right[size - 1 :])),
        (zero, zero),
    ]
    windows = []
    for s, (strip, (before, after)) in enumerate(zip((top, right, bottom, left), ends)):
        rooms[s, 7:8, :] = before
        rooms[s, 8 : 8 + size, :] = strip
        rooms[s, 8 + size : 9 + size, :] = after
        windows.append(
            jnp.concatenate([rooms[s, 7 + k : 7 + k + size, :] for k in range(3)], axis=1).astype(
                bf16
            )
        )
    return windows


def rim_ends(strips, rooms, ends):
    size = strips.shape[1]
    last = size - 1
    ne, nw = rooms[0, 8 + size : 9 + size, :], rooms[0, 7:8, :]
    se, sw = rooms[2, 8 + size : 9 + size, :], rooms[2, 7:8, :]
    across = lambda at: (strips[3, at : at + 1, :], strips[1, at : at + 1, :])
    along = lambda at: (strips[0, at : at + 1, :], strips[2, at : at + 1, :])
    ends[...] = jnp.zeros_like(ends)
    for side, rows in enumerate(
        (
            ((nw, ne), across(0), across(1)),
            ((ne, se), along(last), along(last - 1)),
            ((sw, se), across(last), across(last - 1)),
            ((nw, sw), along(0), along(1)),
        )
    ):
        for depth, (before, after) in enumerate(rows):
            for turned, pair in enumerate(((before, after), (after, before))):
                ends[side, turned, 2 * depth : 2 * depth + 1, :] = pair[0]
                ends[side, turned, 2 * depth + 1 : 2 * depth + 2, :] = pair[1]


def rim_weight_grad(found, own, near, carried, grads, room, out):
    _, size, c = own.shape
    windows, deltas = [], []
    for k in range(4):
        ends = carried[k][2 * size :].astype(f32)
        rows = (
            choose(found[k], own),
            near[k][0:size].astype(f32),
            near[k][size : 2 * size].astype(f32),
        )
        for depth, row in enumerate(rows):
            room[depth, 7:8, :] = ends[2 * depth : 2 * depth + 1]
            room[depth, 8 : 8 + size, :] = row
            room[depth, 8 + size : 9 + size, :] = ends[2 * depth + 1 : 2 * depth + 2]
        part = [
            [room[d, 7 + b : 7 + b + size, :].reshape(size // 8, 8, c) for b in range(3)]
            for d in range(3)
        ]
        turned = found[4 + k][None] == 1
        back = found[8 + k][None]
        swap = lambda here, one, two: (jnp.where(here, two, one), jnp.where(here, one, two))
        for d in range(3):
            part[d][0], part[d][2] = swap(turned, part[d][0], part[d][2])
        for b in range(3):
            inward = (back == 1) | (back == 2)
            part[0][b], part[2][b] = swap(inward, part[0][b], part[2][b])
        for a, b in ((0, 1), (0, 2), (1, 2)):
            upright = (back & 1) == 1
            part[a][b], part[b][a] = swap(upright, part[a][b], part[b][a])
        windows.append(
            jnp.concatenate(
                [part[a][b].reshape(size, c).astype(bf16) for a in range(3) for b in range(3)],
                axis=1,
            )
        )
        delta = choose(found[k], grads).astype(bf16).astype(f32)
        deltas.append((delta * carried[k][size : 2 * size].astype(f32)).astype(bf16))
    term = lax.dot_general(
        jnp.concatenate(windows, axis=0),
        jnp.concatenate(deltas, axis=0),
        TN,
        preferred_element_type=f32,
    )
    for tap in range(9):
        out[tap] += term[tap * c : (tap + 1) * c]


side_taps = ((0, 1, 2), (2, 5, 8), (6, 7, 8), (0, 3, 6))


def halo_terms(windows, weight):
    return [
        jnp.dot(
            window,
            jnp.concatenate([weight[tap] for tap in taps], axis=0),
            preferred_element_type=f32,
        )
        for window, taps in zip(windows, side_taps)
    ]


def halo_weight_grad(windows, strips, out):
    c = out.shape[-1]
    for s, (window, taps) in enumerate(zip(windows, side_taps)):
        term = lax.dot_general(window, strips[s].astype(bf16), TN, preferred_element_type=f32)
        for k, tap in enumerate(taps):
            out[tap] += term[k * c : (k + 1) * c]


def halo_grads(strips, weight, rooms, grads):
    size, c = strips.shape[1:]
    long = size + 8
    for s, taps in enumerate(side_taps):
        rooms[s, 0:8, :] = jnp.zeros((8, c), f32)
        rooms[s, 8 : 8 + size, :] = strips[s]
        rooms[s, 8 + size :, :] = jnp.zeros((8, c), f32)
        copies = jnp.concatenate([rooms[s, 8 - k : 8 - k + long, :] for k in range(3)], axis=1)
        rims = jnp.concatenate([weight[tap] for tap in taps], axis=1)
        rim = lax.dot_general(copies.astype(bf16), rims, NT, preferred_element_type=f32)
        rooms[s, 0:long, :] = rim
        at = lax.broadcasted_iota(jnp.int32, (size, c), 0)
        corner = jnp.where(at == 0, rooms[s, 0:1, :], 0.0) + jnp.where(
            at == size - 1, rooms[s, size + 1 : size + 2, :], 0.0
        )
        grads[s] = rooms[s, 1 : 1 + size, :] + 0.5 * corner


def exact(values):
    return [value.astype(bf16).astype(f32) for value in values]


def first_strips(cols, table, block, weight, *refs):
    outs, found, held, held_weight, own = refs[:4], *refs[4:8]
    strips, columns, rows, near, arrived = refs[8:13]
    size, c = own.shape[1:]
    pairs = [
        (table, near),
        (block.at[pl.ds(0, 2)], rows.at[0]),
        (block.at[pl.ds(size - 2, 2)], rows.at[1]),
        (block.at[:, pl.ds(0, 16), :], columns.at[0]),
        (block.at[:, pl.ds(size - 16, 16), :], columns.at[1]),
        (block, held),
        (weight, held_weight),
    ]
    copies = [
        pltpu.make_async_copy(source, target, arrived.at[k])
        for k, (source, target) in enumerate(pairs)
    ]
    for copy in copies:
        copy.start()
    copies[0].wait()
    write_links(near, cols, found)
    for copy in copies[1:5]:
        copy.wait()
    left, right = columns[0].astype(f32), columns[1].astype(f32)
    for side, edge, second in (
        (0, rows[0, 0].astype(f32), rows[0, 1].astype(f32)),
        (1, right[:, 15, :], right[:, 14, :]),
        (2, rows[1, 1].astype(f32), rows[1, 0].astype(f32)),
        (3, left[:, 0, :], left[:, 1, :]),
    ):
        own[side] = edge
        strips[side, :, 0:c] = edge
        strips[side, :, c:] = second
    send_strips(found, strips, outs)
    for copy in copies[5:]:
        copy.wait()


def first_bulk(block, weight, shifted, pre, hidden, slope, pairs, lower, upper):
    count, size, lanes = pre.shape
    c = lanes // 2
    for i in range(count):
        pairs[i, :, 0:c] = block[2 * i]
        pairs[i, :, c:] = block[2 * i + 1]
    fill_columns(shifted, pairs)
    bulk_conv(shifted, weight, lower, upper, pre, False)
    for i in range(count):
        value, rate = gelu_both(pre[i])
        hidden[i] = value.astype(bf16)
        slope[i] = rate.astype(bf16)


def first_edges(found, *refs):
    received, weight, blocks = refs[:4], refs[4], refs[5:9]
    outs, hidden, slope, halo = refs[9:13], refs[13:17], refs[17:21], refs[21]
    rooms, strips, long, ends, narrow = refs[22:28], *refs[28:32]
    size, c = halo.shape[1:]
    take_strips(found, received, halo)
    terms = halo_terms(halo_windows(halo, long), weight)
    edges = add_strips(load_edges(*blocks), terms, rooms)
    both = [gelu_both(edge) for edge in edges]
    values = exact([value for value, _ in both])
    for k in range(4):
        hidden[k][...] = values[k]
        slope[k][...] = both[k][1]
    for k, edges in enumerate((values, [rate for _, rate in both])):
        edge_strips(edges, narrow)
        strips[:, :, k * c : (k + 1) * c] = narrow[...]
    rim_ends(halo, long, ends)
    send_strips(found, strips, outs)
    for k, out in enumerate(outs):
        straight = choose(found[k], ends.at[:, 0])
        turned = choose(found[k], ends.at[:, 1])
        here = jnp.concatenate([found[4 + k]] * 2, axis=0) == 1
        out[2 * size :] = jnp.where(here, turned, straight).astype(bf16)


def second_bulk(hidden, left, right, top, bottom, weight, cotangent, *refs):
    shifted, pre, out_field, delta, pairs, lower, upper = refs
    count, size, lanes = pre.shape
    c = lanes // 2
    pairs[...] = hidden[...].astype(f32)
    lay_edges(pairs, left, right, top, bottom)
    fill_columns(shifted, pairs)
    bulk_conv(shifted, weight, lower, upper, pre, False)
    for i in range(count):
        for parity in range(2):
            part = slice(parity * c, (parity + 1) * c)
            value, rate = gelu_both(pre[i, :, part])
            out_field[i, :, part] = value.astype(bf16)
            delta[i, :, part] = (cotangent[2 * i + parity].astype(f32) * rate).astype(bf16)


def second_edges(found, *refs):
    received, weight, blocks, wanted = refs[:4], refs[4], refs[5:9], refs[9:13]
    outs, out_field, delta, halo, grads = refs[13:17], refs[17:21], refs[21:25], *refs[25:27]
    rooms, strips, long = refs[27:33], refs[33], refs[34]
    half, depth = blocks[0].shape[:2]
    take_strips(found, received, halo)
    terms = halo_terms(halo_windows(halo, long), weight)
    edges = add_strips(load_edges(*blocks), terms, rooms)
    cots = []
    for ref, at in ((wanted[0], 0), (wanted[1], 16 - depth)):
        block = ref[...].astype(f32)
        block = block.reshape((half, 2) + block.shape[1:])[:, :, at : at + depth, :]
        cots.append(jnp.concatenate([block[:, 0], block[:, 1]], axis=-1))
    cots += [wanted[2][0].astype(f32), wanted[3][0].astype(f32)]
    both = [gelu_both(edge) for edge in edges]
    deltas = exact([cot * rate for cot, (_, rate) in zip(cots, both)])
    for k in range(4):
        out_field[k][...] = both[k][0]
        delta[k][...] = deltas[k]
    edge_strips(deltas, strips)
    halo_grads(strips, weight, long, grads)
    send_strips(found, grads, outs)


def second_back(*refs):
    bulk_delta, delta_edges, halo = refs[0], refs[1:5], refs[5]
    shifted, weight, bulk_slope = refs[6:9]
    grad_weight, grad_hidden, delta_first = refs[9:12]
    pairs, delta, lower, upper, moved, strips, long = refs[12:19]
    count = pairs.shape[0]
    pairs[...] = bulk_delta[...].astype(f32)
    lay_edges(pairs, *delta_edges)
    delta[...] = pairs[...].astype(bf16)
    bulk_weight_grad(shifted, delta, grad_weight)
    edge_strips([ref[...] for ref in delta_edges], strips)
    halo_weight_grad(halo_windows(halo, long), strips, grad_weight)
    fill_columns(moved, pairs)
    bulk_conv(moved, weight, lower, upper, grad_hidden, True)
    for i in range(count):
        delta_first[i] = (grad_hidden[i] * bulk_slope[i].astype(f32)).astype(bf16)


def first_grads(found, *refs):
    blocks, slope, bulk_delta, halo, shifted, other_grad = refs[:4], refs[4:8], *refs[8:12]
    own, near, carried, grads = refs[12], refs[13:17], refs[17:21], refs[21]
    delta, kept, given = refs[22:25]
    pairs, strips, long, grad_weight, room = refs[25:30]
    edges = [edge * rate[...] for edge, rate in zip(load_edges(*blocks), slope)]
    pairs[...] = bulk_delta[...].astype(f32)
    lay_edges(pairs, *edges)
    delta[...] = pairs[...].astype(bf16)
    bulk_weight_grad(shifted, delta, grad_weight)
    edge_strips(edges, strips)
    halo_weight_grad(halo_windows(halo, long), strips, grad_weight)
    rim_weight_grad(found, own, near, carried, grads, room, grad_weight)
    core = lax.axis_index("tile") & 1
    for tap in range(grad_weight.shape[0]):
        one, two = grad_weight[tap], other_grad[tap]
        kept[tap] = jnp.where(core == 0, one, two)
        given[tap] = jnp.where(core == 0, two, one).astype(bf16)


def first_back(found, *refs):
    received, weight, blocks, slope = refs[:4], refs[4], refs[5:9], refs[9:13]
    outs, delta = refs[13:17], refs[17:21]
    rooms, strips, long, grads, back = refs[21:27], *refs[27:31]
    take_strips(found, received, back, True)
    edges = add_strips(load_edges(*blocks), [back[s] for s in range(4)], rooms)
    deltas = exact([edge * rate[...] for edge, rate in zip(edges, slope)])
    for k in range(4):
        delta[k][...] = deltas[k]
    edge_strips(deltas, strips)
    halo_grads(strips, weight, long, grads)
    send_strips(found, grads, outs)


def last_bulk(delta, weight, bulk_out, *refs):
    delta_edges, out_edges, interior, out_field = refs[:4], refs[4:8], *refs[8:10]
    pairs, moved, lower, upper = refs[10:14]
    count, size, lanes = pairs.shape
    c = lanes // 2
    pairs[...] = bulk_out[...].astype(f32)
    lay_edges(pairs, *out_edges)
    for i in range(count):
        out_field[2 * i] = pairs[i, :, 0:c].astype(bf16)
        out_field[2 * i + 1] = pairs[i, :, c:].astype(bf16)
    pairs[...] = delta[...].astype(f32)
    lay_edges(pairs, *delta_edges)
    fill_columns(moved, pairs)
    bulk_conv(moved, weight, lower, upper, interior, True)


def last_edges(found, *refs):
    received, interior, grad = refs[:4], refs[4], refs[5]
    rooms, back, pairs = refs[6:12], refs[12], refs[13]
    count, size, lanes = interior.shape
    c = lanes // 2
    take_strips(found, received, back, True)
    edges = (
        interior[:, 0:8, :],
        interior[:, size - 8 :, :],
        interior[0, :, 0:c],
        interior[count - 1, :, c:],
    )
    edges = add_strips(edges, [back[s] for s in range(4)], rooms)
    pairs[...] = interior[...]
    lay_edges(pairs, *edges)
    for i in range(count):
        grad[2 * i] = pairs[i, :, 0:c].astype(bf16)
        grad[2 * i + 1] = pairs[i, :, c:].astype(bf16)


def call(kernel, name, ins, outs, scratch, cost=0, room=16 << 20, out_spec=None):
    whole = pl.BlockSpec(memory_space=pltpu.VMEM)
    return pl.pallas_call(
        kernel,
        name=name,
        grid=(1,),
        in_specs=[spec or whole for _, spec in ins],
        out_specs=[out_spec or whole] * len(outs),
        out_shape=outs,
        scratch_shapes=scratch,
        compiler_params=pltpu.CompilerParams(vmem_limit_bytes=room),
        cost_estimate=pl.CostEstimate(flops=cost, bytes_accessed=2 << 20, transcendentals=0),
    )(*[array for array, _ in ins])


def flip_swap(block, mask_ens, mask_tile):
    ens, tile = lax.axis_size("ens"), lax.axis_size("tile")
    route = [
        (e * tile + t, (e ^ mask_ens) * tile + (t ^ mask_tile))
        for e in range(ens)
        for t in range(tile)
    ]
    return lax.ppermute(block, ("ens", "tile"), route)


def seat_of():
    return lax.axis_index("tile") >> 2 & 3


def share_out(loads, kept, given, *refs):
    riders, own, sent = refs[: sum(loads)], refs[sum(loads)], refs[sum(loads) + 1 :]
    rows = own.shape[0]
    seat = seat_of()
    quarter = lambda at: pl.ds(pl.multiple_of(at * rows, rows), rows)
    add = lambda at: kept[quarter(at), :] + given[quarter(at), :].astype(f32)
    own[...] = add(seat)
    taken = 0
    for k, block in enumerate(sent):
        block[0:rows] = add(seat ^ (k + 1)).astype(bf16)
        if loads[k]:
            block[rows:] = riders[taken][...]
            taken += 1


def add_up(count, loads, base, *refs):
    got, riders, total = refs[:count], refs[count : count + loads], refs[count + loads]
    loaded = refs[count + loads + 1 :]
    rows = base.shape[0]
    terms = [base[...].astype(f32)] + [block[0:rows].astype(f32) for block in got]
    while len(terms) > 1:
        terms = [terms[i] + terms[i + 1] for i in range(0, len(terms), 2)]
    total[...] = terms[0].astype(bf16)
    for block, rider in zip(loaded, riders):
        block[0:rows] = terms[0].astype(bf16)
        block[rows:] = rider[...]


def line_masks():
    return [4, 8, 12]


def aboard(ways):
    tiles = lax.axis_size("tile")
    line = [tuple(t ^ mask for t in range(tiles)) for mask in line_masks()]
    return [ways.index(way) if way in ways else None for way in line]


def swap_line(blocks, riders, ways):
    riding = aboard(ways)
    got = [flip_swap(block, 0, mask) for block, mask in zip(blocks, line_masks())]
    came = [
        got[riding.index(k)] if k in riding else lax.ppermute(rider, "tile", list(enumerate(way)))
        for k, (rider, way) in enumerate(zip(riders, ways))
    ]
    return got, came


def scatter_line(kept, given, riders, ways):
    rows, lanes = kept.shape[0] // 4, kept.shape[1]
    S = jax.ShapeDtypeStruct
    given, riders = lax.optimization_barrier((flip_swap(given, 0, 1), riders))
    loads = [k is not None for k in aboard(ways)]
    taken = [riders[k] for k in aboard(ways) if k is not None]
    own, *sent = call(
        functools.partial(share_out, loads),
        "share_out",
        [(block, None) for block in (kept, given, *taken)],
        [S((rows, lanes), f32)]
        + [S((rows + load * riders[0].shape[0], lanes), bf16) for load in loads],
        [],
    )
    got, came = swap_line(sent, riders, ways)
    return own, got, came


def sum_rest(own, got, riders, ways):
    tiles = lax.axis_size("tile")
    groups, bit = [[(0, 2), (1, 0), (1, 2)]], 16
    while bit < tiles:
        groups.append([(0, 3 * bit), (0, 2 * bit), (0, bit)] if 2 * bit < tiles else [(0, bit)])
        bit *= 4
    S = jax.ShapeDtypeStruct
    riding = aboard(ways)
    for masks in groups + [None]:
        taken = [riders[k] for k in riding if k is not None] if masks is None else []
        own, *loaded = call(
            functools.partial(add_up, len(got), len(taken)),
            "add_up",
            [(block, None) for block in (own, *got, *taken)],
            [S(own.shape, bf16)]
            + [S((own.shape[0] + rider.shape[0], own.shape[1]), bf16) for rider in taken],
            [],
        )
        if masks is not None:
            got = [flip_swap(own, *mask) for mask in masks]
    return own, [own if k is None else loaded.pop(0) for k in riding]


def stack(*refs):
    rows = refs[0].shape[0]
    for k in range(4):
        refs[4][k] = refs[k][0:rows]


def both_grads(mine, others, first, second, one, two, sent):
    rows = mine.shape[1]
    core, seat = lax.axis_index("tile") & 1, seat_of()
    copies = []
    for k in range(4):
        here, there = mine[k].astype(f32), others[k].astype(f32)
        one[k] = jnp.where(core == 0, here, there)
        two[k] = jnp.where(core == 0, there, here)
        place = pl.ds(pl.multiple_of((seat ^ k) * rows, rows), rows)
        for which, (room, out) in enumerate(((one, first), (two, second))):
            copy = pltpu.make_async_copy(room.at[k], out.at[place], sent.at[which, k])
            copy.start()
            copies.append(copy)
    for copy in copies:
        copy.wait()


def local(fields, weight_first, weight_second, neighbours, cotangent):
    block, wanted = fields[0, 0], cotangent[0, 0]
    size, c = block.shape[0], block.shape[-1]
    half = size // 2
    count = lax.axis_size("tile")
    cols = max(4, count // 8)
    shape = weight_first.shape
    one, two = weight_first.reshape(9, c, c), weight_second.reshape(9, c, c)
    flops = 2 * size * size * 9 * c * c

    S = jax.ShapeDtypeStruct
    sent = [S((size, c), bf16)] * 4
    halo = S((4, size, c), f32)
    edge = [S((half, 8, 2 * c), f32)] * 2 + [S((size, c), f32)] * 2
    pairs = lambda kind: S((half, size, 2 * c), kind)
    shifted = S(((half + 1) * size, 6 * c), bf16)
    V = lambda leaf: pltpu.VMEM(leaf.shape, leaf.dtype)
    ahead = [pltpu.VMEM((6 * c, 2 * c), bf16)] * 2
    back = [pltpu.VMEM((2 * c, 6 * c), bf16)] * 2
    rooms = [V(leaf) for leaf in edge] + [pltpu.VMEM((size, c), f32)] * 2
    long = pltpu.VMEM((4, size + 16, c), f32)
    whole = lambda arrays: [(array, None) for array in arrays]

    def edge_blocks(array):
        last = size // 8 - 1
        return [
            (array, pl.BlockSpec((half, 8, 2 * c), lambda step: (0, 0, 0))),
            (array, pl.BlockSpec((half, 8, 2 * c), lambda step: (0, last, 0))),
            (array, pl.BlockSpec((1, size, c), lambda step: (0, 0, 0))),
            (array, pl.BlockSpec((1, size, c), lambda step: (half - 1, 0, 1))),
        ]

    def image_edges(array):
        last = size // 16 - 1
        return [
            (array, pl.BlockSpec((size, 16, c), lambda step: (0, 0, 0))),
            (array, pl.BlockSpec((size, 16, c), lambda step: (0, last, 0))),
            (array, pl.BlockSpec((1, size, c), lambda step: (0, 0, 0))),
            (array, pl.BlockSpec((1, size, c), lambda step: (size - 1, 0, 0))),
        ]

    wide = pltpu.VMEM((4, size, 2 * c), f32)
    far = pl.BlockSpec(memory_space=pl.ANY)
    stay = lambda array: (pltpu.with_memory_space_constraint(array, pltpu.HBM), far)
    *strips, found, block, one, own = call(
        functools.partial(first_strips, cols),
        "first_strips",
        [stay(neighbours.T), stay(block), stay(one)],
        [S((2 * size, c), bf16)] * 4
        + [S((12, 8, 128), jnp.int32), S(block.shape, bf16), S(one.shape, bf16), halo],
        [wide, pltpu.VMEM((2, size, 16, c), bf16), pltpu.VMEM((2, 2, size, c), bf16)]
        + [pltpu.SMEM(neighbours.shape[::-1], jnp.int32), pltpu.SemaphoreType.DMA((7,))],
    )
    links = (found, None)
    near = swap_all(strips, cols)
    shifted_one, pre_one, hidden, slope = call(
        first_bulk,
        "first_bulk",
        whole([block, one]),
        [shifted, pairs(f32), pairs(bf16), pairs(bf16)],
        [V(pairs(bf16))] + ahead,
        flops,
    )
    found = call(
        first_edges,
        "first_edges",
        [links] + whole(near) + [(one, None)] + edge_blocks(pre_one),
        [S((2 * size + 16, c), bf16)] * 4 + edge + edge + [halo],
        rooms + [wide, long, pltpu.VMEM((4, 2, 16, c), f32), V(halo)],
    )
    strips, hidden_edges, slope_edges, halo_one = found[:4], found[4:8], found[8:12], found[12]
    carried = swap_all(strips, cols)
    shifted_two, pre_two, out_bulk, delta_bulk = call(
        second_bulk,
        "second_bulk",
        whole([hidden, *hidden_edges, two, wanted]),
        [shifted, pairs(f32), pairs(bf16), pairs(bf16)],
        [V(pairs(f32))] + ahead,
        flops,
    )
    found = call(
        second_edges,
        "second_edges",
        [links] + whole(carried) + [(two, None)] + edge_blocks(pre_two) + image_edges(wanted),
        sent + edge + edge + [halo, halo],
        rooms + [V(halo), long],
    )
    strips, out_edges, delta_edges, halo_two, grads = found[:4], found[4:8], found[8:12], *found[12:]
    grad_two, grad_hidden, delta_one = call(
        second_back,
        "second_back",
        whole([delta_bulk, *delta_edges, halo_two, shifted_two, two, slope]),
        [S((9, c, c), f32), pairs(f32), pairs(bf16)],
        [V(pairs(f32)), V(pairs(bf16))] + back + [V(shifted), V(halo), long],
        2 * flops,
    )
    delta_one, kept, given = call(
        first_grads,
        "first_grads",
        [links]
        + edge_blocks(grad_hidden)
        + whole([*slope_edges, delta_one, halo_one, shifted_one, grad_two])
        + whole([own, *near, *carried, grads]),
        [pairs(bf16), S((9, c, c), f32), S((9, c, c), bf16)],
        [V(pairs(f32)), V(halo), long, pltpu.VMEM((9, c, c), f32)]
        + [pltpu.VMEM((3, size + 16, c), f32)],
        flops,
    )
    ways = routes(cols)
    quarter, got, strips = scatter_line(
        kept.reshape(9 * c, c), given.reshape(9 * c, c), strips, ways
    )
    found = call(
        first_back,
        "first_back",
        [links] + whole(strips) + [(one, None)] + edge_blocks(grad_hidden) + whole(slope_edges),
        sent + edge,
        rooms + [V(halo), long, V(halo), V(halo)],
    )
    strips, delta_edges = found[:4], found[4:8]
    interior, out_field = call(
        last_bulk,
        "last_bulk",
        whole([delta_one, one, out_bulk, *delta_edges, *out_edges]),
        [pairs(f32), S(block.shape, bf16)],
        [V(pairs(f32)), V(shifted)] + back,
        flops,
    )
    quarter, blocks = sum_rest(quarter, got, strips, ways)
    quarter, blocks, strips, interior = lax.optimization_barrier(
        (quarter, blocks, strips, interior)
    )
    got, strips = lax.optimization_barrier(swap_line(blocks, strips, ways))
    (grad_block,) = call(
        last_edges,
        "last_edges",
        [links] + whole([*strips, interior]),
        [S(block.shape, bf16)],
        rooms + [V(halo), V(pairs(f32))],
    )
    quarters = [quarter, *got]
    (stacked,) = call(stack, "stack", whole(quarters), [S((4, *quarter.shape), bf16)], [])
    others, grad_block = lax.optimization_barrier((flip_swap(stacked, 0, 1), grad_block))
    grads = call(
        both_grads,
        "both_grads",
        whole([stacked, others]),
        [S((9 * c, c), f32)] * 2,
        [pltpu.VMEM(stacked.shape, f32)] * 2 + [pltpu.SemaphoreType.DMA((2, 4))],
        out_spec=far,
    )
    grad_first, grad_second = (grad.reshape(shape) for grad in grads)
    return (out_field[None, None], grad_block[None, None], grad_first, grad_second)


def solution(mesh):
    placed = (P("ens", "tile", None, None, None), P(), P(), P(), P("ens", "tile", None, None, None))
    return jax.shard_map(
        local,
        mesh=mesh,
        in_specs=placed,
        out_specs=(
            P("ens", "tile", None, None, None),
            P("ens", "tile", None, None, None),
            P(),
            P(),
        ),
        check_vma=False,
    )
```
